32 devices in a mesh: dp: 2 (over x), fsdp: 16 (over z, y, core).
Axes of the slice: x: 2, y: 2, z: 4, core: 2. Of those that a mesh axis runs over, the one named last changes fastest.
Arguments:
- tokens: bfloat16 [12288, 960], P(('dp', 'fsdp')), may hold values from -6 to 6
- lengths: int32 [32, 4], P(('dp', 'fsdp')), may hold values from 1 to 168, 336 in all within a row
- w_query: bfloat16 [960, 960], P('fsdp'), may hold values from -0.1875 to 0.1875
- key_weight: bfloat16 [960, 320], P('fsdp'), may hold values from -0.1875 to 0.1875
- value_weight: bfloat16 [960, 320], P('fsdp'), may hold values from -0.1875 to 0.1875
- output_weight: bfloat16 [960, 960], P('fsdp'), may hold values from -0.75 to 0.75
- w_gate: bfloat16 [960, 2560], P('fsdp'), may hold values from -0.1875 to 0.1875
- w_up: bfloat16 [960, 2560], P('fsdp'), may hold values from -0.1875 to 0.1875
- w_down: bfloat16 [2560, 960], P('fsdp'), may hold values from -0.125 to 0.125
- gain_attn: bfloat16 [960], P('fsdp'), may hold values from 0.099609375 to 1.8984375
- gain_ffn: bfloat16 [960], P('fsdp'), may hold values from 0.099609375 to 1.8984375
- out_grad: bfloat16 [12288, 960], P(('dp', 'fsdp')), may hold values from -6 to 6
Outputs:
- output: bfloat16 [12288, 960], P(('dp', 'fsdp'))
- input_grad: bfloat16 [12288, 960], P(('dp', 'fsdp'))
- grad_query: float32 [960, 960], P('fsdp')
- key_weight_gradient: float32 [960, 320], P('fsdp')
- value_weight_gradient: float32 [960, 320], P('fsdp')
- grad_out: float32 [960, 960], P('fsdp')
- grad_gate: float32 [960, 2560], P('fsdp')
- grad_up: float32 [960, 2560], P('fsdp')
- grad_down: float32 [2560, 960], P('fsdp')
- grad_gain_attn: float32 [960], P('fsdp')
- grad_gain_ffn: float32 [960], P('fsdp')
The draws below stay inside these ranges and needn't reach their ends.
Inputs may be any that keep to these rules, and one draw needn't show every extreme that they name: A row holds the lengths of the 4 documents of one sequence from its first slot on; each row sums to 336 and its largest entry is 168.
All inputs are finite; a program needn't handle non-finite values.
Results may differ from the reference program's by a relative error of at most 0.028.
Values may be sent and summed in bfloat16 or wider, within the bound.
No kernel may reach another device: no remote copies, remote signals or barrier semaphores. Data moves between devices by JAX's collectives and lax.ppermute only.
A program may use at most 192 MiB of HBM per device.

```python
import math
import jax
import jax.numpy as jnp
import numpy as np
from jax import lax

MODEL_WIDTH = 960
QUERY_HEADS = 15
KEY_VALUE_HEADS = 5
HEAD_SIZE = 64
FF = 2560
TOK_DEV = 384
DOCS = 4
PAD = 48
DOC_MOST = 168
SEQS = 32
TOKENS = 12288


def strengthened(entries, key, source, target, blocks, factor):
    def block_of(position):
        return (jnp.arange(entries.shape[position]) // (entries.shape[position] // blocks)).reshape((-1,) + (1,) * (entries.ndim - 1 - position))

    near = jax.random.permutation(key, blocks)[block_of(target)]
    second = (block_of(target) + blocks // 2) % blocks
    return jnp.where((block_of(source) == near) | (block_of(source) == second), factor * entries, entries)


def steps_of(key, shape, pieces, smallest, largest):
    level, own = 1.0, jax.random.fold_in(key, 6)
    for dim, parts in pieces:
        steps = jnp.exp(jax.random.uniform(jax.random.fold_in(own, dim), (parts,), jnp.float32, smallest / len(pieces), largest / len(pieces)))
        level = level * jnp.repeat(steps, shape[dim] // parts).reshape([-1 if axis == dim else 1 for axis in range(len(shape))])
    return level


def split_up(count, total, limit, lean):
    portions = [(1 << 20) // math.isqrt(rank ** lean) + 1 for rank in range(2, count + 1)]
    rest, holding = total - limit - (count - 1), [1] * (count - 1)
    while rest > 0:
        movable = [i for i in range(count - 1) if holding[i] < limit]
        pool, left = sum([portions[i] for i in movable]), rest
        for i in movable:
            more = min(limit - holding[i], max(1, left * portions[i] // pool), rest)
            holding[i] = holding[i] + more
            rest = rest - more
    return np.array([limit] + holding)


def uneven_parts(rng, count, total, reach, slope):
    if count == 2:
        one = jax.random.randint(rng, (), max(1, total - reach), min(reach, total - 1) + 1)
        return jnp.stack([one, total - one])
    sizes = jnp.asarray(split_up(count, total, reach, slope), jnp.int32)
    twos = (count - 1) // 2
    giver, sink = sizes[1:1 + 2 * twos:2], sizes[2:2 + 2 * twos:2]
    slack = jnp.minimum(giver - 1, reach - sink)
    shifted = jax.random.randint(jax.random.fold_in(rng, 1), (twos,), 0, 1 << 20) % (slack + 1)
    sizes = sizes.at[1:1 + 2 * twos:2].set(giver - shifted).at[2:2 + 2 * twos:2].set(sink + shifted)
    return sizes[jax.random.permutation(jax.random.fold_in(rng, 2), count)]


def scatter_about(rng, shape, deviation, limit, shards=(), kind=jnp.bfloat16):
    level = steps_of(rng, shape, shards, -0.22, 0.18) if shards else 1.0
    values = jax.random.normal(rng, shape, jnp.float32) * deviation * level
    return jnp.minimum(jnp.maximum(values, -limit), limit).astype(kind)


def gaussian_with(rng, shape, width, limit, cuts, heavy, held_as=jnp.bfloat16):
    array = width * jax.random.normal(rng, shape, jnp.float32)
    if cuts:
        array = array * steps_of(rng, shape, cuts, -0.22, 0.18)
    return jnp.clip(strengthened(array, jax.random.fold_in(rng, 3), *heavy), -limit, limit).astype(held_as)


def setup_inputs(seed: int = 0) -> dict:
    arg_keys = jax.random.split(jax.random.key(seed), 13)
    tokens = scatter_about(arg_keys[0], (TOKENS, MODEL_WIDTH), 1.0, 6.0, ((0, 32),))
    lengths = jax.vmap(lambda own: uneven_parts(own, DOCS, TOK_DEV - PAD, DOC_MOST, 2))(jax.random.split(arg_keys[1], SEQS)).reshape((SEQS, DOCS)).astype(jnp.int32)
    w_query = scatter_about(arg_keys[2], (MODEL_WIDTH, MODEL_WIDTH), MODEL_WIDTH ** -0.5, 0.1875, ((0, 16),))
    key_weight = scatter_about(arg_keys[3], (MODEL_WIDTH, KEY_VALUE_HEADS * HEAD_SIZE), MODEL_WIDTH ** -0.5, 0.1875, ((0, 16),))
    value_weight = scatter_about(arg_keys[4], (MODEL_WIDTH, KEY_VALUE_HEADS * HEAD_SIZE), MODEL_WIDTH ** -0.5, 0.1875, ((0, 16),))
    output_weight = scatter_about(arg_keys[5], (MODEL_WIDTH, MODEL_WIDTH), (MODEL_WIDTH // 16) ** -0.5, 0.75, ((0, 16),))
    w_gate = scatter_about(arg_keys[6], (MODEL_WIDTH, FF), MODEL_WIDTH ** -0.5, 0.1875, ((0, 16),))
    w_up = scatter_about(arg_keys[7], (MODEL_WIDTH, FF), MODEL_WIDTH ** -0.5, 0.1875, ((0, 16),))
    w_down = scatter_about(arg_keys[8], (FF, MODEL_WIDTH), FF ** -0.5, 0.125, ((0, 16),))
    gain_attn = jnp.clip(1.0 + 0.18 * jax.random.normal(arg_keys[9], (MODEL_WIDTH,), jnp.float32), 0.099609375, 1.8984375).astype(jnp.bfloat16)
    gain_ffn = jnp.clip(1.0 + 0.18 * jax.random.normal(arg_keys[10], (MODEL_WIDTH,), jnp.float32), 0.099609375, 1.8984375).astype(jnp.bfloat16)
    out_grad = gaussian_with(arg_keys[11], (TOKENS, MODEL_WIDTH), 1.0, 6.0, ((0, 32),), (0, 1, 32, 2.75))
    return {"tokens": tokens, "lengths": lengths, "w_query": w_query, "key_weight": key_weight, "value_weight": value_weight, "output_weight": output_weight, "w_gate": w_gate, "w_up": w_up, "w_down": w_down, "gain_attn": gain_attn, "gain_ffn": gain_ffn, "out_grad": out_grad}


@jax.custom_vjp
def lower_precision(v):
    return lax.optimization_barrier(v.astype(jnp.bfloat16)).astype(jnp.float32)

@jax.custom_vjp
def low_back(v):
    return v

def low_keep(v):
    return (lower_precision(v), None)

def low_pass(kept, grad):
    return (grad,)

def back_keep(v):
    return (v, None)

def back_low(kept, grad):
    return (lower_precision(grad),)
lower_precision.defvjp(low_keep, low_pass)
low_back.defvjp(back_keep, back_low)
exact = lax.Precision.HIGHEST
rope_base = 10000.0
norm_eps = 1e-05

def layout(doc_lengths, token_count):
    ends = jnp.cumsum(doc_lengths, axis=1).astype(jnp.int32)
    starts = ends - doc_lengths
    place = jnp.arange(token_count, dtype=jnp.int32)
    document = lax.optimization_barrier(jnp.sum((place[None, :, None] >= ends[:, None, :]).astype(jnp.int32), axis=2))
    inside = place[None, :] < ends[:, -1:]
    segment = jnp.where(inside, document, -1)
    chosen = document[:, :, None] == jnp.arange(doc_lengths.shape[1], dtype=jnp.int32)[None, None, :]
    begin = lax.optimization_barrier(jnp.sum(jnp.where(chosen, starts[:, None, :], 0), axis=2))
    positions = jnp.where(inside, place[None, :] - begin, 0)
    causal = place[:, None] >= place[None, :]
    same = (segment[:, :, None] == segment[:, None, :]) & (segment[:, :, None] >= 0)
    allowed = same & causal[None] | (place[:, None] == place[None, :])[None]
    return (positions, allowed)

def rotation(positions):
    half = HEAD_SIZE // 2
    frequency = jnp.exp(jnp.arange(half, dtype=jnp.float32) * (-2.0 * math.log(rope_base) / HEAD_SIZE))
    angle = positions.astype(jnp.float32)[..., None] * frequency
    return (jnp.cos(angle), jnp.sin(angle))

def apply_rotary(values, cosine_table, sine_table):
    half = values.shape[-1] // 2
    first = values[..., :half]
    second = values[..., half:]
    cosine_table = cosine_table[..., None, :]
    sine_table = sine_table[..., None, :]
    return jnp.concatenate([first * cosine_table - second * sine_table, second * cosine_table + first * sine_table], axis=-1)

def norm(values, gain):
    return values * lax.rsqrt(lax.optimization_barrier(jnp.mean(values * values, axis=-1, keepdims=True)) + norm_eps) * gain

def block(source, weights, cosine_table, sine_table, allowed):
    w_query, key_weight, value_weight, output_weight, w_gate, w_up, w_down, gain_attn, gain_ffn = weights
    batch_rows = source.shape[0]
    token_count = source.shape[1]
    normalized_input = lower_precision(norm(source, gain_attn))
    query_rows = low_back(jnp.einsum('gtd,de->gte', normalized_input, w_query, precision=exact))
    key = low_back(jnp.einsum('gtd,de->gte', normalized_input, key_weight, precision=exact))
    value_rows = lower_precision(low_back(jnp.einsum('gtd,de->gte', normalized_input, value_weight, precision=exact)))
    query_rows = lower_precision(apply_rotary(query_rows.reshape(batch_rows, token_count, QUERY_HEADS, HEAD_SIZE), cosine_table, sine_table))
    query_rows = query_rows.reshape(batch_rows, token_count, KEY_VALUE_HEADS, QUERY_HEADS // KEY_VALUE_HEADS, HEAD_SIZE)
    key = lower_precision(apply_rotary(key.reshape(batch_rows, token_count, KEY_VALUE_HEADS, HEAD_SIZE), cosine_table, sine_table))
    value_rows = value_rows.reshape(batch_rows, token_count, KEY_VALUE_HEADS, HEAD_SIZE)
    score = low_back(jnp.einsum('gtkrd,gukd->gkrtu', query_rows, key, precision=exact)) * HEAD_SIZE ** (-0.5)
    score = jnp.where(allowed[:, None, None], score, -1e+30)
    highest = lax.optimization_barrier(jnp.max(score, axis=-1, keepdims=True))
    powers = jnp.exp(score - highest)
    attention = lower_precision(powers / lax.optimization_barrier(jnp.sum(powers, axis=-1, keepdims=True)))
    mixed = jnp.einsum('gkrtu,gukd->gtkrd', attention, value_rows, precision=exact).reshape(batch_rows, token_count, MODEL_WIDTH)
    mixed = lower_precision(low_back(mixed))
    hidden = source + low_back(jnp.einsum('gtd,de->gte', mixed, output_weight, precision=exact))
    normed_ffn = lower_precision(norm(hidden, gain_ffn))
    gate = low_back(jnp.einsum('gtd,df->gtf', normed_ffn, w_gate, precision=exact))
    up_value = low_back(jnp.einsum('gtd,df->gtf', normed_ffn, w_up, precision=exact))
    inner = lower_precision(jax.nn.silu(gate) * up_value)
    return hidden + low_back(jnp.einsum('gtf,fd->gtd', inner, w_down, precision=exact))

def reference(tokens, lengths, w_query, key_weight, value_weight, output_weight, w_gate, w_up, w_down, gain_attn, gain_ffn, out_grad):
    weights = tuple((w.astype(jnp.float32) for w in (w_query, key_weight, value_weight, output_weight, w_gate, w_up, w_down, gain_attn, gain_ffn)))
    per_step = 8
    rounds = SEQS // per_step
    sources = tokens.astype(jnp.float32).reshape(rounds, per_step, TOK_DEV, MODEL_WIDTH)
    cotangents = out_grad.astype(jnp.float32).reshape(rounds, per_step, TOK_DEV, MODEL_WIDTH)
    doc_lengths = lengths.reshape(rounds, per_step, DOCS)

    def advance(totals, inputs):
        source, cotangent, doc_row = inputs
        positions, allowed = layout(doc_row, TOK_DEV)
        cosine_table, sine_table = rotation(positions)

        def forward(values, params):
            return block(block(values, params, cosine_table, sine_table, allowed), params, cosine_table, sine_table, allowed)
        result, pullback = jax.vjp(forward, source, weights)
        back_source, back_weights = pullback(cotangent)
        totals = tuple((left + right for left, right in zip(totals, back_weights)))
        return (totals, (result.astype(jnp.bfloat16), back_source.astype(jnp.bfloat16)))
    zeros = tuple((jnp.zeros(w.shape, jnp.float32) for w in weights))
    totals, (results, backs) = lax.scan(advance, zeros, (sources, cotangents, doc_lengths))
    return (results.reshape(TOKENS, MODEL_WIDTH), backs.reshape(TOKENS, MODEL_WIDTH), totals[0], totals[1], totals[2], totals[3], totals[4], totals[5], totals[6], totals[7], totals[8])
```

```python
import functools
import math

import jax
import jax.numpy as jnp
from jax import lax
from jax.experimental import pallas as pl
from jax.experimental.pallas import tpu as pltpu
from jax.sharding import PartitionSpec as P

HEAD_SIZE = 64
GROUP = 3
ROPE_BASE = 10000.0
EPS = 1e-05
BF = jnp.bfloat16
F32 = jnp.float32


def layout(doc_lengths, token_count):
    ends = jnp.cumsum(doc_lengths, axis=1)
    starts = ends - doc_lengths
    place = jnp.arange(token_count, dtype=jnp.int32)
    document = jnp.sum((place[None, :, None] >= ends[:, None, :]).astype(jnp.int32), axis=2)
    inside = place[None, :] < ends[:, -1:]
    segment = jnp.where(inside, document, -1)
    chosen = (
        document[:, :, None] == jnp.arange(doc_lengths.shape[1], dtype=jnp.int32)[None, None, :]
    )
    begin = jnp.sum(jnp.where(chosen, starts[:, None, :], 0), axis=2)
    positions = jnp.where(inside, place[None, :] - begin, 0)
    causal = place[:, None] >= place[None, :]
    same = (segment[:, :, None] == segment[:, None, :]) & (segment[:, :, None] >= 0)
    allowed = same & causal[None] | (place[:, None] == place[None, :])[None]
    return (positions, allowed)


def rotation(positions):
    half = HEAD_SIZE // 2
    frequency = jnp.exp(
        jnp.arange(half, dtype=jnp.float32) * (-2.0 * math.log(ROPE_BASE) / HEAD_SIZE)
    )
    angle = positions.astype(jnp.float32)[..., None] * frequency
    return (jnp.cos(angle), jnp.sin(angle))


def apply_rotary(values, cosine_table, sine_table):
    half = values.shape[-1] // 2
    first = values[..., :half]
    second = values[..., half:]
    cosine_table = cosine_table[..., None, :]
    sine_table = sine_table[..., None, :]
    return jnp.concatenate(
        [first * cosine_table - second * sine_table, second * cosine_table + first * sine_table],
        axis=-1,
    )


class Place:
    def __init__(self, mesh):
        self.n, self.groups = mesh.shape["fsdp"], mesh.shape["dp"]
        self.nz = self.n // 4
        i = lax.axis_index("fsdp")
        self.c, self.y, self.z = i % 2, (i // 2) % 2, i // 4
        self.p = lax.axis_index("dp") % 2

    def swap_core(self, v):
        return lax.ppermute(v, "fsdp", [(i, i ^ 1) for i in range(self.n)])

    def shift_z(self, v, k):
        return lax.ppermute(v, "fsdp", [(i, (i + 4 * k) % self.n) for i in range(self.n)])

    def swap_x(self, v):
        return lax.ppermute(v, "dp", [(d, d ^ 1) for d in range(self.groups)])

    def cross(self, v, first):
        pairs = []
        for d in range(self.groups):
            for i in range(self.n):
                along_x = (i % 2 == 0) == first
                e, j = (d ^ 1, i) if along_x else (d, i ^ 2)
                pairs.append((d * self.n + i, e * self.n + j))
        return lax.ppermute(v, ("dp", "fsdp"), pairs)


def pick(v, k, axis=0):
    return lax.dynamic_index_in_dim(v, k, axis, keepdims=False)


def gather_pieces(at, shard):
    rows, cols = shard.shape
    halves = shard.reshape(2, rows // 2, cols)
    keep = pick(halves, at.c)
    got = at.swap_core(pick(halves, 1 - at.c))
    mine = jnp.where(at.p == at.c, keep, got)
    rest = jnp.where(at.p == at.c, got, keep)
    del rest
    line = jnp.stack([mine] + [at.shift_z(mine, k) for k in range(1, at.nz)])
    second = at.cross(line, False)
    both = jnp.concatenate([line, second])
    third = at.cross(both, True)
    own = jnp.concatenate([both, third])
    return own, at.swap_core(own)


def assemble(at, pieces, splits):
    own, other = pieces
    count, half, cols = own.shape
    order = []
    for core_of_piece in (0, 1):
        h = at.c if core_of_piece == 0 else 1 - at.c
        for j in range(count):
            dz, slot = j % at.nz, j // at.nz
            lo, hi = slot % 2, slot // 2
            dy = jnp.where(h == 0, lo, hi)
            dc = jnp.where(h == 0, hi, lo)
            z = (at.z - dz + at.nz) % at.nz
            order.append((((z * 2 + (at.y ^ dy)) * 2 + (at.p ^ dc)) * 2 + h).astype(jnp.int32))
    order = jnp.stack(order)
    bounds = [0]
    for width in splits:
        bounds.append(bounds[-1] + width)

    def body(order_ref, own_ref, other_ref, *rest):
        outs, sem = rest[:-1], rest[-1]
        copies = []
        for source, ref in enumerate((own_ref, other_ref)):
            for j in range(count):
                to = order_ref[source * count + j]
                for k, out in enumerate(outs):
                    copies.append(
                        pltpu.make_async_copy(
                            ref.at[j, :, pl.ds(bounds[k], splits[k])],
                            out.at[to],
                            sem.at[(source * count + j) * len(outs) + k],
                        )
                    )
        for copy in copies:
            copy.start()
        for copy in copies:
            copy.wait()

    outs = pl.pallas_call(
        body,
        grid_spec=pltpu.PrefetchScalarGridSpec(
            num_scalar_prefetch=1,
            grid=(),
            in_specs=[pl.BlockSpec(memory_space=pl.ANY)] * 2,
            out_specs=[pl.BlockSpec(memory_space=pltpu.VMEM)] * len(splits),
            scratch_shapes=[pltpu.SemaphoreType.DMA((2 * count * len(splits),))],
        ),
        out_shape=[jax.ShapeDtypeStruct((2 * count, half, w), BF) for w in splits],
    )(order, own, other)
    return [o.reshape(2 * count * half, o.shape[2]) for o in outs]


def reduce_scatter(at, grad):
    n, rows, cols = grad.shape
    half = rows // 2
    g = grad.reshape(at.nz, 4, 2, half, cols)
    own = pick(g, at.c, 2)
    got = at.swap_core(pick(g, 1 - at.c, 2))

    def chip(k):
        return pick(own, k, 1).astype(F32) + pick(got, k, 1).astype(F32)

    mine = jnp.where(at.c == 0, at.p, at.y)

    def slot(u, v):
        return jnp.where(at.c == 0, 2 * v + u, 2 * u + v)

    first = at.cross(jnp.stack([chip(slot(1 - mine, v)) for v in (0, 1)]).astype(BF), True)
    mine2 = jnp.where(at.c == 0, at.y, at.p)

    def stage1(v):
        return chip(slot(mine, v)) + pick(first, v).astype(F32)

    second = at.cross(stage1(1 - mine2).astype(BF), False)
    kept = stage1(mine2) + second.astype(F32)
    low = kept.astype(BF)
    total = pick(kept, at.z)
    for k in range(1, at.nz):
        total = total + at.shift_z(pick(low, (at.z + k) % at.nz), k).astype(F32)
    step = 2
    while step < at.groups:
        total = total + lax.ppermute(
            total.astype(BF), "dp", [(d, d ^ step) for d in range(at.groups)]
        ).astype(F32)
        step *= 2
    low = total.astype(BF)
    swapped = at.swap_x(low)
    mine_here = at.p == at.c
    keep = jnp.where(mine_here, low, swapped)
    other = at.swap_core(jnp.where(mine_here, swapped, low))
    return jnp.concatenate(
        [jnp.where(at.c == 0, keep, other), jnp.where(at.c == 0, other, keep)]
    ).astype(F32)


def product(left, right):
    return jnp.dot(left, right, preferred_element_type=F32)


def product_back(left, right):
    return lax.dot_general(left, right, (((1,), (1,)), ((), ())), preferred_element_type=F32)


def outer_sum(left, right):
    return lax.dot_general(left, right, (((0,), (0,)), ((), ())), preferred_element_type=F32)


def norm_forward(values, gain, width):
    scale = lax.rsqrt(jnp.sum(values * values, axis=-1, keepdims=True) / width + EPS)
    return (scale, (values * scale * gain).astype(BF))


def norm_backward(values, scale, gain, grad, width):
    unit = values * scale
    gain_grad = jnp.sum(grad * unit, axis=0)
    inner = grad * gain
    mean = jnp.sum(inner * unit, axis=-1, keepdims=True) / width
    return (gain_grad, scale * (inner - unit * mean))


def scores(q, k, allowed):
    score = jnp.einsum("tkrd,ukd->krtu", q, k, preferred_element_type=F32) * HEAD_SIZE ** (-0.5)
    return jnp.where(allowed, score, -1e30)


def block_forward(source, w, rope, allowed, width):
    wqkv, wo, wgate, wup, wdown, gain_attn, gain_ffn = w
    cos, sin = rope
    t = source.shape[0]
    kv = (wqkv.shape[1] - width) // 2
    kvh = kv // HEAD_SIZE
    scale_attn, a1 = norm_forward(source, gain_attn, width)
    qkv = product(a1, wqkv)
    q = apply_rotary(qkv[:, :width].reshape(t, -1, HEAD_SIZE), cos, sin).astype(BF)
    q = q.reshape(t, kvh, GROUP, HEAD_SIZE)
    k = apply_rotary(qkv[:, width : width + kv].reshape(t, kvh, HEAD_SIZE), cos, sin).astype(BF)
    v = qkv[:, width + kv :].astype(BF).reshape(t, kvh, HEAD_SIZE)
    score = scores(q, k, allowed)
    highest = jnp.max(score, axis=-1, keepdims=True)
    powers = jnp.exp(score - highest)
    summed = jnp.sum(powers, axis=-1, keepdims=True)
    lse = highest + jnp.log(summed)
    prob = (powers / summed).astype(BF)
    mixed = jnp.einsum("krtu,ukd->tkrd", prob, v, preferred_element_type=F32)
    mixed = mixed.reshape(t, width).astype(BF)
    hidden = source + product(mixed, wo)
    scale_ffn, a2 = norm_forward(hidden, gain_ffn, width)
    gate = product(a2, wgate)
    up = product(a2, wup)
    inner = (jax.nn.silu(gate) * up).astype(BF)
    result = hidden + product(inner, wdown)
    return result, (source, scale_attn, a1, q, k, v, lse, mixed, hidden, scale_ffn, a2, gate, up, inner)


def block_backward(grad, w, kept, rope, allowed, width):
    wqkv, wo, wgate, wup, wdown, gain_attn, gain_ffn = w
    source, scale_attn, a1, q, k, v, lse, mixed, hidden, scale_ffn, a2, gate, up, inner = kept
    cos, sin = rope
    t = source.shape[0]
    kvh = k.shape[1]
    cl = grad.astype(BF)
    g_inner = product_back(cl, wdown)
    sg = jax.nn.sigmoid(gate)
    g_gate = (g_inner * up * sg * (1.0 + gate * (1.0 - sg))).astype(BF)
    g_up = (g_inner * gate * sg).astype(BF)
    g_a2 = product_back(g_gate, wgate) + product_back(g_up, wup)
    g_gain_ffn, g_hidden = norm_backward(hidden, scale_ffn, gain_ffn, g_a2, width)
    g_hidden = grad + g_hidden
    gl = g_hidden.astype(BF)
    g_mixed = product_back(gl, wo).astype(BF).reshape(t, kvh, GROUP, HEAD_SIZE)
    p = jnp.exp(scores(q, k, allowed) - lse)
    g_p = jnp.einsum("tkrd,ukd->krtu", g_mixed, v, preferred_element_type=F32)
    g_v = jnp.einsum("krtu,tkrd->ukd", p.astype(BF), g_mixed, preferred_element_type=F32)
    g_s = p * (g_p - jnp.sum(p * g_p, axis=-1, keepdims=True))
    g_s = (g_s * HEAD_SIZE ** (-0.5)).astype(BF)
    g_q = jnp.einsum("krtu,ukd->tkrd", g_s, k, preferred_element_type=F32)
    g_k = jnp.einsum("krtu,tkrd->ukd", g_s, q, preferred_element_type=F32)
    g_q = apply_rotary(g_q.reshape(t, -1, HEAD_SIZE), cos, -sin).reshape(t, -1).astype(BF)
    g_k = apply_rotary(g_k, cos, -sin).reshape(t, -1).astype(BF)
    g_v = g_v.reshape(t, -1).astype(BF)
    g_qkv = jnp.concatenate([g_q, g_k, g_v], axis=1)
    g_a1 = product_back(g_qkv, wqkv)
    g_gain_attn, g_source = norm_backward(source, scale_attn, gain_attn, g_a1, width)
    return g_hidden + g_source, (a1, g_qkv, mixed, gl, a2, g_gate, g_up, inner, cl, g_gain_attn, g_gain_ffn)


def spread(v, n, real, padded):
    lead = v.shape[:-1]
    v = v.reshape(lead + (n, real))
    v = jnp.pad(v, [(0, 0)] * len(lead) + [(0, 0), (0, padded - real)])
    return v.reshape(lead + (n * padded,))


def narrow(v, n, real, padded):
    lead = v.shape[:-1]
    return v.reshape(lead + (n, padded))[..., :real].reshape(lead + (n * real,))


def shards(mesh, tokens, lengths, w_query, key_weight, value_weight, output_weight, w_gate, w_up, w_down, gain_attn, gain_ffn, out_grad):
    at = Place(mesh)
    n = at.n
    real, width = w_query.shape
    padded = -(-(real + 2) // 16) * 16
    wide = n * padded

    def pad_rows(v):
        return jnp.pad(v, ((0, padded - v.shape[0]), (0, 0)))

    qkv = jnp.concatenate([w_query, key_weight, value_weight], axis=1)
    gains = jnp.pad(jnp.stack([gain_attn, gain_ffn]), ((0, 0), (0, qkv.shape[1] - real)))
    qkv = pad_rows(jnp.concatenate([qkv, gains]))
    attn = jnp.concatenate([pad_rows(spread(output_weight, n, real, padded)), qkv], axis=1)
    down = spread(w_down, n, real, padded)

    wo, wqkv = assemble(at, gather_pieces(at, attn), [wide, qkv.shape[1]])
    (wgate,) = assemble(at, gather_pieces(at, pad_rows(w_gate)), [w_gate.shape[1]])
    (wup,) = assemble(at, gather_pieces(at, pad_rows(w_up)), [w_up.shape[1]])
    (wdown,) = assemble(at, gather_pieces(at, down), [wide])
    wo = wo.reshape(n, padded, wide)[:, :real].reshape(width, wide)
    gains = wqkv.reshape(n, padded, -1)[:, real : real + 2, :padded].astype(F32)
    weights = (wqkv, wo, wgate, wup, wdown, gains[:, 0].reshape(wide), gains[:, 1].reshape(wide))

    positions, allowed = layout(lengths, tokens.shape[0])
    rope = rotation(positions[0])
    allowed = allowed[0]
    x = spread(tokens, n, real, padded).astype(F32)
    first, kept1 = block_forward(x, weights, rope, allowed, width)
    second, kept2 = block_forward(first, weights, rope, allowed, width)
    cot = spread(out_grad, n, real, padded).astype(F32)
    carried, t2 = block_backward(cot, weights, kept2, rope, allowed, width)
    g_x, t1 = block_backward(carried, weights, kept1, rope, allowed, width)
    a1, g_qkv, mixed, gl, a2, g_gate, g_up, inner, cl = (
        jnp.concatenate([l, r]) for l, r in zip(t1[:9], t2[:9])
    )
    gain_sums = jnp.stack([t1[9] + t2[9], t1[10] + t2[10]], axis=0)

    g_down = outer_sum(inner, cl).astype(BF).reshape(n, -1, wide)
    r_down = reduce_scatter(at, g_down)
    r_gate = reduce_scatter(at, outer_sum(a2, g_gate).astype(BF).reshape(n, padded, -1))
    r_up = reduce_scatter(at, outer_sum(a2, g_up).astype(BF).reshape(n, padded, -1))
    g_out = outer_sum(spread(mixed, n, real, padded), gl).astype(BF).reshape(n, padded, wide)
    g_in = outer_sum(a1, g_qkv).astype(BF).reshape(n, padded, -1)
    g_gains = gain_sums.astype(BF).reshape(2, n, padded).transpose(1, 0, 2)
    g_in = lax.dynamic_update_slice(g_in, g_gains, (0, real, 0))
    r_attn = reduce_scatter(at, jnp.concatenate([g_out, g_in], axis=2))
    r_in = r_attn[:, wide:]
    kv = (r_in.shape[1] - width) // 2
    return (
        narrow(second.astype(BF), n, real, padded),
        narrow(g_x.astype(BF), n, real, padded),
        r_in[:real, :width],
        r_in[:real, width : width + kv],
        r_in[:real, width + kv :],
        narrow(r_attn[:real, :wide], n, real, padded),
        r_gate[:real],
        r_up[:real],
        narrow(r_down, n, real, padded),
        r_in[real, :real],
        r_in[real + 1, :real],
    )


def solution(mesh):
    rows, split, gain = P(("dp", "fsdp"), None), P("fsdp", None), P("fsdp")
    return jax.shard_map(
        functools.partial(shards, mesh),
        mesh=mesh,
        in_specs=(rows, rows) + (split,) * 7 + (gain, gain, rows),
        out_specs=(rows, rows) + (split,) * 7 + (gain, gain),
        check_vma=False,
    )
```

```python
import functools
import math

import jax
import jax.numpy as jnp
from jax import lax
from jax.experimental import pallas as pl
from jax.experimental.pallas import tpu as pltpu
from jax.sharding import PartitionSpec as P

HEAD_SIZE = 64
GROUP = 3
ROPE_BASE = 10000.0
EPS = 1e-05
BF = jnp.bfloat16
F32 = jnp.float32
MIB = 1024 * 1024


def layout(doc_lengths, token_count):
    ends = jnp.cumsum(doc_lengths, axis=1)
    starts = ends - doc_lengths
    place = jnp.arange(token_count, dtype=jnp.int32)
    document = jnp.sum((place[None, :, None] >= ends[:, None, :]).astype(jnp.int32), axis=2)
    inside = place[None, :] < ends[:, -1:]
    segment = jnp.where(inside, document, -1)
    chosen = (
        document[:, :, None] == jnp.arange(doc_lengths.shape[1], dtype=jnp.int32)[None, None, :]
    )
    begin = jnp.sum(jnp.where(chosen, starts[:, None, :], 0), axis=2)
    positions = jnp.where(inside, place[None, :] - begin, 0)
    causal = place[:, None] >= place[None, :]
    same = (segment[:, :, None] == segment[:, None, :]) & (segment[:, :, None] >= 0)
    allowed = same & causal[None] | (place[:, None] == place[None, :])[None]
    return (positions, allowed)


def rotation(positions):
    half = HEAD_SIZE // 2
    frequency = jnp.exp(jnp.arange(half, dtype=F32) * (-2.0 * math.log(ROPE_BASE) / HEAD_SIZE))
    angle = positions.astype(F32)[None, :] * frequency[:, None]
    return (jnp.cos(angle), jnp.sin(angle))


class Place:
    def __init__(self, mesh):
        self.n, self.groups = mesh.shape["fsdp"], mesh.shape["dp"]
        self.nz = self.n // 4
        i = lax.axis_index("fsdp")
        self.c, self.y, self.z = i % 2, (i // 2) % 2, i // 4
        self.p = lax.axis_index("dp") % 2

    def swap_core(self, v):
        return lax.ppermute(v, "fsdp", [(i, i ^ 1) for i in range(self.n)])

    def shift_z(self, v, k):
        return lax.ppermute(v, "fsdp", [(i, (i + 4 * k) % self.n) for i in range(self.n)])

    def swap_x(self, v):
        return lax.ppermute(v, "dp", [(d, d ^ 1) for d in range(self.groups)])

    def cross(self, v, first):
        pairs = []
        for d in range(self.groups):
            for i in range(self.n):
                along_x = (i % 2 == 0) == first
                e, j = (d ^ 1, i) if along_x else (d, i ^ 2)
                pairs.append((d * self.n + i, e * self.n + j))
        return lax.ppermute(v, ("dp", "fsdp"), pairs)

    def piece_order(self):
        order = []
        for h in (self.c, 1 - self.c):
            for j in range(4 * self.nz):
                dz, slot = j % self.nz, j // self.nz
                lo, hi = slot % 2, slot // 2
                dy, dc = jnp.where(h == 0, lo, hi), jnp.where(h == 0, hi, lo)
                z = (self.z - dz + self.nz) % self.nz
                order.append((((z * 2 + (self.y ^ dy)) * 2 + (self.p ^ dc)) * 2 + h).astype(jnp.int32))
        return jnp.stack(order)

    def grad_order(self):
        order = []
        for b in range(2 * self.n):
            h, dc, dy, z = b % 2, (b // 2) % 2, (b // 4) % 2, b // 8
            keep_c, keep_y = (self.p == dc).astype(jnp.int32), (self.y == dy).astype(jnp.int32)
            hi, lo = (keep_c, keep_y) if h == 0 else (keep_y, keep_c)
            dz = (z - self.z + self.nz) % self.nz
            place = (2 * hi + lo) * self.nz + dz
            order.append(place + jnp.where(self.c == h, 0, 4 * self.nz))
        return jnp.stack(order).astype(jnp.int32)


def pick(v, k, axis=0):
    return lax.dynamic_index_in_dim(v, k, axis, keepdims=False)


class Order:
    def __init__(self):
        self.last = ()

    def do(self, step, *inputs):
        leaves, tree = jax.tree.flatten(inputs)
        if self.last:
            leaves = lax.optimization_barrier((*leaves, *self.last))[: len(leaves)]
        out = step(*jax.tree.unflatten(tree, leaves))
        self.last = (jax.tree.leaves(out)[0],)
        return out

    def tie(self, v):
        return lax.optimization_barrier((v, *self.last))[0] if self.last else v

    def got(self, *received):
        out = lax.optimization_barrier((*received, *self.last))[: len(received)]
        self.last = (out[0],)
        return out[0] if len(out) == 1 else out


def add(*terms):
    return functools.reduce(lambda a, b: a + b, [t.astype(F32) for t in terms])


class Gather:
    def __init__(self, at, order):
        self.at, self.order = at, order

    def start(self, make, *inputs):
        def step(*inputs):
            shard = make(*inputs)
            halves = shard.reshape(2, shard.shape[0] // 2, shard.shape[1])
            return pick(halves, self.at.c), pick(halves, 1 - self.at.c)

        self.keep, send = self.order.do(step, *inputs)
        self.moving = self.at.swap_core(send)

    def ready(self):
        at = self.at
        got = self.order.got(self.moving)
        self.mine = self.order.do(lambda k, g: jnp.where(at.p == at.c, k, g)[None], self.keep, got)

    def along_z(self):
        mine = self.order.tie(self.mine)
        self.moving = [self.at.shift_z(mine, k) for k in range(1, self.at.nz)]

    def come(self):
        parts = self.order.got(*self.moving)
        self.parts = parts if isinstance(parts, tuple) else (parts,)

    def line_up(self):
        self.line = self.order.do(lambda *v: jnp.concatenate(v), self.mine, *self.parts)

    def first(self):
        self.moving = self.at.cross(self.order.tie(self.line), False)

    def got_first(self):
        self.got = self.order.got(self.moving)

    def join(self):
        self.both = self.order.do(lambda *v: jnp.concatenate(v), self.line, self.got)

    def second(self):
        both = self.order.tie(self.both)
        self.moving = self.at.cross(both, True)
        self.other = self.at.swap_core(both)

    def got_second(self):
        self.third = self.order.got(self.moving)

    def cores(self):
        self.other_third = self.at.swap_core(self.order.tie(self.third))

    def pieces(self):
        other, other_third = self.order.got(self.other, self.other_third)
        return self.both, self.third, other, other_third


class Scatter:
    def __init__(self, at, order, own, send0, send1):
        self.at, self.order, self.own = at, order, own
        self.swaps = at.swap_core(order.tie(send0)), at.swap_core(order.tie(send1))

    def come(self):
        self.got = self.order.got(self.moving)

    def first(self):
        cut = 2 * self.at.nz
        other = self.order.got(self.swaps[0])
        sent = self.order.do(lambda a, b: add(a[:cut], b).astype(BF), self.own, other)
        self.moving = self.at.cross(sent, True)

    def rest(self):
        self.other = self.order.got(self.swaps[1])

    def second(self):
        nz = self.at.nz
        self.crossed = self.got
        sent = self.order.do(
            lambda a, b, c: add(a[2 * nz : 3 * nz], b[:nz], c[:nz]).astype(BF), self.own, self.other, self.crossed
        )
        self.moving = self.at.cross(sent, False)

    def along_z(self):
        nz = self.at.nz
        self.low = self.order.do(
            lambda a, b, c, d: add(a[3 * nz :], b[nz:], c[nz:], d).astype(BF), self.own, self.other, self.crossed, self.got
        )
        self.moving = [self.at.shift_z(self.low[k], k) for k in range(1, nz)]

    def come_z(self):
        parts = self.order.got(*self.moving)
        self.parts = parts if isinstance(parts, tuple) else (parts,)

    def along_x(self):
        total = self.order.do(lambda v, *w: add(v[0], *w).astype(BF), self.low, *self.parts)
        step = 2
        while step < self.at.groups:
            pairs = [(d, d ^ step) for d in range(self.at.groups)]
            total = add(total, lax.ppermute(total, "dp", pairs)).astype(BF)
            step *= 2
        self.total = total
        self.moving = self.at.swap_x(total)

    def cores(self):
        here = self.at.p == self.at.c
        self.keep, send = self.order.do(
            lambda a, b: (jnp.where(here, a, b), jnp.where(here, b, a)), self.total, self.got
        )
        self.moving = self.at.swap_core(send)

    def result(self):
        first = self.at.c == 0
        return self.order.do(
            lambda a, b: jnp.concatenate([jnp.where(first, a, b), jnp.where(first, b, a)]).astype(F32), self.keep, self.got
        )


VM = pl.BlockSpec(memory_space=pltpu.VMEM)
ANY = pl.BlockSpec(memory_space=pl.ANY)
SMEM = pl.BlockSpec(memory_space=pltpu.SMEM)


def nn(left, right):
    return jnp.dot(left, right, preferred_element_type=F32)


def nt(left, right):
    return lax.dot_general(left, right, (((1,), (1,)), ((), ())), preferred_element_type=F32)


def tn(left, right):
    return lax.dot_general(left, right, (((0,), (0,)), ((), ())), preferred_element_type=F32)


def tt(left, right):
    return lax.dot_general(left, right, (((0,), (1,)), ((), ())), preferred_element_type=F32)


def join(parts, axis):
    return jnp.concatenate(parts, axis=axis) if len(parts) > 1 else parts[0]


def call(body, ins, outs, scratch, flops, limit, specs=None, out_specs=None):
    return pl.pallas_call(
        body,
        in_specs=specs or [VM] * len(ins),
        out_specs=out_specs or [VM] * len(outs),
        out_shape=outs,
        scratch_shapes=scratch,
        compiler_params=pltpu.CompilerParams(vmem_limit_bytes=max(limit, 60) * MIB),
        cost_estimate=pl.CostEstimate(flops=1000, bytes_accessed=1000, transcendentals=0),
    )(*ins)


def fetches(order_ref, pieces, dests, sem, base):
    copies = []
    half = pieces[0].shape[1]
    at = 0
    for ref in pieces:
        for j in range(ref.shape[0]):
            row = pl.multiple_of(order_ref[at] * half, half)
            at += 1
            for dest, col in dests:
                whole = col == 0 and dest.shape[1] == ref.shape[2]
                src = ref.at[j] if whole else ref.at[j, :, pl.ds(col, dest.shape[1])]
                copies.append(
                    pltpu.make_async_copy(src, dest.at[pl.ds(row, half), :], sem.at[base + len(copies)])
                )
    return copies


class Copies:
    def __init__(self, sem):
        self.sem, self.used, self.open = sem, 0, []

    def start(self, source, dest):
        copy = pltpu.make_async_copy(source, dest, self.sem.at[self.used])
        self.used += 1
        copy.start()
        return copy

    def store(self, source, dest):
        self.open.append(self.start(source, dest))

    def blocks(self, order_ref, source, first, count, half, own, send0, send1):
        places, part = own.shape[0], send0.shape[0]
        for b in range(first, first + count):
            src = source.at[pl.ds(b * half, half), :]
            sem = self.sem.at[self.used]
            self.used += 1
            to = order_ref[b]

            @pl.when(to < places)
            def _(src=src, to=to, sem=sem):
                pltpu.make_async_copy(src, own.at[to], sem).start()

            @pl.when((to >= places) & (to < places + part))
            def _(src=src, to=to, sem=sem):
                pltpu.make_async_copy(src, send0.at[to - places], sem).start()

            @pl.when(to >= places + part)
            def _(src=src, to=to, sem=sem):
                pltpu.make_async_copy(src, send1.at[to - places - part], sem).start()

            self.open.append(pltpu.make_async_copy(src, own.at[0], sem))

    def close(self):
        wait(self.open)
        self.open = []


def start(copies):
    for copy in copies:
        copy.start()
    return copies


def wait(copies):
    for copy in copies:
        copy.wait()


def inverse_rms(v, width):
    return lax.rsqrt(jnp.sum(v * v, axis=1, keepdims=True) * (1.0 / width) + EPS)


def norm_back(values, gain, grad, width):
    scale = inverse_rms(values, width)
    unit = values * scale
    gain_grad = jnp.sum(grad * unit, axis=0, keepdims=True)
    inner = grad * gain
    mean = jnp.sum(inner * unit, axis=1, keepdims=True) * (1.0 / width)
    return gain_grad, scale * (inner - unit * mean)


class Sizes:
    def __init__(self, n, real, padded, ff, t, kv):
        self.n, self.real, self.padded, self.ff, self.t = n, real, padded, ff, t
        self.width, self.wide = n * real, n * padded
        self.hq, self.kvh = self.width // HEAD_SIZE, kv // HEAD_SIZE
        self.heads = self.hq + 2 * self.kvh
        self.feat = self.heads * HEAD_SIZE
        self.group = self.hq // self.kvh
        self.lse = -(-self.hq // 8) * 8
        self.block = 128 if t % 128 == 0 else t
        self.blocks = t // self.block
        self.tile = 512 if ff % 512 == 0 else ff


def head(ref, h):
    return ref[h * HEAD_SIZE : (h + 1) * HEAD_SIZE, :]


def by_block(sz, parts, op):
    b = sz.block
    return [
        functools.reduce(op, [parts[j][:, b * (i - j) : b * (i - j + 1)] for j in range(i + 1)])
        for i in range(sz.blocks)
    ]


def plus(a, b):
    return a + b


def attention_forward(sz, x, gain, wqkv_t, wo, cos, sin, bias, a1, heads, lse, mixp, mix):
    b, half = sz.block, HEAD_SIZE // 2
    a1[...] = (x * inverse_rms(x, sz.width) * gain).astype(BF)
    step = max(k for k in (5, 4, 3, 2, 1) if sz.heads % k == 0)
    for c in range(0, sz.heads, step):
        part = nt(wqkv_t[c * HEAD_SIZE : (c + step) * HEAD_SIZE, :], a1[...])
        for h in range(c, c + step):
            lo = (h - c) * HEAD_SIZE
            first, second = part[lo : lo + half], part[lo + half : lo + HEAD_SIZE]
            if h < sz.hq + sz.kvh:
                first, second = (
                    first * cos[...] - second * sin[...],
                    second * cos[...] + first * sin[...],
                )
            if h < sz.hq:
                first, second = first * HEAD_SIZE ** (-0.5), second * HEAD_SIZE ** (-0.5)
            heads[h * HEAD_SIZE : h * HEAD_SIZE + half, :] = first.astype(BF)
            heads[h * HEAD_SIZE + half : (h + 1) * HEAD_SIZE, :] = second.astype(BF)
    if sz.lse > sz.hq:
        lse[...] = jnp.zeros(lse.shape, F32)
    for g in range(sz.kvh):
        k = head(heads, sz.hq + g).T
        vt = head(heads, sz.hq + sz.kvh + g)
        for r in range(sz.group):
            h = g * sz.group + r
            q = head(heads, h)
            ss = [
                nn(k[b * j : b * (j + 1)], q[:, b * j :]) + bias[b * j : b * (j + 1), b * j :]
                for j in range(sz.blocks)
            ]
            top = by_block(sz, [jnp.max(s, axis=0, keepdims=True) for s in ss], jnp.maximum)
            sums, out = [], None
            for j in range(sz.blocks):
                e = jnp.exp(ss[j] - join(top[j:], 1))
                sums.append(jnp.sum(e, axis=0, keepdims=True))
                part = nn(vt[:, b * j : b * (j + 1)], e.astype(BF))
                if j:
                    part = jnp.concatenate([jnp.zeros((HEAD_SIZE, b * j), F32), part], axis=1)
                out = part if out is None else out + part
            summed = join(by_block(sz, sums, plus), 1)
            mix[h * HEAD_SIZE : (h + 1) * HEAD_SIZE, :] = out * (1.0 / summed)
            lse[h : h + 1, :] = join(top, 1) + jnp.log(summed)
    row = lax.broadcasted_iota(jnp.int32, (sz.padded, sz.t), 0)
    for j in range(sz.n):
        part = mix[sz.real * j : sz.real * j + sz.padded, :]
        mixp[sz.padded * j : sz.padded * (j + 1), :] = jnp.where(row < sz.real, part, 0.0).astype(BF)
    return x + tn(mixp[...], wo[...])


def attention_backward(sz, gh, gl, x, gain, wqkv_t, wo, cos, sin, bias, heads, lse, gm, g_heads, gs_ref, p_ref, g_qkv, ready=None):
    b, half = sz.block, HEAD_SIZE // 2
    for j in range(sz.n):
        part = nt(wo[sz.padded * j : sz.padded * (j + 1), :], gl) if sz.n < 4 else None
        if part is not None:
            gm[sz.real * j : sz.real * j + sz.padded, :] = part
    if sz.n >= 4:
        quarter = sz.n // 4
        for c in range(4):
            part = nt(wo[sz.padded * quarter * c : sz.padded * quarter * (c + 1), :], gl)
            for j in range(quarter):
                at = sz.real * (quarter * c + j)
                gm[at : at + sz.padded, :] = part[sz.padded * j : sz.padded * (j + 1)]
    if ready is not None:
        ready(False)
    for g in range(sz.kvh):
        kt = head(heads, sz.hq + g)
        k = kt.T
        v = head(heads, sz.hq + sz.kvh + g).T
        gk = gv = None
        for r in range(sz.group):
            h = g * sz.group + r
            q, gmh = head(heads, h), head(gm, h).astype(BF)
            row = lse[h : h + 1, :]
            ps, gps, down = [], [], []
            for j in range(sz.blocks):
                lo = b * j
                s = nn(k[lo : lo + b], q[:, lo:]) + bias[lo : lo + b, lo:]
                p = jnp.exp(s - row[:, lo:])
                gp = nn(v[lo : lo + b], gmh[:, lo:])
                ps.append(p)
                gps.append(gp)
                down.append(jnp.sum(p * gp, axis=0, keepdims=True))
            d = by_block(sz, down, plus)
            for j in range(sz.blocks):
                lo = b * j
                gs_ref[r, lo : lo + b, lo:] = (ps[j] * (gps[j] - join(d[j:], 1))).astype(BF)
                p_ref[r, lo : lo + b, lo:] = ps[j].astype(BF)
            gq = join(
                [
                    nn(kt[:, : b * (i + 1)], gs_ref[r, : b * (i + 1), b * i : b * (i + 1)])
                    for i in range(sz.blocks)
                ],
                1,
            )
            part_k = join([nt(q[:, b * j :], gs_ref[r, b * j : b * (j + 1), b * j :]) for j in range(sz.blocks)], 1)
            part_v = join([nt(gmh[:, b * j :], p_ref[r, b * j : b * (j + 1), b * j :]) for j in range(sz.blocks)], 1)
            g_heads[h * HEAD_SIZE : (h + 1) * HEAD_SIZE, :] = gq * HEAD_SIZE ** (-0.5)
            gk = part_k if gk is None else gk + part_k
            gv = part_v if gv is None else gv + part_v
        at = (sz.hq + g) * HEAD_SIZE
        g_heads[at : at + HEAD_SIZE, :] = gk
        at = (sz.hq + sz.kvh + g) * HEAD_SIZE
        g_qkv[at : at + HEAD_SIZE, :] = gv.astype(BF)
    for h in range(sz.hq + sz.kvh):
        at = h * HEAD_SIZE
        first, second = g_heads[at : at + half, :], g_heads[at + half : at + HEAD_SIZE, :]
        g_qkv[at : at + half, :] = (first * cos[...] + second * sin[...]).astype(BF)
        g_qkv[at + half : at + HEAD_SIZE, :] = (second * cos[...] - first * sin[...]).astype(BF)
    if ready is not None:
        ready(True)
    gain_grad, back = norm_back(x[...], gain, tn(g_qkv[...], wqkv_t[...]), sz.width)
    return gain_grad, gh[...] + back


def ffn_up(sz, hidden, gain, a2, wg, wu, gate, up, inner):
    a2[...] = (hidden * inverse_rms(hidden, sz.width) * gain).astype(BF)
    for c in range(0, sz.ff, sz.tile):
        cols = slice(c, c + sz.tile)
        gate_part = nn(a2[...], wg[:, cols])
        up_part = nn(a2[...], wu[:, cols])
        gate[:, cols] = gate_part.astype(BF)
        up[:, cols] = up_part.astype(BF)
        inner[:, cols] = (gate_part * jax.nn.sigmoid(gate_part) * up_part).astype(BF)


def ffn_backward(sz, grad, cl, hidden, gain, wg, wu, wd, gate, up, gg, gu, ready=None):
    for i, c in enumerate(range(0, sz.ff, sz.tile)):
        cols = slice(c, c + sz.tile)
        if ready is not None:
            ready(i)
        g_inner = nt(cl[...], wd[cols, :])
        z = gate[:, cols].astype(F32)
        sg = jax.nn.sigmoid(z)
        silu = z * sg
        gg[:, cols] = (g_inner * up[:, cols].astype(F32) * (sg + silu * (1.0 - sg))).astype(BF)
        gu[:, cols] = (g_inner * silu).astype(BF)
    if ready is not None:
        ready(-1)
    g_a2 = nt(gg[...], wg[...]) + nt(gu[...], wu[...])
    gain_grad, back = norm_back(hidden[...], gain, g_a2, sz.width)
    return gain_grad, grad + back


def shape(*dims, dtype=BF):
    return jax.ShapeDtypeStruct(dims, dtype)


def halves(sz, half, cols):
    return [shape(sz.n, half, cols)] + [shape(sz.n // 2, half, cols)] * 2


def first_attention(sz, order, pieces, x, cot, rope, bias):
    t, wide = sz.t, sz.wide

    def body(order_ref, p0, p1, p2, p3, x_hbm, cot_hbm, cos, sin, bias_hbm,
             hidden_hbm, a1_hbm, heads_hbm, lse, mixp_hbm, wqkv_t_hbm, wo_hbm, gains, x_out, cot_out,
             x, cot, hidden, a1, heads, mixp, wqkv_t, wo, wqkv, mix, bias_ref, sem, out_sem):
        io = Copies(out_sem)
        wait(start(fetches(order_ref, (p0, p1, p2, p3), [(wqkv, sz.wide)], sem, 0)))
        loads = [io.start(x_hbm, x), io.start(bias_hbm, bias_ref), io.start(cot_hbm, cot)]
        loads += start(fetches(order_ref, (p0, p1, p2, p3), [(wo, 0)], sem, 2 * sz.n))
        rows = []
        for k in range(2):
            parts = []
            for j in range(sz.n):
                lo = sz.padded * (j + 1) - 16
                tile = wqkv[lo : lo + 16, 0:128].astype(F32)
                at = sz.real + k - (sz.padded - 16)
                parts.append(tile[at : at + 1, : sz.padded])
            rows.append(jnp.concatenate(parts, axis=1))
        gains[...] = jnp.concatenate(rows + [jnp.zeros((6, sz.wide), F32)], axis=0)
        wqkv_t[...] = wqkv[...].T
        wait(loads)
        for a, b in ((wqkv_t, wqkv_t_hbm), (wo, wo_hbm), (x, x_out), (cot, cot_out)):
            io.store(a, b)
        hidden[...] = x[...].astype(F32)
        hidden[...] = attention_forward(
            sz, hidden[...], gains[0:1, :], wqkv_t, wo, cos, sin, bias_ref, a1, heads, lse, mixp, mix
        )
        for a, b in ((hidden, hidden_hbm), (a1, a1_hbm), (heads, heads_hbm), (mixp, mixp_hbm)):
            io.store(a, b)
        io.close()

    v = pltpu.VMEM
    return call(
        body,
        [order, *pieces, x, cot, *rope, bias],
        [
            shape(t, wide, dtype=F32), shape(t, wide), shape(sz.feat, t), shape(sz.lse, t, dtype=F32),
            shape(wide, t), shape(sz.feat, wide), shape(wide, wide), shape(8, wide, dtype=F32),
            shape(t, wide), shape(t, wide),
        ],
        [
            v((t, wide), BF), v((t, wide), BF),
            v((t, wide), F32), v((t, wide), BF), v((sz.feat, t), BF), v((wide, t), BF), v((sz.feat, wide), BF),
            v((wide, wide), BF), v((wide, sz.feat), BF), v((sz.width + 16, t), F32), v((t, t), F32),
            pltpu.SemaphoreType.DMA((4 * sz.n,)), pltpu.SemaphoreType.DMA((12,)),
        ],
        6 * t * wide * sz.feat, 40,
        specs=[SMEM] + [ANY] * 6 + [VM] * 2 + [ANY],
        out_specs=[ANY] * 3 + [VM] + [ANY] * 3 + [VM] + [ANY] * 2,
    )


def first_gate(sz, order, pieces, hidden, gains):
    t, wide, ff = sz.t, sz.wide, sz.ff

    def body(order_ref, p0, p1, p2, p3, hidden_hbm, gains_ref, a2_hbm, gate_hbm, w_hbm, hidden_ref, a2, gate, w, sem, out_sem):
        out = Copies(out_sem)
        load = out.start(hidden_hbm, hidden_ref)
        wait([load])
        copies = start(fetches(order_ref, (p0, p1, p2, p3), [(w, 0)], sem, 0))
        hidden = hidden_ref[...]
        a2[...] = (hidden * inverse_rms(hidden, sz.width) * gains_ref[1:2, :]).astype(BF)
        wait(copies)
        out.store(w, w_hbm)
        out.store(a2, a2_hbm)
        for c in range(0, ff, sz.tile):
            cols = slice(c, c + sz.tile)
            gate[:, cols] = nn(a2[...], w[:, cols]).astype(BF)
        out.store(gate, gate_hbm)
        out.close()

    return call(
        body,
        [order, *pieces, hidden, gains],
        [shape(t, wide), shape(t, ff), shape(wide, ff)],
        [pltpu.VMEM((t, wide), F32), pltpu.VMEM((t, wide), BF), pltpu.VMEM((t, ff), BF), pltpu.VMEM((wide, ff), BF),
         pltpu.SemaphoreType.DMA((2 * sz.n,)), pltpu.SemaphoreType.DMA((4,))],
        2 * t * wide * ff, 40,
        specs=[SMEM] + [ANY] * 5 + [VM], out_specs=[ANY] * 3,
    )


def first_up(sz, order, pieces, a2, gate):
    t, wide, ff = sz.t, sz.wide, sz.ff

    def body(order_ref, p0, p1, p2, p3, a2_hbm, gate_hbm, up_hbm, inner_hbm, w_hbm, a2, gate, up, inner, w, sem, out_sem):
        copies = start(fetches(order_ref, (p0, p1, p2, p3), [(w, 0)], sem, 0))
        out = Copies(out_sem)
        copies += [out.start(a2_hbm, a2), out.start(gate_hbm, gate)]
        wait(copies)
        out.store(w, w_hbm)
        for c in range(0, ff, sz.tile):
            cols = slice(c, c + sz.tile)
            part = nn(a2[...], w[:, cols])
            up[:, cols] = part.astype(BF)
            z = gate[:, cols].astype(F32)
            inner[:, cols] = (z * jax.nn.sigmoid(z) * part).astype(BF)
        out.store(inner, inner_hbm)
        out.store(up, up_hbm)
        out.close()

    return call(
        body,
        [order, *pieces, a2, gate],
        [shape(t, ff), shape(t, ff), shape(wide, ff)],
        [pltpu.VMEM((t, wide), BF)] + [pltpu.VMEM((t, ff), BF)] * 3 + [pltpu.VMEM((wide, ff), BF),
         pltpu.SemaphoreType.DMA((2 * sz.n,)), pltpu.SemaphoreType.DMA((5,))],
        2 * t * wide * ff, 40,
        specs=[SMEM] + [ANY] * 6, out_specs=[ANY] * 3,
    )


def middle(sz, order, back, down_pieces, hidden1, inner1, wqkv_t, wo, wg, wu, gains, rope, bias, out_grad, half):
    aligned = isinstance(down_pieces, tuple)
    downs = list(down_pieces) if aligned else [down_pieces]
    t, wide, ff = sz.t, sz.wide, sz.ff

    def body(*refs):
        order_ref, back_ref, refs = refs[0], refs[1], refs[2:]
        down_refs, refs = refs[: len(downs)], refs[len(downs) :]
        (hidden1_hbm, inner1_hbm, wqkv_hbm, wo_hbm, wg_hbm, wu_hbm, gains_ref, cos, sin, bias_hbm, cl_hbm,
         second_hbm, carried_hbm, wd_hbm, a1_hbm, mixp_hbm, a2_hbm, gg_hbm, gu_hbm, gl_hbm, g_qkv_hbm, gain_grads,
         own, send0, send1,
         wd, wqkv_t, wo, wg, wu, inners, cls, x2, hidden, a1, heads, lse, mixp, a2, gate, up, gg, gu, gl, g_qkv,
         bias_ref, mix, g_heads, gs, probs, sem, piece_sem) = refs
        io = Copies(sem)
        if aligned:
            first = start(fetches(order_ref, down_refs, [(wd, 0)], piece_sem, 0))
        else:
            first = [io.start(down_refs[0], wd)]
        run1, run2 = pl.ds(0, t), pl.ds(t, t)
        first += [io.start(inner1_hbm, inners.at[run1, :]), io.start(hidden1_hbm, x2)]
        wait(first)
        loads = [io.start(wqkv_hbm, wqkv_t), io.start(bias_hbm, bias_ref), io.start(wo_hbm, wo)]
        inner1, inner2 = inners.at[run1, :], inners.at[run2, :]
        cl1, cl2 = cls.at[run1, :], cls.at[run2, :]
        x2[...] = x2[...] + nn(inner1[...], wd[...])
        wait(loads)
        sides = [io.start(wg_hbm, wg), io.start(wu_hbm, wu), io.start(cl_hbm, cls.at[run2, :])]
        hidden[...] = attention_forward(
            sz, x2[...], gains_ref[0:1, :], wqkv_t, wo, cos, sin, bias_ref, a1, heads, lse, mixp, mix
        )
        wait(sides)
        keep = io.start(wd, wd_hbm)
        io.store(a1, a1_hbm)
        io.store(mixp, mixp_hbm)
        ffn_up(sz, hidden[...], gains_ref[1:2, :], a2, wg, wu, gate, up, inner2)
        io.store(a2, a2_hbm)
        gl[...] = (hidden[...] + nn(inner2[...], wd[...])).astype(BF)
        out = io.start(gl, second_hbm)
        gain_f, gh = ffn_backward(
            sz, cl2[...].astype(F32), cl2, hidden[...], gains_ref[1:2, :], wg, wu, wd, gate, up, gg, gu
        )
        io.store(gg, gg_hbm)
        io.store(gu, gu_hbm)
        hidden[...] = gh
        wait([out])
        gl[...] = gh.astype(BF)
        io.store(gl, gl_hbm)
        gain_a, g_x = attention_backward(
            sz, hidden, gl[...], x2, gains_ref[0:1, :], wqkv_t, wo, cos, sin, bias_ref, heads, lse,
            mix, g_heads, gs, probs, g_qkv
        )
        io.store(g_qkv, g_qkv_hbm)
        hidden[...] = g_x
        io.store(hidden, carried_hbm)
        cl1[...] = g_x.astype(BF)
        gain_grads[...] = jnp.concatenate([gain_a, gain_f, jnp.zeros((6, wide), F32)], axis=0)
        wait([keep])
        tile = 640 if ff % 640 == 0 and 640 % half == 0 else ff
        for lo in range(0, ff, tile):
            wd[lo : lo + tile, :] = tn(inners[:, lo : lo + tile], cls[...]).astype(BF)
            if aligned:
                io.blocks(back_ref, wd, lo // half, tile // half, half, own, send0, send1)
        if not aligned:
            io.store(wd, own)
        io.close()

    ins = [order, back, *downs, hidden1, inner1, wqkv_t, wo, wg, wu, gains, *rope, bias, out_grad]
    specs = [SMEM] * 2 + [ANY] * len(downs) + [ANY] * 6 + [VM] * 3 + [ANY] * 2
    places = halves(sz, half, wide) if aligned else [shape(ff, wide), shape(8, 128), shape(8, 128)]
    outs = [
        shape(t, wide), shape(t, wide, dtype=F32), shape(ff, wide), shape(t, wide), shape(wide, t), shape(t, wide),
        shape(t, ff), shape(t, ff), shape(t, wide), shape(sz.feat, t), shape(8, wide, dtype=F32), *places,
    ]
    out_specs = [ANY] * 10 + [VM] + [ANY] * 3
    scratch = [
        pltpu.VMEM((ff, wide), BF), pltpu.VMEM((sz.feat, wide), BF), pltpu.VMEM((wide, wide), BF),
        pltpu.VMEM((wide, ff), BF), pltpu.VMEM((wide, ff), BF), pltpu.VMEM((2 * t, ff), BF), pltpu.VMEM((2 * t, wide), BF),
        pltpu.VMEM((t, wide), F32), pltpu.VMEM((t, wide), F32), pltpu.VMEM((t, wide), BF), pltpu.VMEM((sz.feat, t), BF),
        pltpu.VMEM((sz.lse, t), F32), pltpu.VMEM((wide, t), BF), pltpu.VMEM((t, wide), BF), pltpu.VMEM((t, ff), BF),
        pltpu.VMEM((t, ff), BF), pltpu.VMEM((t, ff), BF), pltpu.VMEM((t, ff), BF), pltpu.VMEM((t, wide), BF),
        pltpu.VMEM((sz.feat, t), BF), pltpu.VMEM((t, t), F32), pltpu.VMEM((sz.width + 16, t), F32),
        pltpu.VMEM((sz.feat, t), F32), pltpu.VMEM((sz.group, t, t), BF), pltpu.VMEM((sz.group, t, t), BF),
        pltpu.SemaphoreType.DMA((2 * sz.n + 24,)), pltpu.SemaphoreType.DMA((2 * sz.n,)),
    ]
    return call(body, ins, outs, scratch, 24 * t * wide * ff, 60, specs, out_specs)


def last_ffn(sz, back, grad, hidden, gains, wg, wu, wd, gate, up, a2s, gg2, half):
    t, wide, ff = sz.t, sz.wide, sz.ff

    def body(back_ref, grad_hbm, hidden_hbm, gains_ref, wg_hbm, wu_hbm, wd_hbm, gate_hbm, up_hbm, a2_1, a2_2, gg2_hbm,
             gh_hbm, gl_hbm, gu_hbm, gain_grad, own, send0, send1,
             grad_ref, hidden, cl, wg, wu, wd, gate, up, ggs, gu, gl, a2, sem):
        io = Copies(sem)
        count = ff // sz.tile
        run1, run2 = pl.ds(0, t), pl.ds(t, t)

        def step(i):
            part = pl.ds(i * sz.tile, sz.tile)
            return [
                io.start(wd_hbm.at[part, :], wd.at[part, :]), io.start(gate_hbm.at[:, part], gate.at[:, part]),
                io.start(up_hbm.at[:, part], up.at[:, part]),
            ]

        load = [io.start(grad_hbm, grad_ref)] + step(0)
        wait(load)
        steps, sides, rest = {}, [], []
        for i in range(1, count):
            steps[i] = step(i)
        cl[...] = grad_ref[...].astype(BF)

        def ready(i):
            if i > 0:
                wait(steps[i])
            if i == min(1, count - 1):
                sides.extend([io.start(wg_hbm, wg), io.start(wu_hbm, wu), io.start(hidden_hbm, hidden)])
            if i < 0:
                wait(sides)
                io.store(gu, gu_hbm)
                rest.extend([
                    io.start(a2_1, a2.at[run1, :]), io.start(a2_2, a2.at[run2, :]), io.start(gg2_hbm, ggs.at[run2, :])
                ])

        gain_f, gh = ffn_backward(
            sz, grad_ref[...], cl, hidden, gains_ref[1:2, :], wg, wu, wd, gate, up, ggs.at[run1, :], gu, ready
        )
        hidden[...] = gh
        gl[...] = gh.astype(BF)
        io.store(hidden, gh_hbm)
        io.store(gl, gl_hbm)
        gain_grad[...] = jnp.concatenate([gain_f, jnp.zeros((7, wide), F32)], axis=0)
        wait(rest)
        tile = 256 if wide % 256 == 0 else wide
        for lo in range(0, wide, tile):
            wg[lo : lo + tile, :] = tn(a2[:, lo : lo + tile], ggs[...]).astype(BF)
            io.blocks(back_ref, wg, lo // half, tile // half, half, own, send0, send1)
        io.close()

    v = pltpu.VMEM
    return call(
        body,
        [back, grad, hidden, gains, wg, wu, wd, gate, up, *a2s, gg2],
        [shape(t, wide, dtype=F32), shape(t, wide), shape(t, ff), shape(8, wide, dtype=F32), *halves(sz, half, ff)],
        [
            v((t, wide), F32), v((t, wide), F32), v((t, wide), BF), v((wide, ff), BF), v((wide, ff), BF), v((ff, wide), BF),
            v((t, ff), BF), v((t, ff), BF), v((2 * t, ff), BF), v((t, ff), BF), v((t, wide), BF), v((2 * t, wide), BF),
            pltpu.SemaphoreType.DMA((3 * (ff // sz.tile) + 2 * sz.n + 16,)),
        ],
        10 * t * wide * ff, 56,
        specs=[SMEM] + [ANY] * 2 + [VM] + [ANY] * 8, out_specs=[ANY] * 3 + [VM] + [ANY] * 3,
    )


def settle(*arrays):
    def body(*refs):
        for a, b in zip(refs[: len(arrays)], refs[len(arrays) :]):
            b[...] = a[...]

    return call(body, list(arrays), [shape(*a.shape, dtype=a.dtype) for a in arrays], [], 0, 20)


def last_attention(sz, back, gh, gl, x, gains, wqkv_t, wo, rope, bias, heads, lse, a2s, gus, mixps, gl2, half):
    t, wide, ff = sz.t, sz.wide, sz.ff
    cols = ff + wide

    def body(back_ref, gh_hbm, gl_hbm, x_hbm, gains_ref, wqkv_hbm, wo_hbm, cos, sin, bias_hbm, heads_hbm, lse_ref,
             a2_1, a2_2, gu_1, gu_2, m1, m2, gl_2,
             g_x_hbm, g_qkv_hbm, gain_grad, own, send0, send1,
             gh, gls, x_low, x, wqkv_t, wo, bias_ref, heads, g_qkv, mix, g_heads, gs, probs, a2, gu, mixp, out, sem):
        io = Copies(sem)
        run1, run2 = pl.ds(0, t), pl.ds(t, t)
        gl = gls.at[run1, :]
        first = [
            io.start(m1, mixp.at[:, run1]), io.start(m2, mixp.at[:, run2]),
            io.start(gl_hbm, gl), io.start(gl_2, gls.at[run2, :]),
        ]
        wait(first)
        second = [
            io.start(a2_1, a2.at[run1, :]), io.start(a2_2, a2.at[run2, :]),
            io.start(gu_1, gu.at[run1, :]), io.start(gu_2, gu.at[run2, :]),
        ]
        tile = 256 if wide % 256 == 0 else wide
        for lo in range(0, wide, tile):
            out[lo : lo + tile, ff:cols] = nn(mixp[lo : lo + tile, :], gls[...]).astype(BF)
        wait(second)
        third = [
            io.start(wo_hbm, wo), io.start(heads_hbm, heads), io.start(bias_hbm, bias_ref),
            io.start(wqkv_hbm, wqkv_t), io.start(gh_hbm, gh), io.start(x_hbm, x_low),
        ]
        for lo in range(0, wide, tile):
            out[lo : lo + tile, 0:ff] = tn(a2[:, lo : lo + tile], gu[...]).astype(BF)
            io.blocks(back_ref, out, lo // half, tile // half, half, own, send0, send1)
        wait(third)
        x[...] = x_low[...].astype(F32)
        gain_a, back_x = attention_backward(
            sz, gh, gl[...], x, gains_ref[0:1, :], wqkv_t, wo, cos, sin, bias_ref,
            heads, lse_ref, mix, g_heads, gs, probs, g_qkv
        )
        io.store(g_qkv, g_qkv_hbm)
        gl[...] = back_x.astype(BF)
        io.store(gl, g_x_hbm)
        gain_grad[...] = jnp.concatenate([gain_a, jnp.zeros((7, wide), F32)], axis=0)
        io.close()

    v = pltpu.VMEM
    return call(
        body,
        [back, gh, gl, x, gains, wqkv_t, wo, *rope, bias, heads, lse, *a2s, *gus, *mixps, gl2],
        [shape(t, wide), shape(sz.feat, t), shape(8, wide, dtype=F32), *halves(sz, half, cols)],
        [
            v((t, wide), F32), v((2 * t, wide), BF), v((t, wide), BF), v((t, wide), F32), v((sz.feat, wide), BF),
            v((wide, wide), BF), v((t, t), F32), v((sz.feat, t), BF), v((sz.feat, t), BF), v((sz.width + 16, t), F32),
            v((sz.feat, t), F32), v((sz.group, t, t), BF), v((sz.group, t, t), BF),
            v((2 * t, wide), BF), v((2 * t, ff), BF), v((wide, 2 * t), BF), v((wide, cols), BF),
            pltpu.SemaphoreType.DMA((2 * sz.n + 32,)),
        ],
        10 * t * wide * sz.feat, 56,
        specs=[SMEM] + [ANY] * 3 + [VM] + [ANY] * 2 + [VM] * 2 + [ANY] * 2 + [VM] + [ANY] * 7,
        out_specs=[ANY] * 2 + [VM] + [ANY] * 3,
    )


def qkv_grad(sz, back, a1s, g_qkv_runs, gain2, gain_f1, gain_a1, half):
    t, wide, cols = sz.t, sz.wide, sz.feat

    def body(back_ref, a_1, a_2, g1, g2, gain2_ref, gain_f_ref, gain_a_ref, own, send0, send1, a1, g_qkv, out, sem):
        io = Copies(sem)
        run1, run2 = pl.ds(0, t), pl.ds(t, t)
        wait([
            io.start(a_1, a1.at[run1, :]), io.start(a_2, a1.at[run2, :]),
            io.start(g1, g_qkv.at[:, run1]), io.start(g2, g_qkv.at[:, run2]),
        ])
        tile = 256 if wide % 256 == 0 else wide
        row = lax.broadcasted_iota(jnp.int32, (sz.padded, sz.padded), 0)
        for lo in range(0, wide, tile):
            into = tt(a1[:, lo : lo + tile], g_qkv[...])
            patches = []
            for s in range(lo, lo + tile, sz.padded):
                here = slice(s, s + sz.padded)
                attn_gain = gain_a_ref[0:1, here] + gain2_ref[0:1, here]
                ffn_gain = gain_f_ref[0:1, here] + gain2_ref[1:2, here]
                patches.append(
                    jnp.where(row == sz.real, attn_gain, jnp.where(row == sz.real + 1, ffn_gain, 0.0))
                )
            patch = jnp.concatenate([join(patches, 0), jnp.zeros((tile, 128 - sz.padded), F32)], axis=1)
            out[lo : lo + tile, 0:128] = (into[:, :128] + patch).astype(BF)
            out[lo : lo + tile, 128:cols] = into[:, 128:].astype(BF)
            io.blocks(back_ref, out, lo // half, tile // half, half, own, send0, send1)
        io.close()

    v = pltpu.VMEM
    return call(
        body,
        [back, *a1s, *g_qkv_runs, gain2, gain_f1, gain_a1],
        halves(sz, half, cols),
        [v((2 * t, wide), BF), v((cols, 2 * t), BF), v((wide, cols), BF), pltpu.SemaphoreType.DMA((2 * sz.n + 8,))],
        4 * t * wide * cols, 40,
        specs=[SMEM] + [ANY] * 4 + [VM] * 3, out_specs=[ANY] * 3,
    )


def spread(v, n, real, padded):
    lead = v.shape[:-1]
    v = v.reshape(lead + (n, real))
    v = jnp.pad(v, [(0, 0)] * len(lead) + [(0, 0), (0, padded - real)])
    return v.reshape(lead + (n * padded,))


def narrow(v, n, real, padded):
    lead = v.shape[:-1]
    return v.reshape(lead + (n, padded))[..., :real].reshape(lead + (n * real,))


def place_blocks(order, pieces):
    both = jnp.concatenate(pieces)
    spots = jnp.zeros(order.shape, jnp.int32).at[order].set(jnp.arange(order.shape[0], dtype=jnp.int32))
    return jnp.take(both, spots, axis=0).reshape(-1, both.shape[2])


def order_blocks(order, grad, half):
    spots = jnp.zeros(order.shape, jnp.int32).at[order].set(jnp.arange(order.shape[0], dtype=jnp.int32))
    both = jnp.take(grad.reshape(-1, half, grad.shape[1]), spots, axis=0)
    cut = order.shape[0] // 4
    return both[: 2 * cut], both[2 * cut : 3 * cut], both[3 * cut :]


def shards(mesh, tokens, lengths, w_query, key_weight, value_weight, output_weight, w_gate, w_up, w_down, gain_attn, gain_ffn, out_grad):
    at = Place(mesh)
    n = at.n
    real, width = w_query.shape
    padded = -(-(real + 2) // 16) * 16
    sz = Sizes(n, real, padded, w_gate.shape[1], tokens.shape[0], key_weight.shape[1])
    wide, ff = sz.wide, sz.ff
    half, down_half = padded // 2, w_down.shape[0] // 2
    aligned = down_half % 16 == 0
    order = Order()
    places, back = at.piece_order(), at.grad_order()

    def pad_rows(v):
        return jnp.pad(v, ((0, padded - v.shape[0]), (0, 0)))

    def attention_shard(w_query, key_weight, value_weight, output_weight, gain_attn, gain_ffn):
        qkv = jnp.concatenate([w_query, key_weight, value_weight], axis=1)
        gains = jnp.pad(jnp.stack([gain_attn, gain_ffn]), ((0, 0), (0, qkv.shape[1] - real)))
        qkv = pad_rows(jnp.concatenate([qkv, gains]))
        return jnp.concatenate([pad_rows(spread(output_weight, n, real, padded)), qkv], axis=1)

    def tables(lengths, tokens, out_grad):
        positions, allowed = layout(lengths, tokens.shape[0])
        bias = jnp.where(allowed[0], 0.0, -1e30).astype(F32).T
        return rotation(positions[0]), bias, spread(tokens, n, real, padded), spread(out_grad, n, real, padded)

    ga, gg, gu, gd = (Gather(at, order) for _ in range(4))
    ga.start(attention_shard, w_query, key_weight, value_weight, output_weight, gain_attn, gain_ffn)
    ga.ready()
    ga.along_z()
    gg.start(pad_rows, w_gate)
    gu.start(pad_rows, w_up)
    gd.start(lambda v: spread(v, n, real, padded), w_down)
    gu.ready()
    gd.ready()
    rope, bias, x1, cot = order.do(tables, lengths, tokens, out_grad)
    ga.come()
    ga.line_up()
    ga.first()
    gg.ready()
    gg.along_z()
    gg.come()
    gu.along_z()
    gg.line_up()
    ga.got_first()
    ga.join()
    ga.second()
    gg.first()
    x1, cot = order.do(settle, x1, cot)
    gu.come()
    gu.line_up()
    ga.got_second()
    ga.cores()
    gg.got_first()
    gg.join()
    gg.second()
    gu.first()
    gd.along_z()
    hidden1, a1_1, heads1, lse1, mixp1, wqkv_t, wo, gains, x1, cot = order.do(
        lambda *v: first_attention(sz, *v), places, ga.pieces(), x1, cot, rope, bias
    )
    gd.come()
    gd.line_up()
    gd.first()
    gg.got_second()
    gg.cores()
    gu.got_first()
    gu.join()
    gu.second()
    a2_1, gate1, wg = order.do(lambda *v: first_gate(sz, *v), places, gg.pieces(), hidden1, gains)
    gd.got_first()
    gd.join()
    gd.second()
    gu.got_second()
    gu.cores()
    up1, inner1, wu = order.do(lambda *v: first_up(sz, *v), places, gu.pieces(), a2_1, gate1)
    gd.got_second()
    gd.cores()
    down_pieces = gd.pieces()
    if not aligned:
        down_pieces = place_blocks(places, down_pieces)

    (second, carried, wd, a1_2, mixp2, a2_2, gg2, gu2, gl2, g_qkv2, gain2, own, *send) = order.do(
        lambda *v: middle(sz, *v, down_half),
        places, back, down_pieces, hidden1, inner1, wqkv_t, wo, wg, wu, gains, rope, bias, cot,
    )
    if not aligned:
        own, *send = order_blocks(back, own, down_half)
    sd = Scatter(at, order, own, *send)
    sd.first()
    sd.rest()
    gh1, gl1, gu1, gain_f1, own, *send = order.do(
        lambda *v: last_ffn(sz, *v, half), back, carried, hidden1, gains, wg, wu, wd, gate1, up1, (a2_1, a2_2), gg2
    )
    sd.come()
    sd.second()
    sg = Scatter(at, order, own, *send)
    sg.first()
    sg.rest()
    g_x, g_qkv1, gain_a1, own, *send = order.do(
        lambda *v: last_attention(sz, *v, half), back, gh1, gl1, x1, gains, wqkv_t, wo, rope, bias, heads1, lse1,
        (a2_1, a2_2), (gu1, gu2), (mixp1, mixp2), gl2
    )
    sd.come()
    sg.come()
    su = Scatter(at, order, own, *send)
    sg.second()
    su.first()
    su.rest()
    sd.along_z()
    own, *send = order.do(
        lambda *v: qkv_grad(sz, *v, half), back, (a1_1, a1_2), (g_qkv1, g_qkv2), gain2, gain_f1, gain_a1
    )
    sg.come()
    sa = Scatter(at, order, own, *send)
    sg.along_z()
    sa.first()
    sa.rest()
    su.come()
    su.second()
    second, g_x = order.do(lambda *v: tuple(narrow(a, n, real, padded) for a in v), second, g_x)
    sa.come()
    sa.second()
    sd.come_z()
    sd.along_x()
    su.come()
    su.along_z()
    sa.come()
    sa.along_z()
    sg.come_z()
    sg.along_x()
    sd.come()
    sd.cores()
    sg.come()
    sg.cores()
    sd.come()
    r_down = sd.result()
    sg.come()
    r_gate = sg.result()
    sa.come_z()
    sa.along_x()
    su.come_z()
    su.along_x()
    sa.come()
    sa.cores()
    su.come()
    su.cores()
    sa.come()
    r_in = sa.result()
    su.come()
    r_up = su.result()
    kv = key_weight.shape[1]
    return (
        second,
        g_x,
        r_in[:real, :width],
        r_in[:real, width : width + kv],
        r_in[:real, width + kv :],
        narrow(r_up[:real, ff:], n, real, padded),
        r_gate[:real],
        r_up[:real, :ff],
        narrow(r_down, n, real, padded),
        r_in[real, :real],
        r_in[real + 1, :real],
    )


def solution(mesh):
    rows, split, gain = P(("dp", "fsdp"), None), P("fsdp", None), P("fsdp")
    return jax.shard_map(
        functools.partial(shards, mesh),
        mesh=mesh,
        in_specs=(rows, rows) + (split,) * 7 + (gain, gain, rows),
        out_specs=(rows, rows) + (split,) * 7 + (gain, gain),
        check_vma=False,
    )
```

```python
import functools
import math

import jax
import jax.numpy as jnp
from jax import lax
from jax.experimental import pallas as pl
from jax.experimental.pallas import tpu as pltpu
from jax.sharding import PartitionSpec as P

HEAD_SIZE = 64
GROUP = 3
ROPE_BASE = 10000.0
EPS = 1e-05
BF = jnp.bfloat16
F32 = jnp.float32
MIB = 1024 * 1024


def layout(doc_lengths, token_count):
    ends = jnp.cumsum(doc_lengths, axis=1)
    starts = ends - doc_lengths
    place = jnp.arange(token_count, dtype=jnp.int32)
    document = jnp.sum((place[None, :, None] >= ends[:, None, :]).astype(jnp.int32), axis=2)
    inside = place[None, :] < ends[:, -1:]
    segment = jnp.where(inside, document, -1)
    chosen = (
        document[:, :, None] == jnp.arange(doc_lengths.shape[1], dtype=jnp.int32)[None, None, :]
    )
    begin = jnp.sum(jnp.where(chosen, starts[:, None, :], 0), axis=2)
    positions = jnp.where(inside, place[None, :] - begin, 0)
    causal = place[:, None] >= place[None, :]
    same = (segment[:, :, None] == segment[:, None, :]) & (segment[:, :, None] >= 0)
    allowed = same & causal[None] | (place[:, None] == place[None, :])[None]
    return (positions, allowed)


def rotation(positions):
    half = HEAD_SIZE // 2
    frequency = jnp.exp(jnp.arange(half, dtype=F32) * (-2.0 * math.log(ROPE_BASE) / HEAD_SIZE))
    angle = positions.astype(F32)[None, :] * frequency[:, None]
    return (jnp.cos(angle), jnp.sin(angle))


class Place:
    def __init__(self, mesh):
        self.n, self.groups = mesh.shape["fsdp"], mesh.shape["dp"]
        self.nz = self.n // 4
        i = lax.axis_index("fsdp")
        self.c, self.y, self.z = i % 2, (i // 2) % 2, i // 4
        self.p = lax.axis_index("dp") % 2

    def swap_core(self, v):
        return lax.ppermute(v, "fsdp", [(i, i ^ 1) for i in range(self.n)])

    def shift_z(self, v, k):
        return lax.ppermute(v, "fsdp", [(i, (i + 4 * k) % self.n) for i in range(self.n)])

    def swap_x(self, v):
        return lax.ppermute(v, "dp", [(d, d ^ 1) for d in range(self.groups)])

    def cross(self, v, first):
        pairs = []
        for d in range(self.groups):
            for i in range(self.n):
                along_x = (i % 2 == 0) == first
                e, j = (d ^ 1, i) if along_x else (d, i ^ 2)
                pairs.append((d * self.n + i, e * self.n + j))
        return lax.ppermute(v, ("dp", "fsdp"), pairs)

    def piece_order(self):
        order = []
        for h in (self.c, 1 - self.c):
            for j in range(4 * self.nz):
                dz, slot = j % self.nz, j // self.nz
                lo, hi = slot % 2, slot // 2
                dy, dc = jnp.where(h == 0, lo, hi), jnp.where(h == 0, hi, lo)
                z = (self.z - dz + self.nz) % self.nz
                order.append((((z * 2 + (self.y ^ dy)) * 2 + (self.p ^ dc)) * 2 + h).astype(jnp.int32))
        return jnp.stack(order)

    def grad_order(self):
        order = [(self.z + k) % self.nz for k in range(self.nz)]
        for h in (self.c, 1 - self.c):
            for hi in (0, 1):
                for lo in (0, 1):
                    of_c, of_y = jnp.where(h == 0, hi, lo), jnp.where(h == 0, lo, hi)
                    c = jnp.where(of_c == 1, self.p, 1 - self.p)
                    y = jnp.where(of_y == 1, self.y, 1 - self.y)
                    order.append((y * 2 + c) * 2 + h)
        return jnp.stack(order).astype(jnp.int32)


def pick(v, k, axis=0):
    return lax.dynamic_index_in_dim(v, k, axis, keepdims=False)


class Order:
    def __init__(self):
        self.last = ()

    def do(self, step, *inputs):
        leaves, tree = jax.tree.flatten(inputs)
        if self.last:
            leaves = lax.optimization_barrier((*leaves, *self.last))[: len(leaves)]
        out = step(*jax.tree.unflatten(tree, leaves))
        self.last = (jax.tree.leaves(out)[0],)
        return out

    def tie(self, v):
        return lax.optimization_barrier((v, *self.last))[0] if self.last else v

    def got(self, *received):
        out = lax.optimization_barrier((*received, *self.last))[: len(received)]
        self.last = (out[0],)
        return out[0] if len(out) == 1 else out


def add(*terms):
    return functools.reduce(lambda a, b: a + b, [t.astype(F32) for t in terms])


class Gather:
    def __init__(self, at, order):
        self.at, self.order = at, order

    def start(self, make, *inputs):
        def step(*inputs):
            shard = make(*inputs)
            halves = shard.reshape(2, shard.shape[0] // 2, shard.shape[1])
            return pick(halves, self.at.c), pick(halves, 1 - self.at.c)

        self.keep, send = self.order.do(step, *inputs)
        self.moving = self.at.swap_core(send)

    def ready(self):
        at = self.at
        got = self.order.got(self.moving)
        self.mine = self.order.do(lambda k, g: jnp.where(at.p == at.c, k, g)[None], self.keep, got)

    def along_z(self):
        mine = self.order.tie(self.mine)
        self.moving = [self.at.shift_z(mine, k) for k in range(1, self.at.nz)]

    def come(self):
        parts = self.order.got(*self.moving)
        self.parts = parts if isinstance(parts, tuple) else (parts,)

    def line_up(self):
        self.line = self.order.do(lambda *v: jnp.concatenate(v), self.mine, *self.parts)

    def first(self):
        self.moving = self.at.cross(self.order.tie(self.line), False)

    def got_first(self):
        self.got = self.order.got(self.moving)

    def second(self):
        self.both = self.order.do(lambda *v: jnp.concatenate(v), self.line, self.got)
        self.moving = self.at.cross(self.both, True)
        self.others = []

    def got_second(self):
        self.third = self.order.got(self.moving)

    def cores(self, *which):
        self.others += [self.at.swap_core(self.order.tie(v)) for v in which or (self.both, self.third)]

    def pieces(self):
        return (self.both, self.third, *self.order.got(*self.others))


class Scatter:
    def __init__(self, at, order, own, *send):
        self.at, self.order, self.own = at, order, own
        self.send, self.swaps, self.other = send, {}, {}

    def core(self, k):
        self.swaps[k] = self.at.swap_core(self.order.tie(self.send[k]))

    def sums(self, *terms):
        cuts = [(lo, lo + count) for _, lo, count in terms]

        def step(*v):
            return add(*[a[lo:hi] for a, (lo, hi) in zip(v, cuts)]).astype(BF)

        return self.order.do(step, *[a for a, _, _ in terms])

    def come(self):
        self.got = self.order.got(self.moving)

    def come_core(self, k):
        self.other[k] = self.order.got(self.swaps[k])

    def first(self):
        two = 2 * self.at.nz
        self.moving = self.at.cross(self.sums((self.own, 0, two), (self.other[0], 0, two)), True)

    def second(self):
        nz = self.at.nz
        self.crossed = self.got
        sent = self.sums((self.own, 2 * nz, nz), (self.other[1], 0, nz), (self.crossed, 0, nz))
        self.moving = self.at.cross(sent, False)

    def along_z(self):
        nz = self.at.nz
        self.low = self.sums((self.own, 3 * nz, nz), (self.other[1], nz, nz), (self.crossed, nz, nz), (self.got, 0, nz))
        self.moving = [self.at.shift_z(self.low[k : k + 1], k) for k in range(1, nz)]

    def come_z(self):
        parts = self.order.got(*self.moving)
        self.parts = parts if isinstance(parts, tuple) else (parts,)

    def along_x(self):
        total = self.sums((self.low, 0, 1), *[(p, 0, 1) for p in self.parts])[0]
        step = 2
        while step < self.at.groups:
            pairs = [(d, d ^ step) for d in range(self.at.groups)]
            total = add(total, lax.ppermute(total, "dp", pairs)).astype(BF)
            step *= 2
        self.total = total
        self.moving = self.at.swap_x(total)

    def cores(self):
        here = self.at.p == self.at.c
        self.keep, send = self.order.do(
            lambda a, b: (jnp.where(here, a, b), jnp.where(here, b, a)), self.total, self.got
        )
        self.moving = self.at.swap_core(send)

    def result(self):
        first = self.at.c == 0
        return self.order.do(
            lambda a, b: jnp.concatenate([jnp.where(first, a, b), jnp.where(first, b, a)]).astype(F32), self.keep, self.got
        )


VM = pl.BlockSpec(memory_space=pltpu.VMEM)
ANY = pl.BlockSpec(memory_space=pl.ANY)
SMEM = pl.BlockSpec(memory_space=pltpu.SMEM)


def nn(left, right):
    return jnp.dot(left, right, preferred_element_type=F32)


def nt(left, right):
    return lax.dot_general(left, right, (((1,), (1,)), ((), ())), preferred_element_type=F32)


def tn(left, right):
    return lax.dot_general(left, right, (((0,), (0,)), ((), ())), preferred_element_type=F32)


def tt(left, right):
    return lax.dot_general(left, right, (((0,), (1,)), ((), ())), preferred_element_type=F32)


def join(parts, axis):
    return jnp.concatenate(parts, axis=axis) if len(parts) > 1 else parts[0]


def call(body, ins, outs, scratch, flops, limit, specs=None, out_specs=None):
    return pl.pallas_call(
        body,
        in_specs=specs or [VM] * len(ins),
        out_specs=out_specs or [VM] * len(outs),
        out_shape=outs,
        scratch_shapes=scratch,
        compiler_params=pltpu.CompilerParams(vmem_limit_bytes=max(limit, 60) * MIB),
        cost_estimate=pl.CostEstimate(flops=1000, bytes_accessed=1000, transcendentals=0),
    )(*ins)


def fetches(order_ref, pieces, dests, sem, base):
    copies = []
    half = pieces[0].shape[1]
    at = 0
    for ref in pieces:
        for j in range(ref.shape[0]):
            row = pl.multiple_of(order_ref[at] * half, half)
            at += 1
            for dest, col in dests:
                whole = col == 0 and dest.shape[1] == ref.shape[2]
                src = ref.at[j] if whole else ref.at[j, :, pl.ds(col, dest.shape[1])]
                copies.append(
                    pltpu.make_async_copy(src, dest.at[pl.ds(row, half), :], sem.at[base + len(copies)])
                )
    return copies


class Copies:
    def __init__(self, sem):
        self.sem, self.used, self.open = sem, 0, []

    def start(self, source, dest):
        copy = pltpu.make_async_copy(source, dest, self.sem.at[self.used])
        self.used += 1
        copy.start()
        return copy

    def store(self, source, dest):
        self.open.append(self.start(source, dest))

    def blocks(self, order_ref, nz, k, source, base, half, own, sends):
        for quarter in range(4):
            place, part = quarter % 2 * nz + k, quarter // 2
            for first, dest in ((0, own.at[2 * nz * part + place]), (4, sends[part].at[place])):
                row = base + pl.multiple_of(order_ref[nz + first + quarter] * half, half)
                self.store(source.at[pl.ds(row, half), :], dest)

    def close(self):
        wait(self.open)
        self.open = []


def start(copies):
    for copy in copies:
        copy.start()
    return copies


def wait(copies):
    for copy in copies:
        copy.wait()


def inverse_rms(v, width):
    return lax.rsqrt(jnp.sum(v * v, axis=1, keepdims=True) * (1.0 / width) + EPS)


def norm_back(values, gain, grad, width):
    scale = inverse_rms(values, width)
    unit = values * scale
    gain_grad = jnp.sum(grad * unit, axis=0, keepdims=True)
    inner = grad * gain
    mean = jnp.sum(inner * unit, axis=1, keepdims=True) * (1.0 / width)
    return gain_grad, scale * (inner - unit * mean)


class Sizes:
    def __init__(self, n, real, padded, ff, t, kv):
        self.n, self.real, self.padded, self.ff, self.t = n, real, padded, ff, t
        self.width, self.wide = n * real, n * padded
        self.hq, self.kvh = self.width // HEAD_SIZE, kv // HEAD_SIZE
        self.heads = self.hq + 2 * self.kvh
        self.feat = self.heads * HEAD_SIZE
        self.group = self.hq // self.kvh
        self.lse = -(-self.hq // 8) * 8
        self.block = 128 if t % 128 == 0 else t
        self.blocks = t // self.block
        self.tile = 512 if ff % 512 == 0 else ff


def head(ref, h):
    return ref[h * HEAD_SIZE : (h + 1) * HEAD_SIZE, :]


def by_block(sz, parts, op):
    b = sz.block
    return [
        functools.reduce(op, [parts[j][:, b * (i - j) : b * (i - j + 1)] for j in range(i + 1)])
        for i in range(sz.blocks)
    ]


def plus(a, b):
    return a + b


def attention_forward(sz, x, gain, wqkv, wo, cos, sin, bias, a1, heads, lse, mixp, mix, done=lambda stage: None):
    b, half = sz.block, HEAD_SIZE // 2
    a1[...] = (x * inverse_rms(x, sz.width) * gain).astype(BF)
    for c in range(0, sz.heads, 4):
        end = min(c + 4, sz.heads)
        part = tt(wqkv[:, c * HEAD_SIZE : end * HEAD_SIZE], a1[...])
        for h in range(c, end):
            lo = (h - c) * HEAD_SIZE
            first, second = part[lo : lo + half], part[lo + half : lo + HEAD_SIZE]
            if h < sz.hq + sz.kvh:
                first, second = (
                    first * cos[...] - second * sin[...],
                    second * cos[...] + first * sin[...],
                )
            if h < sz.hq:
                first, second = first * HEAD_SIZE ** (-0.5), second * HEAD_SIZE ** (-0.5)
            heads[h * HEAD_SIZE : h * HEAD_SIZE + half, :] = first.astype(BF)
            heads[h * HEAD_SIZE + half : (h + 1) * HEAD_SIZE, :] = second.astype(BF)
    done(0)
    if sz.lse > sz.hq:
        lse[...] = jnp.zeros(lse.shape, F32)
    for g in range(sz.kvh):
        k = head(heads, sz.hq + g).T
        vt = head(heads, sz.hq + sz.kvh + g)
        for r in range(sz.group):
            h = g * sz.group + r
            q = head(heads, h)
            ss = [
                nn(k[b * j : b * (j + 1)], q[:, b * j :]) + bias[b * j : b * (j + 1), b * j :]
                for j in range(sz.blocks)
            ]
            top = by_block(sz, [jnp.max(s, axis=0, keepdims=True) for s in ss], jnp.maximum)
            sums, out = [], None
            for j in range(sz.blocks):
                e = jnp.exp(ss[j] - join(top[j:], 1))
                sums.append(jnp.sum(e, axis=0, keepdims=True))
                part = nn(vt[:, b * j : b * (j + 1)], e.astype(BF))
                if j:
                    part = jnp.concatenate([jnp.zeros((HEAD_SIZE, b * j), F32), part], axis=1)
                out = part if out is None else out + part
            summed = join(by_block(sz, sums, plus), 1)
            mix[h * HEAD_SIZE : (h + 1) * HEAD_SIZE, :] = out * (1.0 / summed)
            lse[h : h + 1, :] = join(top, 1) + jnp.log(summed)
    row = lax.broadcasted_iota(jnp.int32, (sz.padded, sz.t), 0)
    for j in range(sz.n):
        part = mix[sz.real * j : sz.real * j + sz.padded, :]
        mixp[sz.padded * j : sz.padded * (j + 1), :] = jnp.where(row < sz.real, part, 0.0).astype(BF)
    done(1)
    return x + tn(mixp[...], wo[...])


def attention_backward(sz, gh, gl, x, gain, wqkv, wo, cos, sin, bias, heads, lse, gm, g_heads, gs_ref, p_ref, g_qkv, ready=None):
    b, half = sz.block, HEAD_SIZE // 2
    for j in range(sz.n):
        part = nt(wo[sz.padded * j : sz.padded * (j + 1), :], gl) if sz.n < 4 else None
        if part is not None:
            gm[sz.real * j : sz.real * j + sz.padded, :] = part
    if sz.n >= 4:
        quarter = sz.n // 4
        for c in range(4):
            part = nt(wo[sz.padded * quarter * c : sz.padded * quarter * (c + 1), :], gl)
            for j in range(quarter):
                at = sz.real * (quarter * c + j)
                gm[at : at + sz.padded, :] = part[sz.padded * j : sz.padded * (j + 1)]
    if ready is not None:
        ready(False)
    for g in range(sz.kvh):
        kt = head(heads, sz.hq + g)
        k = kt.T
        v = head(heads, sz.hq + sz.kvh + g).T
        gk = gv = None
        for r in range(sz.group):
            h = g * sz.group + r
            q, gmh = head(heads, h), head(gm, h).astype(BF)
            row = lse[h : h + 1, :]
            ps, gps, down = [], [], []
            for j in range(sz.blocks):
                lo = b * j
                s = nn(k[lo : lo + b], q[:, lo:]) + bias[lo : lo + b, lo:]
                p = jnp.exp(s - row[:, lo:])
                gp = nn(v[lo : lo + b], gmh[:, lo:])
                ps.append(p)
                gps.append(gp)
                down.append(jnp.sum(p * gp, axis=0, keepdims=True))
            d = by_block(sz, down, plus)
            for j in range(sz.blocks):
                lo = b * j
                gs_ref[r, lo : lo + b, lo:] = (ps[j] * (gps[j] - join(d[j:], 1))).astype(BF)
                p_ref[r, lo : lo + b, lo:] = ps[j].astype(BF)
            gq = join(
                [
                    nn(kt[:, : b * (i + 1)], gs_ref[r, : b * (i + 1), b * i : b * (i + 1)])
                    for i in range(sz.blocks)
                ],
                1,
            )
            part_k = join([nt(q[:, b * j :], gs_ref[r, b * j : b * (j + 1), b * j :]) for j in range(sz.blocks)], 1)
            part_v = join([nt(gmh[:, b * j :], p_ref[r, b * j : b * (j + 1), b * j :]) for j in range(sz.blocks)], 1)
            g_heads[h * HEAD_SIZE : (h + 1) * HEAD_SIZE, :] = gq * HEAD_SIZE ** (-0.5)
            gk = part_k if gk is None else gk + part_k
            gv = part_v if gv is None else gv + part_v
        at = (sz.hq + g) * HEAD_SIZE
        g_heads[at : at + HEAD_SIZE, :] = gk
        at = (sz.hq + sz.kvh + g) * HEAD_SIZE
        g_qkv[at : at + HEAD_SIZE, :] = gv.astype(BF)
    for h in range(sz.hq + sz.kvh):
        at = h * HEAD_SIZE
        first, second = g_heads[at : at + half, :], g_heads[at + half : at + HEAD_SIZE, :]
        g_qkv[at : at + half, :] = (first * cos[...] + second * sin[...]).astype(BF)
        g_qkv[at + half : at + HEAD_SIZE, :] = (second * cos[...] - first * sin[...]).astype(BF)
    if ready is not None:
        ready(True)
    gain_grad, back = norm_back(x[...], gain, tt(g_qkv[...], wqkv[...]), sz.width)
    return gain_grad, gh[...] + back


def ffn_up(sz, hidden, gain, a2, wg, wu, gate, up, inner):
    a2[...] = (hidden * inverse_rms(hidden, sz.width) * gain).astype(BF)
    for c in range(0, sz.ff, sz.tile):
        cols = slice(c, c + sz.tile)
        gate_part = nn(a2[...], wg[:, cols])
        up_part = nn(a2[...], wu[:, cols])
        gate[:, cols] = gate_part.astype(BF)
        up[:, cols] = up_part.astype(BF)
        inner[:, cols] = (gate_part * jax.nn.sigmoid(gate_part) * up_part).astype(BF)


def ffn_back_tile(cl, wd, gate, up, gg, gu, cols):
    g_inner = nt(cl[...], wd[cols, :])
    z = gate[:, cols].astype(F32)
    sg = jax.nn.sigmoid(z)
    silu = z * sg
    gg[:, cols] = (g_inner * up[:, cols].astype(F32) * (sg + silu * (1.0 - sg))).astype(BF)
    gu[:, cols] = (g_inner * silu).astype(BF)


def ffn_backward(sz, grad, cl, hidden, gain, wg, wu, wd, gate, up, gg, gu):
    for c in range(0, sz.ff, sz.tile):
        ffn_back_tile(cl, wd, gate, up, gg, gu, slice(c, c + sz.tile))
    g_a2 = nt(gg[...], wg[...]) + nt(gu[...], wu[...])
    gain_grad, back = norm_back(hidden[...], gain, g_a2, sz.width)
    return gain_grad, grad + back


def shape(*dims, dtype=BF):
    return jax.ShapeDtypeStruct(dims, dtype)


def halves(sz, half, cols):
    return [shape(sz.n, half, cols)] + [shape(sz.n // 2, half, cols)] * 2


def first_attention(sz, order, pieces, x, rope, bias):
    t, wide = sz.t, sz.wide

    def body(order_ref, p0, p1, p2, p3, x_hbm, cos, sin, bias_hbm,
             hidden_hbm, a1_hbm, heads_hbm, lse, mixp_hbm, gains,
             x, hidden, a1, heads, mixp, wo, wqkv, mix, bias_ref, sem, out_sem):
        io = Copies(out_sem)
        first = start(fetches(order_ref, (p0, p1, p2, p3), [(wqkv, sz.wide)], sem, 0))
        loads = [io.start(x_hbm, x), io.start(bias_hbm, bias_ref)]
        loads += start(fetches(order_ref, (p0, p1, p2, p3), [(wo, 0)], sem, 2 * sz.n))
        wait(first)
        rows = []
        for k in range(2):
            parts = []
            for j in range(sz.n):
                lo = sz.padded * (j + 1) - 16
                tile = wqkv[lo : lo + 16, 0:128].astype(F32)
                at = sz.real + k - (sz.padded - 16)
                parts.append(tile[at : at + 1, : sz.padded])
            rows.append(jnp.concatenate(parts, axis=1))
        gains[...] = jnp.concatenate(rows + [jnp.zeros((6, sz.wide), F32)], axis=0)
        wait(loads)
        hidden[...] = x[...].astype(F32)

        def done(stage):
            for a, b in (((a1, a1_hbm), (heads, heads_hbm)), ((mixp, mixp_hbm),))[stage]:
                io.store(a, b)

        hidden[...] = attention_forward(
            sz, hidden[...], gains[0:1, :], wqkv, wo, cos, sin, bias_ref, a1, heads, lse, mixp, mix, done
        )
        io.store(hidden, hidden_hbm)
        io.close()

    v = pltpu.VMEM
    return call(
        body,
        [order, *pieces, x, *rope, bias],
        [
            shape(t, wide, dtype=F32), shape(t, wide), shape(sz.feat, t), shape(sz.lse, t, dtype=F32),
            shape(wide, t), shape(8, wide, dtype=F32),
        ],
        [
            v((t, wide), BF), v((t, wide), F32), v((t, wide), BF), v((sz.feat, t), BF), v((wide, t), BF),
            v((wide, wide), BF), v((wide, sz.feat), BF), v((sz.width + 16, t), F32), v((t, t), F32),
            pltpu.SemaphoreType.DMA((4 * sz.n,)), pltpu.SemaphoreType.DMA((8,)),
        ],
        6 * t * wide * sz.feat, 40,
        specs=[SMEM] + [ANY] * 5 + [VM] * 2 + [ANY],
        out_specs=[ANY] * 3 + [VM, ANY, VM],
    )


def first_gate(sz, order, pieces, hidden, gains):
    t, wide, ff = sz.t, sz.wide, sz.ff

    def body(order_ref, p0, p1, p2, p3, hidden_hbm, gains_ref, a2_hbm, gate_hbm, hidden_ref, a2, gate, w, sem, out_sem):
        out = Copies(out_sem)
        load = out.start(hidden_hbm, hidden_ref)
        copies = start(fetches(order_ref, (p0, p1, p2, p3), [(w, 0)], sem, 0))
        wait([load])
        hidden = hidden_ref[...]
        a2[...] = (hidden * inverse_rms(hidden, sz.width) * gains_ref[1:2, :]).astype(BF)
        wait(copies)
        out.store(a2, a2_hbm)
        for c in range(0, ff, sz.tile):
            cols = slice(c, c + sz.tile)
            gate[:, cols] = nn(a2[...], w[:, cols]).astype(BF)
            out.store(gate.at[:, pl.ds(c, sz.tile)], gate_hbm.at[:, pl.ds(c, sz.tile)])
        out.close()

    return call(
        body,
        [order, *pieces, hidden, gains],
        [shape(t, wide), shape(t, ff)],
        [pltpu.VMEM((t, wide), F32), pltpu.VMEM((t, wide), BF), pltpu.VMEM((t, ff), BF), pltpu.VMEM((wide, ff), BF),
         pltpu.SemaphoreType.DMA((2 * sz.n,)), pltpu.SemaphoreType.DMA((2 + ff // sz.tile,))],
        2 * t * wide * ff, 40,
        specs=[SMEM] + [ANY] * 5 + [VM], out_specs=[ANY] * 2,
    )


def first_up(sz, order, pieces, a2, gate):
    t, wide, ff = sz.t, sz.wide, sz.ff

    def body(order_ref, p0, p1, p2, p3, a2_hbm, gate_hbm, up_hbm, inner_hbm, a2, gate, up, inner, w, sem, out_sem):
        out = Copies(out_sem)
        loads = [out.start(a2_hbm, a2), out.start(gate_hbm, gate)]
        wait(start(fetches(order_ref, (p0, p1, p2, p3), [(w, 0)], sem, 0)))
        wait(loads)
        for c in range(0, ff, sz.tile):
            cols, part = slice(c, c + sz.tile), pl.ds(c, sz.tile)
            value = nn(a2[...], w[:, cols])
            up[:, cols] = value.astype(BF)
            z = gate[:, cols].astype(F32)
            inner[:, cols] = (z * jax.nn.sigmoid(z) * value).astype(BF)
            out.store(inner.at[:, part], inner_hbm.at[:, part])
            out.store(up.at[:, part], up_hbm.at[:, part])
        out.close()

    return call(
        body,
        [order, *pieces, a2, gate],
        [shape(t, ff), shape(t, ff)],
        [pltpu.VMEM((t, wide), BF)] + [pltpu.VMEM((t, ff), BF)] * 3 + [pltpu.VMEM((wide, ff), BF),
         pltpu.SemaphoreType.DMA((2 * sz.n,)), pltpu.SemaphoreType.DMA((2 + 2 * (ff // sz.tile),))],
        2 * t * wide * ff, 40,
        specs=[SMEM] + [ANY] * 6, out_specs=[ANY] * 2,
    )


def middle(sz, order, back, down_pieces, attn_pieces, gate_pieces, up_pieces, hidden1, inner1, gate1, up1, a2_1, gains, rope, bias,
           out_grad, half, down_half):
    aligned = isinstance(down_pieces, tuple)
    downs = list(down_pieces) if aligned else [down_pieces]
    t, wide, ff = sz.t, sz.wide, sz.ff

    def body(*refs):
        order_ref, back_ref, refs = refs[0], refs[1], refs[2:]
        down_refs, refs = refs[: len(downs)], refs[len(downs) :]
        attn_refs, gate_refs, up_refs, refs = refs[:4], refs[4:8], refs[8:12], refs[12:]
        (hidden1_hbm, inner1_hbm, gate1_hbm, up1_hbm, a2_1_hbm, gains_ref, cos, sin, bias_hbm, cl_hbm,
         second_hbm, wqkv_hbm, wo_hbm, a1_hbm, mixp_hbm, a2_hbm, gu_hbm, gl_hbm, g_qkv_hbm, gh1_hbm, gl1_hbm, gu1_hbm,
         gain_grads, *refs) = refs
        down_out, gate_out, refs = refs[:3], refs[3:6], refs[6:]
        (wd, wqkv, wo, wg, wu, inners, cls, x2, hidden, a1, heads, lse, mixp, a2s, gate, up, ggs, gu, gl, g_qkv,
         bias_ref, mix, g_heads, gs, probs, sem, piece_sem) = refs
        io = Copies(sem)
        if aligned:
            first = start(fetches(order_ref, down_refs, [(wd, 0)], piece_sem, 0))
        else:
            first = [io.start(down_refs[0], wd)]
        run1, run2 = pl.ds(0, t), pl.ds(t, t)
        inner1, inner2 = inners.at[run1, :], inners.at[run2, :]
        cl1, cl2 = cls.at[run1, :], cls.at[run2, :]
        a2, gg1, gg2 = a2s.at[run2, :], ggs.at[run1, :], ggs.at[run2, :]
        first += [io.start(inner1_hbm, inner1), io.start(hidden1_hbm, x2)]
        wait(first)
        loads = start(fetches(order_ref, attn_refs, [(wqkv, wide)], piece_sem, 2 * sz.n))
        loads += start(fetches(order_ref, attn_refs, [(wo, 0)], piece_sem, 4 * sz.n))
        loads += [io.start(bias_hbm, bias_ref)]
        x2[...] = x2[...] + nn(inner1[...], wd[...])
        wait(loads)
        sides = start(fetches(order_ref, gate_refs, [(wg, 0)], piece_sem, 6 * sz.n))
        sides += start(fetches(order_ref, up_refs, [(wu, 0)], piece_sem, 8 * sz.n))
        sides += [io.start(cl_hbm, cl2)]
        hidden[...] = attention_forward(
            sz, x2[...], gains_ref[0:1, :], wqkv, wo, cos, sin, bias_ref, a1, heads, lse, mixp, mix
        )
        wait(sides)
        for a, b in ((a1, a1_hbm), (mixp, mixp_hbm), (wqkv, wqkv_hbm), (wo, wo_hbm)):
            io.store(a, b)
        ffn_up(sz, hidden[...], gains_ref[1:2, :], a2, wg, wu, gate, up, inner2)
        io.store(a2, a2_hbm)
        gl[...] = (hidden[...] + nn(inner2[...], wd[...])).astype(BF)
        out = io.start(gl, second_hbm)
        gain_f, gh = ffn_backward(
            sz, cl2[...].astype(F32), cl2, hidden[...], gains_ref[1:2, :], wg, wu, wd, gate, up, gg2, gu
        )
        gus_out = io.start(gu, gu_hbm)
        loads = [io.start(gate1_hbm, gate), io.start(up1_hbm, up), io.start(a2_1_hbm, a2s.at[run1, :])]
        hidden[...] = gh
        wait([out])
        gl[...] = gh.astype(BF)
        out = io.start(gl, gl_hbm)
        gain_a, g_x = attention_backward(
            sz, hidden, gl[...], x2, gains_ref[0:1, :], wqkv, wo, cos, sin, bias_ref, heads, lse,
            mix, g_heads, gs, probs, g_qkv
        )
        io.store(g_qkv, g_qkv_hbm)
        hidden[...] = g_x
        loads.append(io.start(hidden1_hbm, x2))
        cl1[...] = g_x.astype(BF)
        wait(loads + [out, gus_out])
        gain_f1, gh = ffn_backward(
            sz, hidden[...], cl1, x2, gains_ref[1:2, :], wg, wu, wd, gate, up, gg1, gu
        )
        io.store(gu, gu1_hbm)
        hidden[...] = gh
        gl[...] = gh.astype(BF)
        io.store(hidden, gh1_hbm)
        io.store(gl, gl1_hbm)
        gain_grads[...] = jnp.concatenate([gain_a, gain_f + gain_f1, jnp.zeros((6, wide), F32)], axis=0)
        nz = sz.n // 4
        tile = ff // nz
        for k in range(nz):
            if aligned:
                rows = inners[:, pl.ds(pl.multiple_of(back_ref[k] * tile, tile), tile)]
                wd[k * tile : (k + 1) * tile, :] = tn(rows, cls[...]).astype(BF)
                io.blocks(back_ref, nz, k, wd, k * tile, down_half, down_out[0], down_out[1:])
        if not aligned:
            wd[...] = tn(inners[...], cls[...]).astype(BF)
            io.store(wd, down_out[0])
        tile = wide // nz
        for k in range(nz):
            rows = a2s[:, pl.ds(pl.multiple_of(back_ref[k] * tile, tile), tile)]
            wg[k * tile : (k + 1) * tile, :] = tn(rows, ggs[...]).astype(BF)
            io.blocks(back_ref, nz, k, wg, k * tile, half, gate_out[0], gate_out[1:])
        io.close()

    ins = [order, back, *downs, *attn_pieces, *gate_pieces, *up_pieces, hidden1, inner1, gate1, up1, a2_1, gains, *rope, bias,
           out_grad]
    specs = [SMEM] * 2 + [ANY] * (len(downs) + 17) + [VM] * 3 + [ANY] * 2
    places = halves(sz, down_half, wide) if aligned else [shape(ff, wide)] + [shape(8, 128)] * 2
    outs = [
        shape(t, wide), shape(wide, sz.feat), shape(wide, wide), shape(t, wide), shape(wide, t), shape(t, wide), shape(t, ff),
        shape(t, wide), shape(sz.feat, t), shape(t, wide, dtype=F32), shape(t, wide), shape(t, ff),
        shape(8, wide, dtype=F32), *places, *halves(sz, half, ff),
    ]
    out_specs = [ANY] * 12 + [VM] + [ANY] * 6
    v = pltpu.VMEM
    scratch = [
        v((ff, wide), BF), v((wide, sz.feat), BF), v((wide, wide), BF), v((wide, ff), BF), v((wide, ff), BF),
        v((2 * t, ff), BF), v((2 * t, wide), BF), v((t, wide), F32), v((t, wide), F32), v((t, wide), BF), v((sz.feat, t), BF),
        v((sz.lse, t), F32), v((wide, t), BF), v((2 * t, wide), BF), v((t, ff), BF), v((t, ff), BF), v((2 * t, ff), BF),
        v((t, ff), BF), v((t, wide), BF), v((sz.feat, t), BF), v((t, t), F32), v((sz.width + 16, t), F32),
        v((sz.feat, t), F32), v((sz.group, t, t), BF), v((sz.group, t, t), BF),
        pltpu.SemaphoreType.DMA((4 * sz.n + 40,)), pltpu.SemaphoreType.DMA((10 * sz.n,)),
    ]
    return call(body, ins, outs, scratch, 24 * t * wide * ff, 60, specs, out_specs)


def up_out_grad(sz, back, a2s, grads, mixps, gls, half):
    t, wide, ff = sz.t, sz.wide, sz.ff
    cols = ff + wide

    def body(back_ref, a_1, a_2, g_1, g_2, m1, m2, l1, l2, own, s0, s1, a, g, mixp, gl, out, sem):
        io = Copies(sem)
        run1, run2 = pl.ds(0, t), pl.ds(t, t)
        wait([
            io.start(m1, mixp.at[:, run1]), io.start(m2, mixp.at[:, run2]),
            io.start(l1, gl.at[run1, :]), io.start(l2, gl.at[run2, :]),
        ])
        later = [
            io.start(a_1, a.at[run1, :]), io.start(a_2, a.at[run2, :]),
            io.start(g_1, g.at[run1, :]), io.start(g_2, g.at[run2, :]),
        ]
        nz = sz.n // 4
        tile = wide // nz
        starts = [pl.multiple_of(back_ref[k] * tile, tile) for k in range(nz)]
        for k in range(nz):
            out[k * tile : (k + 1) * tile, ff:cols] = nn(mixp[pl.ds(starts[k], tile), :], gl[...]).astype(BF)
        wait(later)
        for k in range(nz):
            out[k * tile : (k + 1) * tile, 0:ff] = tn(a[:, pl.ds(starts[k], tile)], g[...]).astype(BF)
            io.blocks(back_ref, nz, k, out, k * tile, half, own, (s0, s1))
        io.close()

    v = pltpu.VMEM
    return call(
        body, [back, *a2s, *grads, *mixps, *gls], halves(sz, half, cols),
        [
            v((2 * t, wide), BF), v((2 * t, ff), BF), v((wide, 2 * t), BF), v((2 * t, wide), BF), v((wide, cols), BF),
            pltpu.SemaphoreType.DMA((2 * sz.n + 8,)),
        ],
        4 * t * wide * cols, 48,
        specs=[SMEM] + [ANY] * 8, out_specs=[ANY] * 3,
    )


def settle(*arrays):
    def body(*refs):
        for a, b in zip(refs[: len(arrays)], refs[len(arrays) :]):
            b[...] = a[...]

    return call(body, list(arrays), [shape(*a.shape, dtype=a.dtype) for a in arrays], [], 0, 20)


def last_attention(sz, gh, gl, x, gains, wqkv, wo, rope, bias, heads, lse):
    t, wide = sz.t, sz.wide

    def body(gh_hbm, gl_hbm, x_hbm, gains_ref, wqkv_hbm, wo_hbm, cos, sin, bias_hbm, heads_hbm, lse_ref,
             g_x_hbm, g_qkv_hbm, gain_grad,
             gh, gl, x_low, x, wqkv, wo, bias_ref, heads, g_qkv, mix, g_heads, gs, probs, sem):
        io = Copies(sem)
        first = [io.start(gl_hbm, gl), io.start(wo_hbm, wo)]
        second = [io.start(heads_hbm, heads), io.start(bias_hbm, bias_ref)]
        wait(first)
        later = []

        def ready(last):
            if last:
                wait(later)
                x[...] = x_low[...].astype(F32)
            else:
                wait(second)
                later.extend([io.start(wqkv_hbm, wqkv), io.start(gh_hbm, gh), io.start(x_hbm, x_low)])

        gain_a, back_x = attention_backward(
            sz, gh, gl[...], x, gains_ref[0:1, :], wqkv, wo, cos, sin, bias_ref,
            heads, lse_ref, mix, g_heads, gs, probs, g_qkv, ready
        )
        io.store(g_qkv, g_qkv_hbm)
        gl[...] = back_x.astype(BF)
        io.store(gl, g_x_hbm)
        gain_grad[...] = jnp.concatenate([gain_a, jnp.zeros((7, wide), F32)], axis=0)
        io.close()

    v = pltpu.VMEM
    return call(
        body,
        [gh, gl, x, gains, wqkv, wo, *rope, bias, heads, lse],
        [shape(t, wide), shape(sz.feat, t), shape(8, wide, dtype=F32)],
        [
            v((t, wide), F32), v((t, wide), BF), v((t, wide), BF), v((t, wide), F32), v((wide, sz.feat), BF),
            v((wide, wide), BF), v((t, t), F32), v((sz.feat, t), BF), v((sz.feat, t), BF), v((sz.width + 16, t), F32),
            v((sz.feat, t), F32), v((sz.group, t, t), BF), v((sz.group, t, t), BF), pltpu.SemaphoreType.DMA((16,)),
        ],
        10 * t * wide * sz.feat, 40,
        specs=[ANY] * 3 + [VM] + [ANY] * 2 + [VM] * 2 + [ANY] * 2 + [VM],
        out_specs=[ANY] * 2 + [VM],
    )


def qkv_grad(sz, back, a1s, g_qkv_runs, gain2, gain_a1, half):
    t, wide, cols = sz.t, sz.wide, sz.feat

    def body(back_ref, a_1, a_2, g1, g2, gain2_ref, gain_a_ref, own, s0, s1, a1, g_qkv, out, sem):
        io = Copies(sem)
        run1, run2 = pl.ds(0, t), pl.ds(t, t)
        wait([
            io.start(a_1, a1.at[run1, :]), io.start(a_2, a1.at[run2, :]),
            io.start(g1, g_qkv.at[:, run1]), io.start(g2, g_qkv.at[:, run2]),
        ])
        nz = sz.n // 4
        tile = wide // nz
        row = lax.broadcasted_iota(jnp.int32, (sz.padded, sz.padded), 0)
        for k in range(nz):
            here = pl.ds(pl.multiple_of(back_ref[k] * tile, tile), tile)
            into = tt(a1[:, here], g_qkv[...])
            attn_gain = gain_a_ref[0:1, here] + gain2_ref[0:1, here]
            ffn_gain = gain2_ref[1:2, here]
            patches = []
            for s in range(0, tile, sz.padded):
                a, f = attn_gain[:, s : s + sz.padded], ffn_gain[:, s : s + sz.padded]
                patches.append(jnp.where(row == sz.real, a, jnp.where(row == sz.real + 1, f, 0.0)))
            patch = jnp.concatenate([join(patches, 0), jnp.zeros((tile, 128 - sz.padded), F32)], axis=1)
            lo = k * tile
            out[lo : lo + tile, 0:128] = (into[:, :128] + patch).astype(BF)
            out[lo : lo + tile, 128:cols] = into[:, 128:].astype(BF)
            io.blocks(back_ref, nz, k, out, lo, half, own, (s0, s1))
        io.close()

    v = pltpu.VMEM
    return call(
        body,
        [back, *a1s, *g_qkv_runs, gain2, gain_a1],
        halves(sz, half, cols),
        [v((2 * t, wide), BF), v((cols, 2 * t), BF), v((wide, cols), BF), pltpu.SemaphoreType.DMA((2 * sz.n + 8,))],
        4 * t * wide * cols, 40,
        specs=[SMEM] + [ANY] * 4 + [VM] * 2, out_specs=[ANY] * 3,
    )


def spread(v, n, real, padded):
    lead = v.shape[:-1]
    v = v.reshape(lead + (n, real))
    v = jnp.pad(v, [(0, 0)] * len(lead) + [(0, 0), (0, padded - real)])
    return v.reshape(lead + (n * padded,))


def narrow(v, n, real, padded):
    lead = v.shape[:-1]
    return v.reshape(lead + (n, padded))[..., :real].reshape(lead + (n * real,))


def place_blocks(order, pieces):
    both = jnp.concatenate(pieces)
    spots = jnp.zeros(order.shape, jnp.int32).at[order].set(jnp.arange(order.shape[0], dtype=jnp.int32))
    return jnp.take(both, spots, axis=0).reshape(-1, both.shape[2])


def order_blocks(order, grad, half, nz):
    blocks = grad.reshape(nz, 8, half, grad.shape[1])
    at_z = jnp.take(blocks, order[:nz], axis=0)
    parts = [jnp.take(at_z, order[nz + k], axis=1) for k in range(8)]
    return jnp.concatenate(parts[:4]), jnp.concatenate(parts[4:6]), jnp.concatenate(parts[6:])


def shards(mesh, tokens, lengths, w_query, key_weight, value_weight, output_weight, w_gate, w_up, w_down, gain_attn, gain_ffn, out_grad):
    at = Place(mesh)
    n = at.n
    real, width = w_query.shape
    padded = -(-(real + 2) // 16) * 16
    sz = Sizes(n, real, padded, w_gate.shape[1], tokens.shape[0], key_weight.shape[1])
    wide, ff = sz.wide, sz.ff
    half, down_half = padded // 2, w_down.shape[0] // 2
    aligned = down_half % 16 == 0
    order = Order()
    places, back = at.piece_order(), at.grad_order()

    def pad_rows(v):
        return jnp.pad(v, ((0, padded - v.shape[0]), (0, 0)))

    def attention_shard(w_query, key_weight, value_weight, output_weight, gain_attn, gain_ffn):
        qkv = jnp.concatenate([w_query, key_weight, value_weight], axis=1)
        gains = jnp.pad(jnp.stack([gain_attn, gain_ffn]), ((0, 0), (0, qkv.shape[1] - real)))
        qkv = pad_rows(jnp.concatenate([qkv, gains]))
        return jnp.concatenate([pad_rows(spread(output_weight, n, real, padded)), qkv], axis=1)

    def tables(lengths, tokens, out_grad):
        positions, allowed = layout(lengths, tokens.shape[0])
        bias = jnp.where(allowed[0], 0.0, -1e30).astype(F32).T
        return rotation(positions[0]), bias, spread(tokens, n, real, padded), spread(out_grad, n, real, padded)

    ga, gg, gu, gd = (Gather(at, order) for _ in range(4))
    ga.start(attention_shard, w_query, key_weight, value_weight, output_weight, gain_attn, gain_ffn)
    ga.ready()
    ga.along_z()
    gg.start(pad_rows, w_gate)
    gu.start(pad_rows, w_up)
    gd.start(lambda v: spread(v, n, real, padded), w_down)
    gg.ready()
    gu.ready()
    gd.ready()
    rope, bias, x1, cot = order.do(tables, lengths, tokens, out_grad)
    ga.come()
    ga.line_up()
    ga.first()
    gg.along_z()
    ga.got_first()
    ga.second()
    gg.come()
    gg.line_up()
    gg.first()
    gu.along_z()
    x1, cot = order.do(settle, x1, cot)
    ga.got_second()
    gg.got_first()
    gu.come()
    ga.cores()
    gg.second()
    gu.line_up()
    gu.first()
    attn_pieces = ga.pieces()
    gd.along_z()
    hidden1, a1_1, heads1, lse1, mixp1, gains = order.do(
        lambda *v: first_attention(sz, *v), places, attn_pieces, x1, rope, bias
    )
    gd.come()
    gg.got_second()
    gg.cores()
    gu.got_first()
    gu.second()
    gd.line_up()
    gd.first()
    gate_pieces = gg.pieces()
    a2_1, gate1 = order.do(lambda *v: first_gate(sz, *v), places, gate_pieces, hidden1, gains)
    gd.got_first()
    gd.second()
    gu.got_second()
    gu.cores()
    up_pieces = gu.pieces()
    gd.cores(gd.both)
    up1, inner1 = order.do(lambda *v: first_up(sz, *v), places, up_pieces, a2_1, gate1)
    gd.got_second()
    gd.cores(gd.third)
    down_pieces = gd.pieces()
    if not aligned:
        down_pieces = place_blocks(places, down_pieces)

    (second, wqkv, wo, a1_2, mixp2, a2_2, gu2, gl2, g_qkv2, gh1, gl1, gu1, gain2, *grads) = order.do(
        lambda *v: middle(sz, *v, half, down_half),
        places, back, down_pieces, attn_pieces, gate_pieces, up_pieces, hidden1, inner1, gate1, up1, a2_1, gains, rope, bias, cot,
    )
    downs, gates = grads[:3], grads[3:]
    if not aligned:
        downs = order_blocks(back, downs[0], down_half, at.nz)
    sd = Scatter(at, order, *downs)
    sg = Scatter(at, order, *gates)
    sd.core(0)
    sg.core(0)
    sd.core(1)
    sg.core(1)
    sd.come_core(0)
    sd.first()
    sg.come_core(0)
    sg.first()
    sd.come_core(1)
    sg.come_core(1)
    own, *send = order.do(
        lambda *v: up_out_grad(sz, *v, half), back, (a2_1, a2_2), (gu1, gu2), (mixp1, mixp2), (gl1, gl2)
    )
    sd.come()
    su = Scatter(at, order, own, *send)
    su.core(0)
    su.core(1)
    sd.second()
    su.come_core(0)
    su.first()
    su.come_core(1)
    g_x, g_qkv1, gain_a1 = order.do(
        lambda *v: last_attention(sz, *v), gh1, gl1, x1, gains, wqkv, wo, rope, bias, heads1, lse1
    )
    sg.come()
    sd.come()
    sg.second()
    sd.along_z()
    own, *send = order.do(
        lambda *v: qkv_grad(sz, *v, half), back, (a1_1, a1_2), (g_qkv1, g_qkv2), gain2, gain_a1
    )
    sg.come()
    su.come()
    su.second()
    sd.come_z()
    sg.along_z()
    sa = Scatter(at, order, own, *send)
    sa.core(0)
    sa.core(1)
    sa.come_core(0)
    sa.first()
    sa.come_core(1)
    su.come()
    sg.come_z()
    su.along_z()
    sa.come()
    sa.second()
    sd.along_x()
    sg.along_x()
    second, g_x = order.do(settle, second, g_x)
    su.come_z()
    sa.come()
    sa.along_z()
    su.along_x()
    sd.come()
    sd.cores()
    sa.come_z()
    sa.along_x()
    sg.come()
    sg.cores()
    su.come()
    su.cores()
    sd.come()
    sg.come()
    su.come()
    r_up = su.result()
    r_gate = sg.result()
    r_down = sd.result()
    second, g_x = narrow(second, n, real, padded), narrow(g_x, n, real, padded)
    sa.come()
    sa.cores()
    sa.come()
    r_in = sa.result()
    kv = key_weight.shape[1]
    return (
        second,
        g_x,
        r_in[:real, :width],
        r_in[:real, width : width + kv],
        r_in[:real, width + kv :],
        narrow(r_up[:real, ff:], n, real, padded),
        r_gate[:real],
        r_up[:real, :ff],
        narrow(r_down, n, real, padded),
        r_in[real, :real],
        r_in[real + 1, :real],
    )


def solution(mesh):
    rows, split, gain = P(("dp", "fsdp"), None), P("fsdp", None), P("fsdp")
    return jax.shard_map(
        functools.partial(shards, mesh),
        mesh=mesh,
        in_specs=(rows, rows) + (split,) * 7 + (gain, gain, rows),
        out_specs=(rows, rows) + (split,) * 7 + (gain, gain),
        check_vma=False,
    )
```

```python
import functools
import math

import jax
import jax.numpy as jnp
from jax import lax
from jax.experimental import pallas as pl
from jax.experimental.pallas import tpu as pltpu
from jax.sharding import PartitionSpec as P

HEAD_SIZE = 64
GROUP = 3
ROPE_BASE = 10000.0
EPS = 1e-05
BF = jnp.bfloat16
F32 = jnp.float32
MIB = 1024 * 1024


def layout(doc_lengths, token_count):
    ends = jnp.cumsum(doc_lengths, axis=1)
    starts = ends - doc_lengths
    place = jnp.arange(token_count, dtype=jnp.int32)
    document = jnp.sum((place[None, :, None] >= ends[:, None, :]).astype(jnp.int32), axis=2)
    inside = place[None, :] < ends[:, -1:]
    segment = jnp.where(inside, document, -1)
    chosen = (
        document[:, :, None] == jnp.arange(doc_lengths.shape[1], dtype=jnp.int32)[None, None, :]
    )
    begin = jnp.sum(jnp.where(chosen, starts[:, None, :], 0), axis=2)
    positions = jnp.where(inside, place[None, :] - begin, 0)
    causal = place[:, None] >= place[None, :]
    same = (segment[:, :, None] == segment[:, None, :]) & (segment[:, :, None] >= 0)
    allowed = same & causal[None] | (place[:, None] == place[None, :])[None]
    return (positions, allowed)


def rotation(positions):
    half = HEAD_SIZE // 2
    frequency = jnp.exp(jnp.arange(half, dtype=F32) * (-2.0 * math.log(ROPE_BASE) / HEAD_SIZE))
    angle = positions.astype(F32)[None, :] * frequency[:, None]
    return (jnp.cos(angle), jnp.sin(angle))


class Place:
    def __init__(self, mesh):
        self.n, self.groups = mesh.shape["fsdp"], mesh.shape["dp"]
        self.nz = self.n // 4
        i = lax.axis_index("fsdp")
        self.c, self.y, self.z = i % 2, (i // 2) % 2, i // 4
        self.p = lax.axis_index("dp") % 2

    def swap_core(self, v):
        return lax.ppermute(v, "fsdp", [(i, i ^ 1) for i in range(self.n)])

    def shift_z(self, v, k):
        return lax.ppermute(v, "fsdp", [(i, (i + 4 * k) % self.n) for i in range(self.n)])

    def swap_x(self, v):
        return lax.ppermute(v, "dp", [(d, d ^ 1) for d in range(self.groups)])

    def cross(self, v, first):
        pairs = []
        for d in range(self.groups):
            for i in range(self.n):
                along_x = (i % 2 == 0) == first
                e, j = (d ^ 1, i) if along_x else (d, i ^ 2)
                pairs.append((d * self.n + i, e * self.n + j))
        return lax.ppermute(v, ("dp", "fsdp"), pairs)

    def piece_order(self):
        order = []
        for h in (self.c, 1 - self.c):
            for j in range(4 * self.nz):
                dz, slot = j % self.nz, j // self.nz
                lo, hi = slot % 2, slot // 2
                dy, dc = jnp.where(h == 0, lo, hi), jnp.where(h == 0, hi, lo)
                z = (self.z - dz + self.nz) % self.nz
                order.append((((z * 2 + (self.y ^ dy)) * 2 + (self.p ^ dc)) * 2 + h).astype(jnp.int32))
        return jnp.stack(order)

    def grad_order(self):
        order = [(self.z + k) % self.nz for k in range(self.nz)]
        for h in (self.c, 1 - self.c):
            for hi in (0, 1):
                for lo in (0, 1):
                    of_c, of_y = jnp.where(h == 0, hi, lo), jnp.where(h == 0, lo, hi)
                    c = jnp.where(of_c == 1, self.p, 1 - self.p)
                    y = jnp.where(of_y == 1, self.y, 1 - self.y)
                    order.append((y * 2 + c) * 2 + h)
        return jnp.stack(order).astype(jnp.int32)


def pick(v, k, axis=0):
    return lax.dynamic_index_in_dim(v, k, axis, keepdims=False)


class Order:
    def __init__(self):
        self.last = ()

    def do(self, step, *inputs):
        leaves, tree = jax.tree.flatten(inputs)
        if self.last:
            leaves = lax.optimization_barrier((*leaves, *self.last))[: len(leaves)]
        out = step(*jax.tree.unflatten(tree, leaves))
        self.last = (jax.tree.leaves(out)[0],)
        return out

    def tie(self, v):
        return lax.optimization_barrier((v, *self.last))[0] if self.last else v

    def got(self, *received):
        out = lax.optimization_barrier((*received, *self.last))[: len(received)]
        self.last = (out[0],)
        return out[0] if len(out) == 1 else out


def add(*terms):
    return functools.reduce(lambda a, b: a + b, [t.astype(F32) for t in terms])


class Gather:
    def __init__(self, at, order):
        self.at, self.order = at, order

    def start(self, make, *inputs):
        def step(*inputs):
            shard = make(*inputs)
            halves = shard.reshape(2, shard.shape[0] // 2, shard.shape[1])
            return pick(halves, self.at.c), pick(halves, 1 - self.at.c)

        self.keep, send = self.order.do(step, *inputs)
        self.moving = self.at.swap_core(send)

    def ready(self):
        at = self.at
        got = self.order.got(self.moving)
        self.mine = self.order.do(lambda k, g: jnp.where(at.p == at.c, k, g)[None], self.keep, got)

    def along_z(self):
        mine = self.order.tie(self.mine)
        self.moving = [self.at.shift_z(mine, k) for k in range(1, self.at.nz)]

    def come(self):
        parts = self.order.got(*self.moving)
        self.parts = parts if isinstance(parts, tuple) else (parts,)

    def line_up(self):
        self.line = self.order.do(lambda *v: jnp.concatenate(v), self.mine, *self.parts)

    def first(self):
        self.moving = self.at.cross(self.order.tie(self.line), False)

    def got_first(self):
        self.got = self.order.got(self.moving)

    def second(self):
        self.both = self.order.do(lambda *v: jnp.concatenate(v), self.line, self.got)
        self.moving = self.at.cross(self.both, True)
        self.others = []

    def got_second(self):
        self.third = self.order.got(self.moving)

    def cores(self, *which):
        self.others += [self.at.swap_core(self.order.tie(v)) for v in which or (self.both, self.third)]

    def pieces(self):
        return (self.both, self.third, *self.order.got(*self.others))


class Scatter:
    def __init__(self, at, order, own, *send):
        self.at, self.order, self.own = at, order, own
        self.send, self.swaps, self.other = send, {}, {}

    def core(self, k):
        self.swaps[k] = self.at.swap_core(self.order.tie(self.send[k]))

    def sums(self, *terms):
        cuts = [(lo, lo + count) for _, lo, count in terms]

        def step(*v):
            return add(*[a[lo:hi] for a, (lo, hi) in zip(v, cuts)]).astype(BF)

        return self.order.do(step, *[a for a, _, _ in terms])

    def come(self):
        self.got = self.order.got(self.moving)

    def come_core(self, k):
        self.other[k] = self.order.got(self.swaps[k])

    def first(self):
        two = 2 * self.at.nz
        self.moving = self.at.cross(self.sums((self.own, 0, two), (self.other[0], 0, two)), True)

    def second(self):
        nz = self.at.nz
        self.crossed = self.got
        sent = self.sums((self.own, 2 * nz, nz), (self.other[1], 0, nz), (self.crossed, 0, nz))
        self.moving = self.at.cross(sent, False)

    def along_z(self):
        nz = self.at.nz
        self.low = self.sums((self.own, 3 * nz, nz), (self.other[1], nz, nz), (self.crossed, nz, nz), (self.got, 0, nz))
        self.moving = [self.at.shift_z(self.low[k : k + 1], k) for k in range(1, nz)]

    def come_z(self):
        parts = self.order.got(*self.moving)
        self.parts = parts if isinstance(parts, tuple) else (parts,)

    def along_x(self):
        total = self.sums((self.low, 0, 1), *[(p, 0, 1) for p in self.parts])[0]
        step = 2
        while step < self.at.groups:
            pairs = [(d, d ^ step) for d in range(self.at.groups)]
            total = add(total, lax.ppermute(total, "dp", pairs)).astype(BF)
            step *= 2
        self.total = total
        self.moving = self.at.swap_x(total)

    def cores(self):
        here = self.at.p == self.at.c
        self.keep, send = self.order.do(
            lambda a, b: (jnp.where(here, a, b), jnp.where(here, b, a)), self.total, self.got
        )
        self.moving = self.at.swap_core(send)

    def result(self):
        first = self.at.c == 0
        return self.order.do(
            lambda a, b: jnp.concatenate([jnp.where(first, a, b), jnp.where(first, b, a)]).astype(F32), self.keep, self.got
        )


VM = pl.BlockSpec(memory_space=pltpu.VMEM)
ANY = pl.BlockSpec(memory_space=pl.ANY)
SMEM = pl.BlockSpec(memory_space=pltpu.SMEM)


def nn(left, right):
    return jnp.dot(left, right, preferred_element_type=F32)


def nt(left, right):
    return lax.dot_general(left, right, (((1,), (1,)), ((), ())), preferred_element_type=F32)


def tn(left, right):
    return lax.dot_general(left, right, (((0,), (0,)), ((), ())), preferred_element_type=F32)


def tt(left, right):
    return lax.dot_general(left, right, (((0,), (1,)), ((), ())), preferred_element_type=F32)


def join(parts, axis):
    return jnp.concatenate(parts, axis=axis) if len(parts) > 1 else parts[0]


def call(body, ins, outs, scratch, flops, limit, specs=None, out_specs=None):
    return pl.pallas_call(
        body,
        in_specs=specs or [VM] * len(ins),
        out_specs=out_specs or [VM] * len(outs),
        out_shape=outs,
        scratch_shapes=scratch,
        compiler_params=pltpu.CompilerParams(vmem_limit_bytes=max(limit, 60) * MIB),
        cost_estimate=pl.CostEstimate(flops=1000, bytes_accessed=1000, transcendentals=0),
    )(*ins)


def fetches(order_ref, pieces, dests, sem, base):
    copies = []
    half = pieces[0].shape[1]
    at = 0
    for ref in pieces:
        for j in range(ref.shape[0]):
            row = pl.multiple_of(order_ref[at] * half, half)
            at += 1
            for dest, col in dests:
                whole = col == 0 and dest.shape[1] == ref.shape[2]
                src = ref.at[j] if whole else ref.at[j, :, pl.ds(col, dest.shape[1])]
                copies.append(
                    pltpu.make_async_copy(src, dest.at[pl.ds(row, half), :], sem.at[base + len(copies)])
                )
    return copies


class Copies:
    def __init__(self, sem):
        self.sem, self.used, self.open = sem, 0, []

    def start(self, source, dest):
        copy = pltpu.make_async_copy(source, dest, self.sem.at[self.used])
        self.used += 1
        copy.start()
        return copy

    def store(self, source, dest):
        self.open.append(self.start(source, dest))

    def blocks(self, order_ref, nz, k, source, base, half, own, sends):
        for quarter in range(4):
            place, part = quarter % 2 * nz + k, quarter // 2
            for first, dest in ((0, own.at[2 * nz * part + place]), (4, sends[part].at[place])):
                row = base + pl.multiple_of(order_ref[nz + first + quarter] * half, half)
                self.store(source.at[pl.ds(row, half), :], dest)

    def close(self):
        wait(self.open)
        self.open = []


def start(copies):
    for copy in copies:
        copy.start()
    return copies


def wait(copies):
    for copy in copies:
        copy.wait()


def inverse_rms(v, width):
    return lax.rsqrt(jnp.sum(v * v, axis=1, keepdims=True) * (1.0 / width) + EPS)


def norm_back(values, gain, grad, width):
    scale = inverse_rms(values, width)
    unit = values * scale
    gain_grad = jnp.sum(grad * unit, axis=0, keepdims=True)
    inner = grad * gain
    mean = jnp.sum(inner * unit, axis=1, keepdims=True) * (1.0 / width)
    return gain_grad, scale * (inner - unit * mean)


class Sizes:
    def __init__(self, n, real, padded, ff, t, kv):
        self.n, self.real, self.padded, self.ff, self.t = n, real, padded, ff, t
        self.width, self.wide = n * real, n * padded
        self.hq, self.kvh = self.width // HEAD_SIZE, kv // HEAD_SIZE
        self.heads = self.hq + 2 * self.kvh
        self.feat = self.heads * HEAD_SIZE
        self.group = self.hq // self.kvh
        self.lse = -(-self.hq // 8) * 8
        self.block = 128 if t % 128 == 0 else t
        self.blocks = t // self.block
        self.tile = 512 if ff % 512 == 0 else ff


def head(ref, h):
    return ref[h * HEAD_SIZE : (h + 1) * HEAD_SIZE, :]


def by_block(sz, parts, op):
    b = sz.block
    return [
        functools.reduce(op, [parts[j][:, b * (i - j) : b * (i - j + 1)] for j in range(i + 1)])
        for i in range(sz.blocks)
    ]


def plus(a, b):
    return a + b


def block_product(sz, left, parts):
    b, out = sz.block, None
    for j in range(sz.blocks):
        part = nn(left[:, b * j : b * (j + 1)], parts[j])
        if j:
            part = jnp.concatenate([jnp.zeros((left.shape[0], b * j), F32), part], axis=1)
        out = part if out is None else out + part
    return out


def attention_forward(sz, x, gain, wqkv, wo, cos, sin, bias, a1, heads, lse, mixp, mix, done=lambda stage: None):
    b, half = sz.block, HEAD_SIZE // 2
    a1[...] = (x * inverse_rms(x, sz.width) * gain).astype(BF)
    for c in range(0, sz.heads, 4):
        end = min(c + 4, sz.heads)
        part = tt(wqkv[:, c * HEAD_SIZE : end * HEAD_SIZE], a1[...])
        for h in range(c, end):
            lo = (h - c) * HEAD_SIZE
            first, second = part[lo : lo + half], part[lo + half : lo + HEAD_SIZE]
            if h < sz.hq + sz.kvh:
                first, second = (
                    first * cos[...] - second * sin[...],
                    second * cos[...] + first * sin[...],
                )
            if h < sz.hq:
                first, second = first * HEAD_SIZE ** (-0.5), second * HEAD_SIZE ** (-0.5)
            heads[h * HEAD_SIZE : h * HEAD_SIZE + half, :] = first.astype(BF)
            heads[h * HEAD_SIZE + half : (h + 1) * HEAD_SIZE, :] = second.astype(BF)
    done(0)
    if sz.lse > sz.hq:
        lse[...] = jnp.zeros(lse.shape, F32)
    for first in range(0, sz.kvh, 3):
        groups = range(first, min(first + 3, sz.kvh))
        keys = {g: head(heads, sz.hq + g).T for g in groups}
        values = {g: head(heads, sz.hq + sz.kvh + g) for g in groups}
        pairs = [(g, g * sz.group + r) for g in groups for r in range(sz.group)]
        scores = []
        for g, h in pairs:
            q = head(heads, h)
            scores.append([
                nn(keys[g][b * j : b * (j + 1)], q[:, b * j :]) + bias[b * j : b * (j + 1), b * j :]
                for j in range(sz.blocks)
            ])
        tops = [by_block(sz, [jnp.max(s, axis=0, keepdims=True) for s in ss], jnp.maximum) for ss in scores]
        powers, sums = [], []
        for ss, top in zip(scores, tops):
            e = [jnp.exp(ss[j] - join(top[j:], 1)) for j in range(sz.blocks)]
            sums.append(join(by_block(sz, [jnp.sum(v, axis=0, keepdims=True) for v in e], plus), 1))
            powers.append([v.astype(BF) for v in e])
        for (g, h), e, top, summed in zip(pairs, powers, tops, sums):
            out = block_product(sz, values[g], e)
            mix[h * HEAD_SIZE : (h + 1) * HEAD_SIZE, :] = out * (1.0 / summed)
            lse[h : h + 1, :] = join(top, 1) + jnp.log(summed)
    row = lax.broadcasted_iota(jnp.int32, (sz.padded, sz.t), 0)
    for j in range(sz.n):
        part = mix[sz.real * j : sz.real * j + sz.padded, :]
        mixp[sz.padded * j : sz.padded * (j + 1), :] = jnp.where(row < sz.real, part, 0.0).astype(BF)
    done(1)
    return x + tn(mixp[...], wo[...])


def attention_backward(sz, gh, gl, x, gain, wqkv, wo, cos, sin, bias, heads, lse, gm, g_heads, g_qkv, ready=None):
    b, half = sz.block, HEAD_SIZE // 2
    for j in range(sz.n):
        part = nt(wo[sz.padded * j : sz.padded * (j + 1), :], gl) if sz.n < 4 else None
        if part is not None:
            gm[sz.real * j : sz.real * j + sz.padded, :] = part
    if sz.n >= 4:
        quarter = sz.n // 4
        for c in range(4):
            part = nt(wo[sz.padded * quarter * c : sz.padded * quarter * (c + 1), :], gl)
            for j in range(quarter):
                at = sz.real * (quarter * c + j)
                gm[at : at + sz.padded, :] = part[sz.padded * j : sz.padded * (j + 1)]
    if ready is not None:
        ready(False)
    for g in range(sz.kvh):
        kt = head(heads, sz.hq + g)
        k = kt.T
        v = head(heads, sz.hq + sz.kvh + g).T
        hs = range(g * sz.group, (g + 1) * sz.group)
        qs, gms = [head(heads, h) for h in hs], [head(gm, h).astype(BF) for h in hs]
        cut = [(b * j, b * (j + 1)) for j in range(sz.blocks)]
        scores = [[nn(k[lo:hi], q[:, lo:]) + bias[lo:hi, lo:] for lo, hi in cut] for q in qs]
        gps = [[nn(v[lo:hi], m[:, lo:]) for lo, hi in cut] for m in gms]
        ps = [[jnp.exp(s - lse[h : h + 1, :][:, lo:]) for s, (lo, _) in zip(ss, cut)] for ss, h in zip(scores, hs)]
        gk = gv = None
        for h, q, m, p, gp in zip(hs, qs, gms, ps, gps):
            d = by_block(sz, [jnp.sum(a * c, axis=0, keepdims=True) for a, c in zip(p, gp)], plus)
            g_s = [(p[j] * (gp[j] - join(d[j:], 1))).astype(BF) for j in range(sz.blocks)]
            low = [a.astype(BF) for a in p]
            part_k = join([nt(q[:, lo:], a) for (lo, _), a in zip(cut, g_s)], 1)
            part_v = join([nt(m[:, lo:], a) for (lo, _), a in zip(cut, low)], 1)
            g_heads[h * HEAD_SIZE : (h + 1) * HEAD_SIZE, :] = block_product(sz, kt, g_s) * HEAD_SIZE ** (-0.5)
            gk = part_k if gk is None else gk + part_k
            gv = part_v if gv is None else gv + part_v
        at = (sz.hq + g) * HEAD_SIZE
        g_heads[at : at + HEAD_SIZE, :] = gk
        at = (sz.hq + sz.kvh + g) * HEAD_SIZE
        g_qkv[at : at + HEAD_SIZE, :] = gv.astype(BF)
    for h in range(sz.hq + sz.kvh):
        at = h * HEAD_SIZE
        first, second = g_heads[at : at + half, :], g_heads[at + half : at + HEAD_SIZE, :]
        g_qkv[at : at + half, :] = (first * cos[...] + second * sin[...]).astype(BF)
        g_qkv[at + half : at + HEAD_SIZE, :] = (second * cos[...] - first * sin[...]).astype(BF)
    if ready is not None:
        ready(True)
    gain_grad, back = norm_back(x[...], gain, tt(g_qkv[...], wqkv[...]), sz.width)
    return gain_grad, gh[...] + back


def ffn_up(sz, hidden, gain, a2, wg, wu, gate, up, inner):
    a2[...] = (hidden * inverse_rms(hidden, sz.width) * gain).astype(BF)
    for c in range(0, sz.ff, sz.tile):
        cols = slice(c, c + sz.tile)
        gate_part = nn(a2[...], wg[:, cols])
        up_part = nn(a2[...], wu[:, cols])
        gate[:, cols] = gate_part.astype(BF)
        up[:, cols] = up_part.astype(BF)
        inner[:, cols] = (gate_part * jax.nn.sigmoid(gate_part) * up_part).astype(BF)


def ffn_back_tile(cl, wd, gate, up, gg, gu, cols):
    g_inner = nt(cl[...], wd[cols, :])
    z = gate[:, cols].astype(F32)
    sg = jax.nn.sigmoid(z)
    silu = z * sg
    gg[:, cols] = (g_inner * up[:, cols].astype(F32) * (sg + silu * (1.0 - sg))).astype(BF)
    gu[:, cols] = (g_inner * silu).astype(BF)


def ffn_backward(sz, grad, cl, hidden, gain, wg, wu, wd, gate, up, gg, gu):
    for c in range(0, sz.ff, sz.tile):
        ffn_back_tile(cl, wd, gate, up, gg, gu, slice(c, c + sz.tile))
    g_a2 = nt(gg[...], wg[...]) + nt(gu[...], wu[...])
    gain_grad, back = norm_back(hidden[...], gain, g_a2, sz.width)
    return gain_grad, grad + back


def shape(*dims, dtype=BF):
    return jax.ShapeDtypeStruct(dims, dtype)


def halves(sz, half, cols):
    return [shape(sz.n, half, cols)] + [shape(sz.n // 2, half, cols)] * 2


def first_attention(sz, order, pieces, x, rope, bias):
    t, wide = sz.t, sz.wide

    def body(order_ref, p0, p1, p2, p3, x_hbm, cos, sin, bias_hbm,
             hidden_hbm, a1_hbm, heads_hbm, lse, mixp_hbm, gains,
             x, hidden, a1, heads, mixp, wo, wqkv, mix, bias_ref, sem, out_sem):
        io = Copies(out_sem)
        first = start(fetches(order_ref, (p0, p1, p2, p3), [(wqkv, sz.wide)], sem, 0))
        loads = [io.start(x_hbm, x), io.start(bias_hbm, bias_ref)]
        loads += start(fetches(order_ref, (p0, p1, p2, p3), [(wo, 0)], sem, 2 * sz.n))
        wait(first)
        rows = []
        for k in range(2):
            parts = []
            for j in range(sz.n):
                lo = sz.padded * (j + 1) - 16
                tile = wqkv[lo : lo + 16, 0:128].astype(F32)
                at = sz.real + k - (sz.padded - 16)
                parts.append(tile[at : at + 1, : sz.padded])
            rows.append(jnp.concatenate(parts, axis=1))
        gains[...] = jnp.concatenate(rows + [jnp.zeros((6, sz.wide), F32)], axis=0)
        wait(loads)
        hidden[...] = x[...].astype(F32)

        def done(stage):
            for a, b in (((a1, a1_hbm), (heads, heads_hbm)), ((mixp, mixp_hbm),))[stage]:
                io.store(a, b)

        hidden[...] = attention_forward(
            sz, hidden[...], gains[0:1, :], wqkv, wo, cos, sin, bias_ref, a1, heads, lse, mixp, mix, done
        )
        io.store(hidden, hidden_hbm)
        io.close()

    v = pltpu.VMEM
    return call(
        body,
        [order, *pieces, x, *rope, bias],
        [
            shape(t, wide, dtype=F32), shape(t, wide), shape(sz.feat, t), shape(sz.lse, t, dtype=F32),
            shape(wide, t), shape(8, wide, dtype=F32),
        ],
        [
            v((t, wide), BF), v((t, wide), F32), v((t, wide), BF), v((sz.feat, t), BF), v((wide, t), BF),
            v((wide, wide), BF), v((wide, sz.feat), BF), v((sz.width + 16, t), F32), v((t, t), F32),
            pltpu.SemaphoreType.DMA((4 * sz.n,)), pltpu.SemaphoreType.DMA((8,)),
        ],
        6 * t * wide * sz.feat, 40,
        specs=[SMEM] + [ANY] * 5 + [VM] * 2 + [ANY],
        out_specs=[ANY] * 3 + [VM, ANY, VM],
    )


def first_gate(sz, order, pieces, hidden, gains):
    t, wide, ff = sz.t, sz.wide, sz.ff

    def body(order_ref, p0, p1, p2, p3, hidden_hbm, gains_ref, a2_hbm, gate_hbm, hidden_ref, a2, gate, w, sem, out_sem):
        out = Copies(out_sem)
        load = out.start(hidden_hbm, hidden_ref)
        copies = start(fetches(order_ref, (p0, p1, p2, p3), [(w, 0)], sem, 0))
        wait([load])
        hidden = hidden_ref[...]
        a2[...] = (hidden * inverse_rms(hidden, sz.width) * gains_ref[1:2, :]).astype(BF)
        wait(copies)
        out.store(a2, a2_hbm)
        for c in range(0, ff, sz.tile):
            cols = slice(c, c + sz.tile)
            gate[:, cols] = nn(a2[...], w[:, cols]).astype(BF)
            out.store(gate.at[:, pl.ds(c, sz.tile)], gate_hbm.at[:, pl.ds(c, sz.tile)])
        out.close()

    return call(
        body,
        [order, *pieces, hidden, gains],
        [shape(t, wide), shape(t, ff)],
        [pltpu.VMEM((t, wide), F32), pltpu.VMEM((t, wide), BF), pltpu.VMEM((t, ff), BF), pltpu.VMEM((wide, ff), BF),
         pltpu.SemaphoreType.DMA((2 * sz.n,)), pltpu.SemaphoreType.DMA((2 + ff // sz.tile,))],
        2 * t * wide * ff, 40,
        specs=[SMEM] + [ANY] * 5 + [VM], out_specs=[ANY] * 2,
    )


def first_up(sz, order, pieces, a2, gate):
    t, wide, ff = sz.t, sz.wide, sz.ff

    def body(order_ref, p0, p1, p2, p3, a2_hbm, gate_hbm, up_hbm, inner_hbm, a2, gate, up, inner, w, sem, out_sem):
        out = Copies(out_sem)
        loads = [out.start(a2_hbm, a2), out.start(gate_hbm, gate)]
        wait(start(fetches(order_ref, (p0, p1, p2, p3), [(w, 0)], sem, 0)))
        wait(loads)
        for c in range(0, ff, sz.tile):
            cols, part = slice(c, c + sz.tile), pl.ds(c, sz.tile)
            value = nn(a2[...], w[:, cols])
            up[:, cols] = value.astype(BF)
            z = gate[:, cols].astype(F32)
            inner[:, cols] = (z * jax.nn.sigmoid(z) * value).astype(BF)
            out.store(inner.at[:, part], inner_hbm.at[:, part])
            out.store(up.at[:, part], up_hbm.at[:, part])
        out.close()

    return call(
        body,
        [order, *pieces, a2, gate],
        [shape(t, ff), shape(t, ff)],
        [pltpu.VMEM((t, wide), BF)] + [pltpu.VMEM((t, ff), BF)] * 3 + [pltpu.VMEM((wide, ff), BF),
         pltpu.SemaphoreType.DMA((2 * sz.n,)), pltpu.SemaphoreType.DMA((2 + 2 * (ff // sz.tile),))],
        2 * t * wide * ff, 40,
        specs=[SMEM] + [ANY] * 6, out_specs=[ANY] * 2,
    )


def middle(sz, order, back, down_pieces, attn_pieces, gate_pieces, up_pieces, hidden1, inner1, gate1, up1, a2_1, gains, rope, bias,
           out_grad, half, down_half):
    aligned = isinstance(down_pieces, tuple)
    downs = list(down_pieces) if aligned else [down_pieces]
    t, wide, ff = sz.t, sz.wide, sz.ff

    def body(*refs):
        order_ref, back_ref, refs = refs[0], refs[1], refs[2:]
        down_refs, refs = refs[: len(downs)], refs[len(downs) :]
        attn_refs, gate_refs, up_refs, refs = refs[:4], refs[4:8], refs[8:12], refs[12:]
        (hidden1_hbm, inner1_hbm, gate1_hbm, up1_hbm, a2_1_hbm, gains_ref, cos, sin, bias_hbm, cl_hbm,
         second_hbm, wqkv_hbm, wo_hbm, a1_hbm, mixp_hbm, a2_hbm, gu_hbm, gl_hbm, g_qkv_hbm, gh1_hbm, gl1_hbm, gu1_hbm,
         gain_grads, *refs) = refs
        down_out, gate_out, refs = refs[:3], refs[3:6], refs[6:]
        (wd, wqkv, wo, wg, wu, inners, cls, x2, hidden, a1, heads, lse, mixp, a2s, gate, up, ggs, gu, gl, g_qkv,
         bias_ref, mix, g_heads, sem, piece_sem) = refs
        io = Copies(sem)
        if aligned:
            first = start(fetches(order_ref, down_refs, [(wd, 0)], piece_sem, 0))
        else:
            first = [io.start(down_refs[0], wd)]
        run1, run2 = pl.ds(0, t), pl.ds(t, t)
        inner1, inner2 = inners.at[run1, :], inners.at[run2, :]
        cl1, cl2 = cls.at[run1, :], cls.at[run2, :]
        a2, gg1, gg2 = a2s.at[run2, :], ggs.at[run1, :], ggs.at[run2, :]
        first += [io.start(inner1_hbm, inner1), io.start(hidden1_hbm, x2)]
        wait(first)
        loads = start(fetches(order_ref, attn_refs, [(wqkv, wide)], piece_sem, 2 * sz.n))
        loads += start(fetches(order_ref, attn_refs, [(wo, 0)], piece_sem, 4 * sz.n))
        loads += [io.start(bias_hbm, bias_ref)]
        x2[...] = x2[...] + nn(inner1[...], wd[...])
        wait(loads)
        sides = start(fetches(order_ref, gate_refs, [(wg, 0)], piece_sem, 6 * sz.n))
        sides += start(fetches(order_ref, up_refs, [(wu, 0)], piece_sem, 8 * sz.n))
        sides += [io.start(cl_hbm, cl2)]
        hidden[...] = attention_forward(
            sz, x2[...], gains_ref[0:1, :], wqkv, wo, cos, sin, bias_ref, a1, heads, lse, mixp, mix
        )
        wait(sides)
        for a, b in ((a1, a1_hbm), (mixp, mixp_hbm), (wqkv, wqkv_hbm), (wo, wo_hbm)):
            io.store(a, b)
        ffn_up(sz, hidden[...], gains_ref[1:2, :], a2, wg, wu, gate, up, inner2)
        io.store(a2, a2_hbm)
        gl[...] = (hidden[...] + nn(inner2[...], wd[...])).astype(BF)
        out = io.start(gl, second_hbm)
        gain_f, gh = ffn_backward(
            sz, cl2[...].astype(F32), cl2, hidden[...], gains_ref[1:2, :], wg, wu, wd, gate, up, gg2, gu
        )
        gus_out = io.start(gu, gu_hbm)
        loads = [io.start(gate1_hbm, gate), io.start(up1_hbm, up), io.start(a2_1_hbm, a2s.at[run1, :])]
        hidden[...] = gh
        wait([out])
        gl[...] = gh.astype(BF)
        out = io.start(gl, gl_hbm)
        gain_a, g_x = attention_backward(
            sz, hidden, gl[...], x2, gains_ref[0:1, :], wqkv, wo, cos, sin, bias_ref, heads, lse,
            mix, g_heads, g_qkv
        )
        io.store(g_qkv, g_qkv_hbm)
        hidden[...] = g_x
        loads.append(io.start(hidden1_hbm, x2))
        cl1[...] = g_x.astype(BF)
        wait(loads + [out, gus_out])
        gain_f1, gh = ffn_backward(
            sz, hidden[...], cl1, x2, gains_ref[1:2, :], wg, wu, wd, gate, up, gg1, gu
        )
        io.store(gu, gu1_hbm)
        hidden[...] = gh
        gl[...] = gh.astype(BF)
        io.store(hidden, gh1_hbm)
        io.store(gl, gl1_hbm)
        gain_grads[...] = jnp.concatenate([gain_a, gain_f + gain_f1, jnp.zeros((6, wide), F32)], axis=0)
        nz = sz.n // 4
        tile = ff // nz
        for k in range(nz):
            if aligned:
                rows = inners[:, pl.ds(pl.multiple_of(back_ref[k] * tile, tile), tile)]
                wd[k * tile : (k + 1) * tile, :] = tn(rows, cls[...]).astype(BF)
                io.blocks(back_ref, nz, k, wd, k * tile, down_half, down_out[0], down_out[1:])
        if not aligned:
            wd[...] = tn(inners[...], cls[...]).astype(BF)
            io.store(wd, down_out[0])
        tile = wide // nz
        for k in range(nz):
            rows = a2s[:, pl.ds(pl.multiple_of(back_ref[k] * tile, tile), tile)]
            wg[k * tile : (k + 1) * tile, :] = tn(rows, ggs[...]).astype(BF)
            io.blocks(back_ref, nz, k, wg, k * tile, half, gate_out[0], gate_out[1:])
        io.close()

    ins = [order, back, *downs, *attn_pieces, *gate_pieces, *up_pieces, hidden1, inner1, gate1, up1, a2_1, gains, *rope, bias,
           out_grad]
    specs = [SMEM] * 2 + [ANY] * (len(downs) + 17) + [VM] * 3 + [ANY] * 2
    places = halves(sz, down_half, wide) if aligned else [shape(ff, wide)] + [shape(8, 128)] * 2
    outs = [
        shape(t, wide), shape(wide, sz.feat), shape(wide, wide), shape(t, wide), shape(wide, t), shape(t, wide), shape(t, ff),
        shape(t, wide), shape(sz.feat, t), shape(t, wide, dtype=F32), shape(t, wide), shape(t, ff),
        shape(8, wide, dtype=F32), *places, *halves(sz, half, ff),
    ]
    out_specs = [ANY] * 12 + [VM] + [ANY] * 6
    v = pltpu.VMEM
    scratch = [
        v((ff, wide), BF), v((wide, sz.feat), BF), v((wide, wide), BF), v((wide, ff), BF), v((wide, ff), BF),
        v((2 * t, ff), BF), v((2 * t, wide), BF), v((t, wide), F32), v((t, wide), F32), v((t, wide), BF), v((sz.feat, t), BF),
        v((sz.lse, t), F32), v((wide, t), BF), v((2 * t, wide), BF), v((t, ff), BF), v((t, ff), BF), v((2 * t, ff), BF),
        v((t, ff), BF), v((t, wide), BF), v((sz.feat, t), BF), v((t, t), F32), v((sz.width + 16, t), F32),
        v((sz.feat, t), F32),
        pltpu.SemaphoreType.DMA((4 * sz.n + 40,)), pltpu.SemaphoreType.DMA((10 * sz.n,)),
    ]
    return call(body, ins, outs, scratch, 24 * t * wide * ff, 60, specs, out_specs)


def up_out_grad(sz, back, a2s, grads, mixps, gls, half):
    t, wide, ff = sz.t, sz.wide, sz.ff
    cols = ff + wide

    def body(back_ref, a_1, a_2, g_1, g_2, m1, m2, l1, l2, own, s0, s1, a, g, mixp, gl, out, sem):
        io = Copies(sem)
        run1, run2 = pl.ds(0, t), pl.ds(t, t)
        wait([
            io.start(m1, mixp.at[:, run1]), io.start(m2, mixp.at[:, run2]),
            io.start(l1, gl.at[run1, :]), io.start(l2, gl.at[run2, :]),
        ])
        later = [
            io.start(a_1, a.at[run1, :]), io.start(a_2, a.at[run2, :]),
            io.start(g_1, g.at[run1, :]), io.start(g_2, g.at[run2, :]),
        ]
        nz = sz.n // 4
        tile = wide // nz
        starts = [pl.multiple_of(back_ref[k] * tile, tile) for k in range(nz)]
        for k in range(nz):
            out[k * tile : (k + 1) * tile, ff:cols] = nn(mixp[pl.ds(starts[k], tile), :], gl[...]).astype(BF)
        wait(later)
        for k in range(nz):
            out[k * tile : (k + 1) * tile, 0:ff] = tn(a[:, pl.ds(starts[k], tile)], g[...]).astype(BF)
            io.blocks(back_ref, nz, k, out, k * tile, half, own, (s0, s1))
        io.close()

    v = pltpu.VMEM
    return call(
        body, [back, *a2s, *grads, *mixps, *gls], halves(sz, half, cols),
        [
            v((2 * t, wide), BF), v((2 * t, ff), BF), v((wide, 2 * t), BF), v((2 * t, wide), BF), v((wide, cols), BF),
            pltpu.SemaphoreType.DMA((2 * sz.n + 8,)),
        ],
        4 * t * wide * cols, 48,
        specs=[SMEM] + [ANY] * 8, out_specs=[ANY] * 3,
    )


def settle(*arrays):
    def body(*refs):
        for a, b in zip(refs[: len(arrays)], refs[len(arrays) :]):
            b[...] = a[...]

    return call(body, list(arrays), [shape(*a.shape, dtype=a.dtype) for a in arrays], [], 0, 20)


def last_attention(sz, gh, gl, x, gains, wqkv, wo, rope, bias, heads, lse):
    t, wide = sz.t, sz.wide

    def body(gh_hbm, gl_hbm, x_hbm, gains_ref, wqkv_hbm, wo_hbm, cos, sin, bias_hbm, heads_hbm, lse_ref,
             g_x_hbm, g_qkv_hbm, gain_grad,
             gh, gl, x_low, x, wqkv, wo, bias_ref, heads, g_qkv, mix, g_heads, sem):
        io = Copies(sem)
        first = [io.start(gl_hbm, gl), io.start(wo_hbm, wo)]
        second = [io.start(heads_hbm, heads), io.start(bias_hbm, bias_ref)]
        wait(first)
        later = []

        def ready(last):
            if last:
                wait(later)
                x[...] = x_low[...].astype(F32)
            else:
                wait(second)
                later.extend([io.start(wqkv_hbm, wqkv), io.start(gh_hbm, gh), io.start(x_hbm, x_low)])

        gain_a, back_x = attention_backward(
            sz, gh, gl[...], x, gains_ref[0:1, :], wqkv, wo, cos, sin, bias_ref,
            heads, lse_ref, mix, g_heads, g_qkv, ready
        )
        io.store(g_qkv, g_qkv_hbm)
        gl[...] = back_x.astype(BF)
        io.store(gl, g_x_hbm)
        gain_grad[...] = jnp.concatenate([gain_a, jnp.zeros((7, wide), F32)], axis=0)
        io.close()

    v = pltpu.VMEM
    return call(
        body,
        [gh, gl, x, gains, wqkv, wo, *rope, bias, heads, lse],
        [shape(t, wide), shape(sz.feat, t), shape(8, wide, dtype=F32)],
        [
            v((t, wide), F32), v((t, wide), BF), v((t, wide), BF), v((t, wide), F32), v((wide, sz.feat), BF),
            v((wide, wide), BF), v((t, t), F32), v((sz.feat, t), BF), v((sz.feat, t), BF), v((sz.width + 16, t), F32),
            v((sz.feat, t), F32), pltpu.SemaphoreType.DMA((16,)),
        ],
        10 * t * wide * sz.feat, 40,
        specs=[ANY] * 3 + [VM] + [ANY] * 2 + [VM] * 2 + [ANY] * 2 + [VM],
        out_specs=[ANY] * 2 + [VM],
    )


def qkv_grad(sz, back, a1s, g_qkv_runs, gain2, gain_a1, half):
    t, wide, cols = sz.t, sz.wide, sz.feat

    def body(back_ref, a_1, a_2, g1, g2, gain2_ref, gain_a_ref, own, s0, s1, a1, g_qkv, out, sem):
        io = Copies(sem)
        run1, run2 = pl.ds(0, t), pl.ds(t, t)
        wait([
            io.start(a_1, a1.at[run1, :]), io.start(a_2, a1.at[run2, :]),
            io.start(g1, g_qkv.at[:, run1]), io.start(g2, g_qkv.at[:, run2]),
        ])
        nz = sz.n // 4
        tile = wide // nz
        row = lax.broadcasted_iota(jnp.int32, (sz.padded, sz.padded), 0)
        for k in range(nz):
            here = pl.ds(pl.multiple_of(back_ref[k] * tile, tile), tile)
            into = tt(a1[:, here], g_qkv[...])
            attn_gain = gain_a_ref[0:1, here] + gain2_ref[0:1, here]
            ffn_gain = gain2_ref[1:2, here]
            patches = []
            for s in range(0, tile, sz.padded):
                a, f = attn_gain[:, s : s + sz.padded], ffn_gain[:, s : s + sz.padded]
                patches.append(jnp.where(row == sz.real, a, jnp.where(row == sz.real + 1, f, 0.0)))
            patch = jnp.concatenate([join(patches, 0), jnp.zeros((tile, 128 - sz.padded), F32)], axis=1)
            lo = k * tile
            out[lo : lo + tile, 0:128] = (into[:, :128] + patch).astype(BF)
            out[lo : lo + tile, 128:cols] = into[:, 128:].astype(BF)
            io.blocks(back_ref, nz, k, out, lo, half, own, (s0, s1))
        io.close()

    v = pltpu.VMEM
    return call(
        body,
        [back, *a1s, *g_qkv_runs, gain2, gain_a1],
        halves(sz, half, cols),
        [v((2 * t, wide), BF), v((cols, 2 * t), BF), v((wide, cols), BF), pltpu.SemaphoreType.DMA((2 * sz.n + 8,))],
        4 * t * wide * cols, 40,
        specs=[SMEM] + [ANY] * 4 + [VM] * 2, out_specs=[ANY] * 3,
    )


def spread(v, n, real, padded):
    lead = v.shape[:-1]
    v = v.reshape(lead + (n, real))
    v = jnp.pad(v, [(0, 0)] * len(lead) + [(0, 0), (0, padded - real)])
    return v.reshape(lead + (n * padded,))


def narrow(v, n, real, padded):
    lead = v.shape[:-1]
    return v.reshape(lead + (n, padded))[..., :real].reshape(lead + (n * real,))


def place_blocks(order, pieces):
    both = jnp.concatenate(pieces)
    spots = jnp.zeros(order.shape, jnp.int32).at[order].set(jnp.arange(order.shape[0], dtype=jnp.int32))
    return jnp.take(both, spots, axis=0).reshape(-1, both.shape[2])


def order_blocks(order, grad, half, nz):
    blocks = grad.reshape(nz, 8, half, grad.shape[1])
    at_z = jnp.take(blocks, order[:nz], axis=0)
    parts = [jnp.take(at_z, order[nz + k], axis=1) for k in range(8)]
    return jnp.concatenate(parts[:4]), jnp.concatenate(parts[4:6]), jnp.concatenate(parts[6:])


def shards(mesh, tokens, lengths, w_query, key_weight, value_weight, output_weight, w_gate, w_up, w_down, gain_attn, gain_ffn, out_grad):
    at = Place(mesh)
    n = at.n
    real, width = w_query.shape
    padded = -(-(real + 2) // 16) * 16
    sz = Sizes(n, real, padded, w_gate.shape[1], tokens.shape[0], key_weight.shape[1])
    wide, ff = sz.wide, sz.ff
    half, down_half = padded // 2, w_down.shape[0] // 2
    aligned = down_half % 16 == 0
    order = Order()
    places, back = at.piece_order(), at.grad_order()

    def pad_rows(v):
        return jnp.pad(v, ((0, padded - v.shape[0]), (0, 0)))

    def attention_shard(w_query, key_weight, value_weight, output_weight, gain_attn, gain_ffn):
        qkv = jnp.concatenate([w_query, key_weight, value_weight], axis=1)
        gains = jnp.pad(jnp.stack([gain_attn, gain_ffn]), ((0, 0), (0, qkv.shape[1] - real)))
        qkv = pad_rows(jnp.concatenate([qkv, gains]))
        return jnp.concatenate([pad_rows(spread(output_weight, n, real, padded)), qkv], axis=1)

    def tables(lengths, tokens, out_grad):
        positions, allowed = layout(lengths, tokens.shape[0])
        bias = jnp.where(allowed[0], 0.0, -1e30).astype(F32).T
        return rotation(positions[0]), bias, spread(tokens, n, real, padded), spread(out_grad, n, real, padded)

    ga, gg, gu, gd = (Gather(at, order) for _ in range(4))
    ga.start(attention_shard, w_query, key_weight, value_weight, output_weight, gain_attn, gain_ffn)
    ga.ready()
    ga.along_z()
    gg.start(pad_rows, w_gate)
    gu.start(pad_rows, w_up)
    gd.start(lambda v: spread(v, n, real, padded), w_down)
    gg.ready()
    gu.ready()
    gd.ready()
    rope, bias, x1, cot = order.do(tables, lengths, tokens, out_grad)
    ga.come()
    ga.line_up()
    ga.first()
    gg.along_z()
    ga.got_first()
    ga.second()
    gg.come()
    gg.line_up()
    gg.first()
    gu.along_z()
    x1, cot = order.do(settle, x1, cot)
    ga.got_second()
    gg.got_first()
    gu.come()
    ga.cores()
    gg.second()
    gu.line_up()
    gu.first()
    attn_pieces = ga.pieces()
    gd.along_z()
    hidden1, a1_1, heads1, lse1, mixp1, gains = order.do(
        lambda *v: first_attention(sz, *v), places, attn_pieces, x1, rope, bias
    )
    gd.come()
    gg.got_second()
    gg.cores()
    gu.got_first()
    gu.second()
    gd.line_up()
    gd.first()
    gate_pieces = gg.pieces()
    a2_1, gate1 = order.do(lambda *v: first_gate(sz, *v), places, gate_pieces, hidden1, gains)
    gd.got_first()
    gd.second()
    gu.got_second()
    gu.cores()
    up_pieces = gu.pieces()
    gd.cores(gd.both)
    up1, inner1 = order.do(lambda *v: first_up(sz, *v), places, up_pieces, a2_1, gate1)
    gd.got_second()
    gd.cores(gd.third)
    down_pieces = gd.pieces()
    if not aligned:
        down_pieces = place_blocks(places, down_pieces)

    (second, wqkv, wo, a1_2, mixp2, a2_2, gu2, gl2, g_qkv2, gh1, gl1, gu1, gain2, *grads) = order.do(
        lambda *v: middle(sz, *v, half, down_half),
        places, back, down_pieces, attn_pieces, gate_pieces, up_pieces, hidden1, inner1, gate1, up1, a2_1, gains, rope, bias, cot,
    )
    downs, gates = grads[:3], grads[3:]
    if not aligned:
        downs = order_blocks(back, downs[0], down_half, at.nz)
    sd = Scatter(at, order, *downs)
    sg = Scatter(at, order, *gates)
    sd.core(0)
    sg.core(0)
    sd.core(1)
    sg.core(1)
    sd.come_core(0)
    sd.first()
    sg.come_core(0)
    sg.first()
    sd.come_core(1)
    sg.come_core(1)
    own, *send = order.do(
        lambda *v: up_out_grad(sz, *v, half), back, (a2_1, a2_2), (gu1, gu2), (mixp1, mixp2), (gl1, gl2)
    )
    sd.come()
    su = Scatter(at, order, own, *send)
    su.core(0)
    su.core(1)
    sd.second()
    su.come_core(0)
    su.first()
    su.come_core(1)
    g_x, g_qkv1, gain_a1 = order.do(
        lambda *v: last_attention(sz, *v), gh1, gl1, x1, gains, wqkv, wo, rope, bias, heads1, lse1
    )
    sg.come()
    sd.come()
    sg.second()
    sd.along_z()
    own, *send = order.do(
        lambda *v: qkv_grad(sz, *v, half), back, (a1_1, a1_2), (g_qkv1, g_qkv2), gain2, gain_a1
    )
    sg.come()
    sd.come_z()
    sg.along_z()
    su.come()
    su.second()
    sa = Scatter(at, order, own, *send)
    sa.core(0)
    sa.core(1)
    sa.come_core(0)
    sa.first()
    sa.come_core(1)
    su.come()
    sg.come_z()
    su.along_z()
    sa.come()
    sa.second()
    sd.along_x()
    sg.along_x()
    second, g_x = order.do(settle, second, g_x)
    su.come_z()
    sa.come()
    sa.along_z()
    su.along_x()
    sd.come()
    sd.cores()
    sa.come_z()
    sa.along_x()
    sg.come()
    sg.cores()
    sd.come()
    r_down = sd.result()
    su.come()
    su.cores()
    sg.come()
    r_gate = sg.result()
    su.come()
    r_up = su.result()
    second, g_x = narrow(second, n, real, padded), narrow(g_x, n, real, padded)
    sa.come()
    sa.cores()
    sa.come()
    r_in = sa.result()
    kv = key_weight.shape[1]
    return (
        second,
        g_x,
        r_in[:real, :width],
        r_in[:real, width : width + kv],
        r_in[:real, width + kv :],
        narrow(r_up[:real, ff:], n, real, padded),
        r_gate[:real],
        r_up[:real, :ff],
        narrow(r_down, n, real, padded),
        r_in[real, :real],
        r_in[real + 1, :real],
    )


def solution(mesh):
    rows, split, gain = P(("dp", "fsdp"), None), P("fsdp", None), P("fsdp")
    return jax.shard_map(
        functools.partial(shards, mesh),
        mesh=mesh,
        in_specs=(rows, rows) + (split,) * 7 + (gain, gain, rows),
        out_specs=(rows, rows) + (split,) * 7 + (gain, gain),
        check_vma=False,
    )
```

```python
import functools
import math

import jax
import jax.numpy as jnp
from jax import lax
from jax.experimental import pallas as pl
from jax.experimental.pallas import tpu as pltpu
from jax.sharding import PartitionSpec as P

HEAD_SIZE = 64
GROUP = 3
ROPE_BASE = 10000.0
EPS = 1e-05
BF = jnp.bfloat16
F32 = jnp.float32
MIB = 1024 * 1024


def layout(doc_lengths, token_count):
    ends = jnp.cumsum(doc_lengths, axis=1)
    starts = ends - doc_lengths
    place = jnp.arange(token_count, dtype=jnp.int32)
    document = jnp.sum((place[None, :, None] >= ends[:, None, :]).astype(jnp.int32), axis=2)
    inside = place[None, :] < ends[:, -1:]
    segment = jnp.where(inside, document, -1)
    chosen = (
        document[:, :, None] == jnp.arange(doc_lengths.shape[1], dtype=jnp.int32)[None, None, :]
    )
    begin = jnp.sum(jnp.where(chosen, starts[:, None, :], 0), axis=2)
    positions = jnp.where(inside, place[None, :] - begin, 0)
    causal = place[:, None] >= place[None, :]
    same = (segment[:, :, None] == segment[:, None, :]) & (segment[:, :, None] >= 0)
    allowed = same & causal[None] | (place[:, None] == place[None, :])[None]
    return (positions, allowed)


def rotation(positions):
    half = HEAD_SIZE // 2
    frequency = jnp.exp(jnp.arange(half, dtype=F32) * (-2.0 * math.log(ROPE_BASE) / HEAD_SIZE))
    angle = positions.astype(F32)[None, :] * frequency[:, None]
    return (jnp.cos(angle), jnp.sin(angle))


class Place:
    def __init__(self, mesh):
        self.n, self.groups = mesh.shape["fsdp"], mesh.shape["dp"]
        self.nz = self.n // 4
        i = lax.axis_index("fsdp")
        self.c, self.y, self.z = i % 2, (i // 2) % 2, i // 4
        self.p = lax.axis_index("dp") % 2

    def swap_core(self, v):
        return lax.ppermute(v, "fsdp", [(i, i ^ 1) for i in range(self.n)])

    def shift_z(self, v, k):
        return lax.ppermute(v, "fsdp", [(i, (i + 4 * k) % self.n) for i in range(self.n)])

    def swap_x(self, v):
        return lax.ppermute(v, "dp", [(d, d ^ 1) for d in range(self.groups)])

    def cross(self, v, first):
        pairs = []
        for d in range(self.groups):
            for i in range(self.n):
                along_x = (i % 2 == 0) == first
                e, j = (d ^ 1, i) if along_x else (d, i ^ 2)
                pairs.append((d * self.n + i, e * self.n + j))
        return lax.ppermute(v, ("dp", "fsdp"), pairs)

    def piece_order(self):
        order = []
        for h in (self.c, 1 - self.c):
            for j in range(4 * self.nz):
                dz, slot = j % self.nz, j // self.nz
                lo, hi = slot % 2, slot // 2
                dy, dc = jnp.where(h == 0, lo, hi), jnp.where(h == 0, hi, lo)
                z = (self.z - dz + self.nz) % self.nz
                order.append((((z * 2 + (self.y ^ dy)) * 2 + (self.p ^ dc)) * 2 + h).astype(jnp.int32))
        return jnp.stack(order)

    def grad_order(self):
        order = [(self.z + k) % self.nz for k in range(self.nz)]
        for h in (self.c, 1 - self.c):
            for hi in (0, 1):
                for lo in (0, 1):
                    of_c, of_y = jnp.where(h == 0, hi, lo), jnp.where(h == 0, lo, hi)
                    c = jnp.where(of_c == 1, self.p, 1 - self.p)
                    y = jnp.where(of_y == 1, self.y, 1 - self.y)
                    order.append((y * 2 + c) * 2 + h)
        return jnp.stack(order).astype(jnp.int32)


def pick(v, k, axis=0):
    return lax.dynamic_index_in_dim(v, k, axis, keepdims=False)


class Order:
    def __init__(self):
        self.last = ()

    def do(self, step, *inputs):
        leaves, tree = jax.tree.flatten(inputs)
        if self.last:
            leaves = lax.optimization_barrier((*leaves, *self.last))[: len(leaves)]
        out = step(*jax.tree.unflatten(tree, leaves))
        self.last = (jax.tree.leaves(out)[0],)
        return out

    def tie(self, v):
        return lax.optimization_barrier((v, *self.last))[0] if self.last else v

    def got(self, *received):
        out = lax.optimization_barrier((*received, *self.last))[: len(received)]
        self.last = (out[0],)
        return out[0] if len(out) == 1 else out


def add(*terms):
    return functools.reduce(lambda a, b: a + b, [t.astype(F32) for t in terms])


class Gather:
    def __init__(self, at, order):
        self.at, self.order = at, order

    def start(self, make, *inputs):
        def step(*inputs):
            shard = make(*inputs)
            halves = shard.reshape(2, shard.shape[0] // 2, shard.shape[1])
            return pick(halves, self.at.c), pick(halves, 1 - self.at.c)

        self.keep, send = self.order.do(step, *inputs)
        self.moving = self.at.swap_core(send)

    def ready(self):
        at = self.at
        got = self.order.got(self.moving)
        self.mine = self.order.do(lambda k, g: jnp.where(at.p == at.c, k, g)[None], self.keep, got)

    def along_z(self):
        mine = self.order.tie(self.mine)
        self.moving = [self.at.shift_z(mine, k) for k in range(1, self.at.nz)]

    def come(self):
        parts = self.order.got(*self.moving)
        self.parts = parts if isinstance(parts, tuple) else (parts,)

    def line_up(self):
        self.line = self.order.do(lambda *v: jnp.concatenate(v), self.mine, *self.parts)

    def first(self):
        self.moving = self.at.cross(self.order.tie(self.line), False)

    def got_first(self):
        self.got = self.order.got(self.moving)

    def second(self):
        self.both = self.order.do(lambda *v: jnp.concatenate(v), self.line, self.got)
        self.moving = self.at.cross(self.both, True)
        self.others = []

    def got_second(self):
        self.third = self.order.got(self.moving)

    def cores(self, *which):
        self.others += [self.at.swap_core(self.order.tie(v)) for v in which or (self.both, self.third)]

    def pieces(self):
        return (self.both, self.third, *self.order.got(*self.others))


class Scatter:
    def __init__(self, at, order, own, *send):
        self.at, self.order, self.own = at, order, own
        self.send, self.swaps, self.other = send, {}, {}

    def core(self, k):
        self.swaps[k] = self.at.swap_core(self.order.tie(self.send[k]))

    def sums(self, *terms):
        cuts = [(lo, lo + count) for _, lo, count in terms]

        def step(*v):
            return add(*[a[lo:hi] for a, (lo, hi) in zip(v, cuts)]).astype(BF)

        return self.order.do(step, *[a for a, _, _ in terms])

    def come(self):
        self.got = self.order.got(self.moving)

    def come_core(self, k):
        self.other[k] = self.order.got(self.swaps[k])

    def first(self):
        two = 2 * self.at.nz
        self.moving = self.at.cross(self.sums((self.own, 0, two), (self.other[0], 0, two)), True)

    def second(self):
        nz = self.at.nz
        self.crossed = self.got
        sent = self.sums((self.own, 2 * nz, nz), (self.other[1], 0, nz), (self.crossed, 0, nz))
        self.moving = self.at.cross(sent, False)

    def along_z(self):
        nz = self.at.nz
        self.low = self.sums((self.own, 3 * nz, nz), (self.other[1], nz, nz), (self.crossed, nz, nz), (self.got, 0, nz))
        self.moving = [self.at.shift_z(self.low[k : k + 1], k) for k in range(1, nz)]

    def come_z(self):
        parts = self.order.got(*self.moving)
        self.parts = parts if isinstance(parts, tuple) else (parts,)

    def along_x(self):
        total = self.sums((self.low, 0, 1), *[(p, 0, 1) for p in self.parts])[0]
        step = 2
        while step < self.at.groups:
            pairs = [(d, d ^ step) for d in range(self.at.groups)]
            total = add(total, lax.ppermute(total, "dp", pairs)).astype(BF)
            step *= 2
        self.total = total
        self.moving = self.at.swap_x(total)

    def cores(self):
        here = self.at.p == self.at.c
        self.keep, send = self.order.do(
            lambda a, b: (jnp.where(here, a, b), jnp.where(here, b, a)), self.total, self.got
        )
        self.moving = self.at.swap_core(send)

    def result(self):
        first = self.at.c == 0
        return self.order.do(
            lambda a, b: jnp.concatenate([jnp.where(first, a, b), jnp.where(first, b, a)]).astype(F32), self.keep, self.got
        )


VM = pl.BlockSpec(memory_space=pltpu.VMEM)
ANY = pl.BlockSpec(memory_space=pl.ANY)
SMEM = pl.BlockSpec(memory_space=pltpu.SMEM)


def nn(left, right):
    return jnp.dot(left, right, preferred_element_type=F32)


def nt(left, right):
    return lax.dot_general(left, right, (((1,), (1,)), ((), ())), preferred_element_type=F32)


def tn(left, right):
    return lax.dot_general(left, right, (((0,), (0,)), ((), ())), preferred_element_type=F32)


def tt(left, right):
    return lax.dot_general(left, right, (((0,), (1,)), ((), ())), preferred_element_type=F32)


def join(parts, axis):
    return jnp.concatenate(parts, axis=axis) if len(parts) > 1 else parts[0]


def call(body, ins, outs, scratch, flops, limit, specs=None, out_specs=None):
    return pl.pallas_call(
        body,
        in_specs=specs or [VM] * len(ins),
        out_specs=out_specs or [VM] * len(outs),
        out_shape=outs,
        scratch_shapes=scratch,
        compiler_params=pltpu.CompilerParams(vmem_limit_bytes=max(limit, 60) * MIB),
        cost_estimate=pl.CostEstimate(flops=1000, bytes_accessed=1000, transcendentals=0),
    )(*ins)


def fetches(order_ref, pieces, dests, sem, base):
    copies = []
    half = pieces[0].shape[1]
    at = 0
    for ref in pieces:
        for j in range(ref.shape[0]):
            row = pl.multiple_of(order_ref[at] * half, half)
            at += 1
            for dest, col in dests:
                whole = col == 0 and dest.shape[1] == ref.shape[2]
                src = ref.at[j] if whole else ref.at[j, :, pl.ds(col, dest.shape[1])]
                copies.append(
                    pltpu.make_async_copy(src, dest.at[pl.ds(row, half), :], sem.at[base + len(copies)])
                )
    return copies


class Copies:
    def __init__(self, sem):
        self.sem, self.used, self.open = sem, 0, []

    def start(self, source, dest):
        copy = pltpu.make_async_copy(source, dest, self.sem.at[self.used])
        self.used += 1
        copy.start()
        return copy

    def store(self, source, dest):
        self.open.append(self.start(source, dest))

    def blocks(self, order_ref, nz, k, source, base, half, own, sends):
        for quarter in range(4):
            place, part = quarter % 2 * nz + k, quarter // 2
            for first, dest in ((0, own.at[2 * nz * part + place]), (4, sends[part].at[place])):
                row = base + pl.multiple_of(order_ref[nz + first + quarter] * half, half)
                self.store(source.at[pl.ds(row, half), :], dest)

    def close(self):
        wait(self.open)
        self.open = []


def start(copies):
    for copy in copies:
        copy.start()
    return copies


def wait(copies):
    for copy in copies:
        copy.wait()


def inverse_rms(v, width):
    return lax.rsqrt(jnp.sum(v * v, axis=1, keepdims=True) * (1.0 / width) + EPS)


def norm_back(values, gain, grad, width):
    scale = inverse_rms(values, width)
    unit = values * scale
    gain_grad = jnp.sum(grad * unit, axis=0, keepdims=True)
    inner = grad * gain
    mean = jnp.sum(inner * unit, axis=1, keepdims=True) * (1.0 / width)
    return gain_grad, scale * (inner - unit * mean)


class Sizes:
    def __init__(self, n, real, padded, ff, t, kv):
        self.n, self.real, self.padded, self.ff, self.t = n, real, padded, ff, t
        self.width, self.wide = n * real, n * padded
        self.hq, self.kvh = self.width // HEAD_SIZE, kv // HEAD_SIZE
        self.heads = self.hq + 2 * self.kvh
        self.feat = self.heads * HEAD_SIZE
        self.group = self.hq // self.kvh
        self.lse = -(-self.hq // 8) * 8
        self.block = 128 if t % 128 == 0 else t
        self.blocks = t // self.block
        self.tile = 512 if ff % 512 == 0 else ff


def head(ref, h):
    return ref[h * HEAD_SIZE : (h + 1) * HEAD_SIZE, :]


def by_block(sz, parts, op):
    b = sz.block
    return [
        functools.reduce(op, [parts[j][:, b * (i - j) : b * (i - j + 1)] for j in range(i + 1)])
        for i in range(sz.blocks)
    ]


def plus(a, b):
    return a + b


def block_product(sz, left, parts):
    b, out = sz.block, None
    for j in range(sz.blocks):
        part = nn(left[:, b * j : b * (j + 1)], parts[j])
        if j:
            part = jnp.concatenate([jnp.zeros((left.shape[0], b * j), F32), part], axis=1)
        out = part if out is None else out + part
    return out


def attention_forward(sz, x, gain, wqkv, wo, cos, sin, bias, a1, heads, lse, mixp, mix, done=lambda stage: None):
    b, half = sz.block, HEAD_SIZE // 2
    a1[...] = (x * inverse_rms(x, sz.width) * gain).astype(BF)
    for c in range(0, sz.heads, 4):
        end = min(c + 4, sz.heads)
        part = tt(wqkv[:, c * HEAD_SIZE : end * HEAD_SIZE], a1[...])
        for h in range(c, end):
            lo = (h - c) * HEAD_SIZE
            first, second = part[lo : lo + half], part[lo + half : lo + HEAD_SIZE]
            if h < sz.hq + sz.kvh:
                first, second = (
                    first * cos[...] - second * sin[...],
                    second * cos[...] + first * sin[...],
                )
            if h < sz.hq:
                first, second = first * HEAD_SIZE ** (-0.5), second * HEAD_SIZE ** (-0.5)
            heads[h * HEAD_SIZE : h * HEAD_SIZE + half, :] = first.astype(BF)
            heads[h * HEAD_SIZE + half : (h + 1) * HEAD_SIZE, :] = second.astype(BF)
    done(0)
    if sz.lse > sz.hq:
        lse[...] = jnp.zeros(lse.shape, F32)
    for first in range(0, sz.kvh, 3):
        groups = range(first, min(first + 3, sz.kvh))
        keys = {g: head(heads, sz.hq + g).T for g in groups}
        values = {g: head(heads, sz.hq + sz.kvh + g) for g in groups}
        pairs = [(g, g * sz.group + r) for g in groups for r in range(sz.group)]
        scores = []
        for g, h in pairs:
            q = head(heads, h)
            scores.append([
                nn(keys[g][b * j : b * (j + 1)], q[:, b * j :]) + bias[b * j : b * (j + 1), b * j :]
                for j in range(sz.blocks)
            ])
        tops = [by_block(sz, [jnp.max(s, axis=0, keepdims=True) for s in ss], jnp.maximum) for ss in scores]
        powers, sums = [], []
        for ss, top in zip(scores, tops):
            e = [jnp.exp(ss[j] - join(top[j:], 1)) for j in range(sz.blocks)]
            sums.append(join(by_block(sz, [jnp.sum(v, axis=0, keepdims=True) for v in e], plus), 1))
            powers.append([v.astype(BF) for v in e])
        for (g, h), e, top, summed in zip(pairs, powers, tops, sums):
            out = block_product(sz, values[g], e)
            mix[h * HEAD_SIZE : (h + 1) * HEAD_SIZE, :] = out * (1.0 / summed)
            lse[h : h + 1, :] = join(top, 1) + jnp.log(summed)
    row = lax.broadcasted_iota(jnp.int32, (sz.padded, sz.t), 0)
    for j in range(sz.n):
        part = mix[sz.real * j : sz.real * j + sz.padded, :]
        mixp[sz.padded * j : sz.padded * (j + 1), :] = jnp.where(row < sz.real, part, 0.0).astype(BF)
    done(1)
    return x + tn(mixp[...], wo[...])


def attention_backward(sz, gh, gl, x, gain, wqkv, wo, cos, sin, bias, heads, lse, gm, g_heads, g_qkv, ready=None):
    b, half = sz.block, HEAD_SIZE // 2
    for j in range(sz.n):
        part = nt(wo[sz.padded * j : sz.padded * (j + 1), :], gl) if sz.n < 4 else None
        if part is not None:
            gm[sz.real * j : sz.real * j + sz.padded, :] = part
    if sz.n >= 4:
        quarter = sz.n // 4
        for c in range(4):
            part = nt(wo[sz.padded * quarter * c : sz.padded * quarter * (c + 1), :], gl)
            for j in range(quarter):
                at = sz.real * (quarter * c + j)
                gm[at : at + sz.padded, :] = part[sz.padded * j : sz.padded * (j + 1)]
    if ready is not None:
        ready(False)
    for g in range(sz.kvh):
        kt = head(heads, sz.hq + g)
        k = kt.T
        v = head(heads, sz.hq + sz.kvh + g).T
        hs = range(g * sz.group, (g + 1) * sz.group)
        qs, gms = [head(heads, h) for h in hs], [head(gm, h).astype(BF) for h in hs]
        cut = [(b * j, b * (j + 1)) for j in range(sz.blocks)]
        scores = [[nn(k[lo:hi], q[:, lo:]) + bias[lo:hi, lo:] for lo, hi in cut] for q in qs]
        gps = [[nn(v[lo:hi], m[:, lo:]) for lo, hi in cut] for m in gms]
        ps = [[jnp.exp(s - lse[h : h + 1, :][:, lo:]) for s, (lo, _) in zip(ss, cut)] for ss, h in zip(scores, hs)]
        gk = gv = None
        for h, q, m, p, gp in zip(hs, qs, gms, ps, gps):
            d = by_block(sz, [jnp.sum(a * c, axis=0, keepdims=True) for a, c in zip(p, gp)], plus)
            g_s = [(p[j] * (gp[j] - join(d[j:], 1))).astype(BF) for j in range(sz.blocks)]
            low = [a.astype(BF) for a in p]
            part_k = join([nt(q[:, lo:], a) for (lo, _), a in zip(cut, g_s)], 1)
            part_v = join([nt(m[:, lo:], a) for (lo, _), a in zip(cut, low)], 1)
            g_heads[h * HEAD_SIZE : (h + 1) * HEAD_SIZE, :] = block_product(sz, kt, g_s) * HEAD_SIZE ** (-0.5)
            gk = part_k if gk is None else gk + part_k
            gv = part_v if gv is None else gv + part_v
        at = (sz.hq + g) * HEAD_SIZE
        g_heads[at : at + HEAD_SIZE, :] = gk
        at = (sz.hq + sz.kvh + g) * HEAD_SIZE
        g_qkv[at : at + HEAD_SIZE, :] = gv.astype(BF)
    for h in range(sz.hq + sz.kvh):
        at = h * HEAD_SIZE
        first, second = g_heads[at : at + half, :], g_heads[at + half : at + HEAD_SIZE, :]
        g_qkv[at : at + half, :] = (first * cos[...] + second * sin[...]).astype(BF)
        g_qkv[at + half : at + HEAD_SIZE, :] = (second * cos[...] - first * sin[...]).astype(BF)
    if ready is not None:
        ready(True)
    gain_grad, back = norm_back(x[...], gain, tt(g_qkv[...], wqkv[...]), sz.width)
    return gain_grad, gh[...] + back


def ffn_up(sz, hidden, gain, a2, wg, wu, gate, up, inner):
    a2[...] = (hidden * inverse_rms(hidden, sz.width) * gain).astype(BF)
    for c in range(0, sz.ff, sz.tile):
        cols = slice(c, c + sz.tile)
        gate_part = nn(a2[...], wg[:, cols])
        up_part = nn(a2[...], wu[:, cols])
        gate[:, cols] = gate_part.astype(BF)
        up[:, cols] = up_part.astype(BF)
        inner[:, cols] = (gate_part * jax.nn.sigmoid(gate_part) * up_part).astype(BF)


def ffn_back_tile(cl, wd, gate, up, gg, gu, cols):
    g_inner = nt(cl[...], wd[cols, :])
    z = gate[:, cols].astype(F32)
    sg = jax.nn.sigmoid(z)
    silu = z * sg
    gg[:, cols] = (g_inner * up[:, cols].astype(F32) * (sg + silu * (1.0 - sg))).astype(BF)
    gu[:, cols] = (g_inner * silu).astype(BF)


def ffn_backward(sz, grad, cl, hidden, gain, wg, wu, wd, gate, up, gg, gu):
    for c in range(0, sz.ff, sz.tile):
        ffn_back_tile(cl, wd, gate, up, gg, gu, slice(c, c + sz.tile))
    g_a2 = nt(gg[...], wg[...]) + nt(gu[...], wu[...])
    gain_grad, back = norm_back(hidden[...], gain, g_a2, sz.width)
    return gain_grad, grad + back


def shape(*dims, dtype=BF):
    return jax.ShapeDtypeStruct(dims, dtype)


def halves(sz, half, cols):
    return [shape(sz.n, half, cols)] + [shape(sz.n // 2, half, cols)] * 2


def first_attention(sz, order, pieces, x, rope, bias):
    t, wide = sz.t, sz.wide

    def body(order_ref, p0, p1, p2, p3, x_hbm, cos, sin, bias_hbm,
             hidden_hbm, a1_hbm, heads_hbm, lse, mixp_hbm, gains,
             x, hidden, a1, heads, mixp, wo, wqkv, mix, bias_ref, sem, out_sem):
        io = Copies(out_sem)
        first = start(fetches(order_ref, (p0, p1, p2, p3), [(wqkv, sz.wide)], sem, 0))
        loads = [io.start(x_hbm, x), io.start(bias_hbm, bias_ref)]
        last = start(fetches(order_ref, (p0, p1, p2, p3), [(wo, 0)], sem, 2 * sz.n))
        wait(first)
        rows = []
        for k in range(2):
            parts = []
            for j in range(sz.n):
                lo = sz.padded * (j + 1) - 16
                tile = wqkv[lo : lo + 16, 0:128].astype(F32)
                at = sz.real + k - (sz.padded - 16)
                parts.append(tile[at : at + 1, : sz.padded])
            rows.append(jnp.concatenate(parts, axis=1))
        gains[...] = jnp.concatenate(rows + [jnp.zeros((6, sz.wide), F32)], axis=0)
        wait(loads)
        hidden[...] = x[...].astype(F32)

        def done(stage):
            for a, b in (((a1, a1_hbm), (heads, heads_hbm)), ((mixp, mixp_hbm),))[stage]:
                io.store(a, b)
            if stage == 1:
                wait(last)

        hidden[...] = attention_forward(
            sz, hidden[...], gains[0:1, :], wqkv, wo, cos, sin, bias_ref, a1, heads, lse, mixp, mix, done
        )
        io.store(hidden, hidden_hbm)
        io.close()

    v = pltpu.VMEM
    return call(
        body,
        [order, *pieces, x, *rope, bias],
        [
            shape(t, wide, dtype=F32), shape(t, wide), shape(sz.feat, t), shape(sz.lse, t, dtype=F32),
            shape(wide, t), shape(8, wide, dtype=F32),
        ],
        [
            v((t, wide), BF), v((t, wide), F32), v((t, wide), BF), v((sz.feat, t), BF), v((wide, t), BF),
            v((wide, wide), BF), v((wide, sz.feat), BF), v((sz.width + 16, t), F32), v((t, t), F32),
            pltpu.SemaphoreType.DMA((4 * sz.n,)), pltpu.SemaphoreType.DMA((8,)),
        ],
        6 * t * wide * sz.feat, 40,
        specs=[SMEM] + [ANY] * 5 + [VM] * 2 + [ANY],
        out_specs=[ANY] * 3 + [VM, ANY, VM],
    )


def first_gate(sz, order, pieces, hidden, gains):
    t, wide, ff = sz.t, sz.wide, sz.ff

    def body(order_ref, p0, p1, p2, p3, hidden_hbm, gains_ref, a2_hbm, gate_hbm, hidden_ref, a2, gate, w, sem, out_sem):
        out = Copies(out_sem)
        load = out.start(hidden_hbm, hidden_ref)
        copies = start(fetches(order_ref, (p0, p1, p2, p3), [(w, 0)], sem, 0))
        wait([load])
        hidden = hidden_ref[...]
        a2[...] = (hidden * inverse_rms(hidden, sz.width) * gains_ref[1:2, :]).astype(BF)
        wait(copies)
        out.store(a2, a2_hbm)
        for c in range(0, ff, sz.tile):
            cols = slice(c, c + sz.tile)
            gate[:, cols] = nn(a2[...], w[:, cols]).astype(BF)
            out.store(gate.at[:, pl.ds(c, sz.tile)], gate_hbm.at[:, pl.ds(c, sz.tile)])
        out.close()

    return call(
        body,
        [order, *pieces, hidden, gains],
        [shape(t, wide), shape(t, ff)],
        [pltpu.VMEM((t, wide), F32), pltpu.VMEM((t, wide), BF), pltpu.VMEM((t, ff), BF), pltpu.VMEM((wide, ff), BF),
         pltpu.SemaphoreType.DMA((2 * sz.n,)), pltpu.SemaphoreType.DMA((2 + ff // sz.tile,))],
        2 * t * wide * ff, 40,
        specs=[SMEM] + [ANY] * 5 + [VM], out_specs=[ANY] * 2,
    )


def first_up(sz, order, pieces, a2, gate):
    t, wide, ff = sz.t, sz.wide, sz.ff

    def body(order_ref, p0, p1, p2, p3, a2_hbm, gate_hbm, up_hbm, inner_hbm, a2, gate, up, inner, w, sem, out_sem):
        out = Copies(out_sem)
        loads = [out.start(a2_hbm, a2), out.start(gate_hbm, gate)]
        wait(start(fetches(order_ref, (p0, p1, p2, p3), [(w, 0)], sem, 0)))
        wait(loads)
        for c in range(0, ff, sz.tile):
            cols, part = slice(c, c + sz.tile), pl.ds(c, sz.tile)
            value = nn(a2[...], w[:, cols])
            up[:, cols] = value.astype(BF)
            z = gate[:, cols].astype(F32)
            inner[:, cols] = (z * jax.nn.sigmoid(z) * value).astype(BF)
            out.store(inner.at[:, part], inner_hbm.at[:, part])
            out.store(up.at[:, part], up_hbm.at[:, part])
        out.close()

    return call(
        body,
        [order, *pieces, a2, gate],
        [shape(t, ff), shape(t, ff)],
        [pltpu.VMEM((t, wide), BF)] + [pltpu.VMEM((t, ff), BF)] * 3 + [pltpu.VMEM((wide, ff), BF),
         pltpu.SemaphoreType.DMA((2 * sz.n,)), pltpu.SemaphoreType.DMA((2 + 2 * (ff // sz.tile),))],
        2 * t * wide * ff, 40,
        specs=[SMEM] + [ANY] * 6, out_specs=[ANY] * 2,
    )


def middle(sz, order, back, down_pieces, attn_pieces, gate_pieces, up_pieces, hidden1, inner1, gate1, up1, a2_1, gains, rope, bias,
           out_grad, half, down_half):
    aligned = isinstance(down_pieces, tuple)
    downs = list(down_pieces) if aligned else [down_pieces]
    t, wide, ff = sz.t, sz.wide, sz.ff

    def body(*refs):
        order_ref, back_ref, refs = refs[0], refs[1], refs[2:]
        down_refs, refs = refs[: len(downs)], refs[len(downs) :]
        attn_refs, gate_refs, up_refs, refs = refs[:4], refs[4:8], refs[8:12], refs[12:]
        (hidden1_hbm, inner1_hbm, gate1_hbm, up1_hbm, a2_1_hbm, gains_ref, cos, sin, bias_hbm, cl_hbm,
         second_hbm, wqkv_hbm, wo_hbm, a1_hbm, mixp_hbm, a2_hbm, gu_hbm, gl_hbm, g_qkv_hbm, gh1_hbm, gl1_hbm, gu1_hbm,
         gain_grads, *refs) = refs
        down_out, gate_out, refs = refs[:3], refs[3:6], refs[6:]
        (wd, wqkv, wo, wg, wu, inners, cls, x2, hidden, a1, heads, lse, mixp, a2s, gate, up, ggs, gu, gl, g_qkv,
         bias_ref, mix, g_heads, sem, piece_sem) = refs
        io = Copies(sem)
        if aligned:
            first = start(fetches(order_ref, down_refs, [(wd, 0)], piece_sem, 0))
        else:
            first = [io.start(down_refs[0], wd)]
        run1, run2 = pl.ds(0, t), pl.ds(t, t)
        inner1, inner2 = inners.at[run1, :], inners.at[run2, :]
        cl1, cl2 = cls.at[run1, :], cls.at[run2, :]
        a2, gg1, gg2 = a2s.at[run2, :], ggs.at[run1, :], ggs.at[run2, :]
        first += [io.start(inner1_hbm, inner1), io.start(hidden1_hbm, x2)]
        wait(first)
        loads = start(fetches(order_ref, attn_refs, [(wqkv, wide)], piece_sem, 2 * sz.n))
        loads += [io.start(bias_hbm, bias_ref)]
        last = start(fetches(order_ref, attn_refs, [(wo, 0)], piece_sem, 4 * sz.n))
        x2[...] = x2[...] + nn(inner1[...], wd[...])
        wait(loads)
        sides = start(fetches(order_ref, gate_refs, [(wg, 0)], piece_sem, 6 * sz.n))
        sides += start(fetches(order_ref, up_refs, [(wu, 0)], piece_sem, 8 * sz.n))
        sides += [io.start(cl_hbm, cl2)]
        hidden[...] = attention_forward(
            sz, x2[...], gains_ref[0:1, :], wqkv, wo, cos, sin, bias_ref, a1, heads, lse, mixp, mix,
            lambda stage: wait(last) if stage == 1 else None
        )
        wait(sides)
        for a, b in ((a1, a1_hbm), (mixp, mixp_hbm), (wqkv, wqkv_hbm), (wo, wo_hbm)):
            io.store(a, b)
        ffn_up(sz, hidden[...], gains_ref[1:2, :], a2, wg, wu, gate, up, inner2)
        io.store(a2, a2_hbm)
        gl[...] = (hidden[...] + nn(inner2[...], wd[...])).astype(BF)
        out = io.start(gl, second_hbm)
        gain_f, gh = ffn_backward(
            sz, cl2[...].astype(F32), cl2, hidden[...], gains_ref[1:2, :], wg, wu, wd, gate, up, gg2, gu
        )
        gus_out = io.start(gu, gu_hbm)
        loads = [io.start(gate1_hbm, gate), io.start(up1_hbm, up), io.start(a2_1_hbm, a2s.at[run1, :])]
        hidden[...] = gh
        wait([out])
        gl[...] = gh.astype(BF)
        out = io.start(gl, gl_hbm)
        gain_a, g_x = attention_backward(
            sz, hidden, gl[...], x2, gains_ref[0:1, :], wqkv, wo, cos, sin, bias_ref, heads, lse,
            mix, g_heads, g_qkv
        )
        io.store(g_qkv, g_qkv_hbm)
        hidden[...] = g_x
        loads.append(io.start(hidden1_hbm, x2))
        cl1[...] = g_x.astype(BF)
        wait(loads + [out, gus_out])
        gain_f1, gh = ffn_backward(
            sz, hidden[...], cl1, x2, gains_ref[1:2, :], wg, wu, wd, gate, up, gg1, gu
        )
        io.store(gu, gu1_hbm)
        hidden[...] = gh
        gl[...] = gh.astype(BF)
        io.store(hidden, gh1_hbm)
        io.store(gl, gl1_hbm)
        gain_grads[...] = jnp.concatenate([gain_a, gain_f + gain_f1, jnp.zeros((6, wide), F32)], axis=0)
        nz = sz.n // 4
        tile = ff // nz
        for k in range(nz):
            if aligned:
                rows = inners[:, pl.ds(pl.multiple_of(back_ref[k] * tile, tile), tile)]
                wd[k * tile : (k + 1) * tile, :] = tn(rows, cls[...]).astype(BF)
                io.blocks(back_ref, nz, k, wd, k * tile, down_half, down_out[0], down_out[1:])
        if not aligned:
            wd[...] = tn(inners[...], cls[...]).astype(BF)
            io.store(wd, down_out[0])
        tile = wide // nz
        for k in range(nz):
            rows = a2s[:, pl.ds(pl.multiple_of(back_ref[k] * tile, tile), tile)]
            wg[k * tile : (k + 1) * tile, :] = tn(rows, ggs[...]).astype(BF)
            io.blocks(back_ref, nz, k, wg, k * tile, half, gate_out[0], gate_out[1:])
        io.close()

    ins = [order, back, *downs, *attn_pieces, *gate_pieces, *up_pieces, hidden1, inner1, gate1, up1, a2_1, gains, *rope, bias,
           out_grad]
    specs = [SMEM] * 2 + [ANY] * (len(downs) + 17) + [VM] * 3 + [ANY] * 2
    places = halves(sz, down_half, wide) if aligned else [shape(ff, wide)] + [shape(8, 128)] * 2
    outs = [
        shape(t, wide), shape(wide, sz.feat), shape(wide, wide), shape(t, wide), shape(wide, t), shape(t, wide), shape(t, ff),
        shape(t, wide), shape(sz.feat, t), shape(t, wide, dtype=F32), shape(t, wide), shape(t, ff),
        shape(8, wide, dtype=F32), *places, *halves(sz, half, ff),
    ]
    out_specs = [ANY] * 12 + [VM] + [ANY] * 6
    v = pltpu.VMEM
    scratch = [
        v((ff, wide), BF), v((wide, sz.feat), BF), v((wide, wide), BF), v((wide, ff), BF), v((wide, ff), BF),
        v((2 * t, ff), BF), v((2 * t, wide), BF), v((t, wide), F32), v((t, wide), F32), v((t, wide), BF), v((sz.feat, t), BF),
        v((sz.lse, t), F32), v((wide, t), BF), v((2 * t, wide), BF), v((t, ff), BF), v((t, ff), BF), v((2 * t, ff), BF),
        v((t, ff), BF), v((t, wide), BF), v((sz.feat, t), BF), v((t, t), F32), v((sz.width + 16, t), F32),
        v((sz.feat, t), F32),
        pltpu.SemaphoreType.DMA((4 * sz.n + 40,)), pltpu.SemaphoreType.DMA((10 * sz.n,)),
    ]
    return call(body, ins, outs, scratch, 24 * t * wide * ff, 60, specs, out_specs)


def up_out_grad(sz, back, a2s, grads, mixps, gls, half):
    t, wide, ff = sz.t, sz.wide, sz.ff
    cols = ff + wide

    def body(back_ref, a_1, a_2, g_1, g_2, m1, m2, l1, l2, own, s0, s1, a, g, mixp, gl, out, sem):
        io = Copies(sem)
        run1, run2 = pl.ds(0, t), pl.ds(t, t)
        wait([
            io.start(m1, mixp.at[:, run1]), io.start(m2, mixp.at[:, run2]),
            io.start(l1, gl.at[run1, :]), io.start(l2, gl.at[run2, :]),
        ])
        later = [
            io.start(a_1, a.at[run1, :]), io.start(a_2, a.at[run2, :]),
            io.start(g_1, g.at[run1, :]), io.start(g_2, g.at[run2, :]),
        ]
        nz = sz.n // 4
        tile = wide // nz
        starts = [pl.multiple_of(back_ref[k] * tile, tile) for k in range(nz)]
        for k in range(nz):
            out[k * tile : (k + 1) * tile, ff:cols] = nn(mixp[pl.ds(starts[k], tile), :], gl[...]).astype(BF)
        wait(later)
        for k in range(nz):
            out[k * tile : (k + 1) * tile, 0:ff] = tn(a[:, pl.ds(starts[k], tile)], g[...]).astype(BF)
            io.blocks(back_ref, nz, k, out, k * tile, half, own, (s0, s1))
        io.close()

    v = pltpu.VMEM
    return call(
        body, [back, *a2s, *grads, *mixps, *gls], halves(sz, half, cols),
        [
            v((2 * t, wide), BF), v((2 * t, ff), BF), v((wide, 2 * t), BF), v((2 * t, wide), BF), v((wide, cols), BF),
            pltpu.SemaphoreType.DMA((2 * sz.n + 8,)),
        ],
        4 * t * wide * cols, 48,
        specs=[SMEM] + [ANY] * 8, out_specs=[ANY] * 3,
    )


def settle(*arrays):
    def body(*refs):
        for a, b in zip(refs[: len(arrays)], refs[len(arrays) :]):
            b[...] = a[...]

    return call(body, list(arrays), [shape(*a.shape, dtype=a.dtype) for a in arrays], [], 0, 20)


def last_attention(sz, gh, gl, x, gains, wqkv, wo, rope, bias, heads, lse):
    t, wide = sz.t, sz.wide

    def body(gh_hbm, gl_hbm, x_hbm, gains_ref, wqkv_hbm, wo_hbm, cos, sin, bias_hbm, heads_hbm, lse_ref,
             g_x_hbm, g_qkv_hbm, gain_grad,
             gh, gl, x_low, x, wqkv, wo, bias_ref, heads, g_qkv, mix, g_heads, sem):
        io = Copies(sem)
        first = [io.start(gl_hbm, gl), io.start(wo_hbm, wo)]
        second = [io.start(heads_hbm, heads), io.start(bias_hbm, bias_ref)]
        wait(first)
        later = []

        def ready(last):
            if last:
                io.store(g_qkv, g_qkv_hbm)
                wait(later)
                x[...] = x_low[...].astype(F32)
            else:
                wait(second)
                later.extend([io.start(wqkv_hbm, wqkv), io.start(gh_hbm, gh), io.start(x_hbm, x_low)])

        gain_a, back_x = attention_backward(
            sz, gh, gl[...], x, gains_ref[0:1, :], wqkv, wo, cos, sin, bias_ref,
            heads, lse_ref, mix, g_heads, g_qkv, ready
        )
        gl[...] = back_x.astype(BF)
        io.store(gl, g_x_hbm)
        gain_grad[...] = jnp.concatenate([gain_a, jnp.zeros((7, wide), F32)], axis=0)
        io.close()

    v = pltpu.VMEM
    return call(
        body,
        [gh, gl, x, gains, wqkv, wo, *rope, bias, heads, lse],
        [shape(t, wide), shape(sz.feat, t), shape(8, wide, dtype=F32)],
        [
            v((t, wide), F32), v((t, wide), BF), v((t, wide), BF), v((t, wide), F32), v((wide, sz.feat), BF),
            v((wide, wide), BF), v((t, t), F32), v((sz.feat, t), BF), v((sz.feat, t), BF), v((sz.width + 16, t), F32),
            v((sz.feat, t), F32), pltpu.SemaphoreType.DMA((16,)),
        ],
        10 * t * wide * sz.feat, 40,
        specs=[ANY] * 3 + [VM] + [ANY] * 2 + [VM] * 2 + [ANY] * 2 + [VM],
        out_specs=[ANY] * 2 + [VM],
    )


def qkv_grad(sz, back, a1s, g_qkv_runs, gain2, gain_a1, half):
    t, wide, cols = sz.t, sz.wide, sz.feat

    def body(back_ref, a_1, a_2, g1, g2, gain2_ref, gain_a_ref, own, s0, s1, a1, g_qkv, out, sem):
        io = Copies(sem)
        run1, run2 = pl.ds(0, t), pl.ds(t, t)
        wait([
            io.start(a_1, a1.at[run1, :]), io.start(a_2, a1.at[run2, :]),
            io.start(g1, g_qkv.at[:, run1]), io.start(g2, g_qkv.at[:, run2]),
        ])
        nz = sz.n // 4
        tile = wide // nz
        row = lax.broadcasted_iota(jnp.int32, (sz.padded, sz.padded), 0)
        for k in range(nz):
            here = pl.ds(pl.multiple_of(back_ref[k] * tile, tile), tile)
            into = tt(a1[:, here], g_qkv[...])
            attn_gain = gain_a_ref[0:1, here] + gain2_ref[0:1, here]
            ffn_gain = gain2_ref[1:2, here]
            patches = []
            for s in range(0, tile, sz.padded):
                a, f = attn_gain[:, s : s + sz.padded], ffn_gain[:, s : s + sz.padded]
                patches.append(jnp.where(row == sz.real, a, jnp.where(row == sz.real + 1, f, 0.0)))
            patch = jnp.concatenate([join(patches, 0), jnp.zeros((tile, 128 - sz.padded), F32)], axis=1)
            lo = k * tile
            out[lo : lo + tile, 0:128] = (into[:, :128] + patch).astype(BF)
            out[lo : lo + tile, 128:cols] = into[:, 128:].astype(BF)
            io.blocks(back_ref, nz, k, out, lo, half, own, (s0, s1))
        io.close()

    v = pltpu.VMEM
    return call(
        body,
        [back, *a1s, *g_qkv_runs, gain2, gain_a1],
        halves(sz, half, cols),
        [v((2 * t, wide), BF), v((cols, 2 * t), BF), v((wide, cols), BF), pltpu.SemaphoreType.DMA((2 * sz.n + 8,))],
        4 * t * wide * cols, 40,
        specs=[SMEM] + [ANY] * 4 + [VM] * 2, out_specs=[ANY] * 3,
    )


def spread(v, n, real, padded):
    lead = v.shape[:-1]
    v = v.reshape(lead + (n, real))
    v = jnp.pad(v, [(0, 0)] * len(lead) + [(0, 0), (0, padded - real)])
    return v.reshape(lead + (n * padded,))


def narrow(v, n, real, padded):
    lead = v.shape[:-1]
    return v.reshape(lead + (n, padded))[..., :real].reshape(lead + (n * real,))


def place_blocks(order, pieces):
    both = jnp.concatenate(pieces)
    spots = jnp.zeros(order.shape, jnp.int32).at[order].set(jnp.arange(order.shape[0], dtype=jnp.int32))
    return jnp.take(both, spots, axis=0).reshape(-1, both.shape[2])


def order_blocks(order, grad, half, nz):
    blocks = grad.reshape(nz, 8, half, grad.shape[1])
    at_z = jnp.take(blocks, order[:nz], axis=0)
    parts = [jnp.take(at_z, order[nz + k], axis=1) for k in range(8)]
    return jnp.concatenate(parts[:4]), jnp.concatenate(parts[4:6]), jnp.concatenate(parts[6:])


def shards(mesh, tokens, lengths, w_query, key_weight, value_weight, output_weight, w_gate, w_up, w_down, gain_attn, gain_ffn, out_grad):
    at = Place(mesh)
    n = at.n
    real, width = w_query.shape
    padded = -(-(real + 2) // 16) * 16
    sz = Sizes(n, real, padded, w_gate.shape[1], tokens.shape[0], key_weight.shape[1])
    wide, ff = sz.wide, sz.ff
    half, down_half = padded // 2, w_down.shape[0] // 2
    aligned = down_half % 16 == 0
    order = Order()
    places, back = at.piece_order(), at.grad_order()

    def pad_rows(v):
        return jnp.pad(v, ((0, padded - v.shape[0]), (0, 0)))

    def attention_shard(w_query, key_weight, value_weight, output_weight, gain_attn, gain_ffn):
        qkv = jnp.concatenate([w_query, key_weight, value_weight], axis=1)
        gains = jnp.pad(jnp.stack([gain_attn, gain_ffn]), ((0, 0), (0, qkv.shape[1] - real)))
        qkv = pad_rows(jnp.concatenate([qkv, gains]))
        return jnp.concatenate([pad_rows(spread(output_weight, n, real, padded)), qkv], axis=1)

    def tables(lengths, tokens, out_grad):
        positions, allowed = layout(lengths, tokens.shape[0])
        bias = jnp.where(allowed[0], 0.0, -1e30).astype(F32).T
        return rotation(positions[0]), bias, spread(tokens, n, real, padded), spread(out_grad, n, real, padded)

    ga, gg, gu, gd = (Gather(at, order) for _ in range(4))
    ga.start(attention_shard, w_query, key_weight, value_weight, output_weight, gain_attn, gain_ffn)
    ga.ready()
    ga.along_z()
    gg.start(pad_rows, w_gate)
    gu.start(pad_rows, w_up)
    gd.start(lambda v: spread(v, n, real, padded), w_down)
    gg.ready()
    gu.ready()
    gd.ready()
    rope, bias, x1, cot = order.do(tables, lengths, tokens, out_grad)
    ga.come()
    ga.line_up()
    ga.first()
    gg.along_z()
    ga.got_first()
    ga.second()
    gg.come()
    gg.line_up()
    gg.first()
    gu.along_z()
    x1, cot = order.do(settle, x1, cot)
    ga.got_second()
    gg.got_first()
    gu.come()
    ga.cores()
    gg.second()
    gu.line_up()
    gu.first()
    attn_pieces = ga.pieces()
    gd.along_z()
    hidden1, a1_1, heads1, lse1, mixp1, gains = order.do(
        lambda *v: first_attention(sz, *v), places, attn_pieces, x1, rope, bias
    )
    gd.come()
    gg.got_second()
    gg.cores()
    gu.got_first()
    gu.second()
    gd.line_up()
    gd.first()
    gate_pieces = gg.pieces()
    a2_1, gate1 = order.do(lambda *v: first_gate(sz, *v), places, gate_pieces, hidden1, gains)
    gd.got_first()
    gd.second()
    gu.got_second()
    gu.cores()
    up_pieces = gu.pieces()
    gd.cores(gd.both)
    up1, inner1 = order.do(lambda *v: first_up(sz, *v), places, up_pieces, a2_1, gate1)
    gd.got_second()
    gd.cores(gd.third)
    down_pieces = gd.pieces()
    if not aligned:
        down_pieces = place_blocks(places, down_pieces)

    (second, wqkv, wo, a1_2, mixp2, a2_2, gu2, gl2, g_qkv2, gh1, gl1, gu1, gain2, *grads) = order.do(
        lambda *v: middle(sz, *v, half, down_half),
        places, back, down_pieces, attn_pieces, gate_pieces, up_pieces, hidden1, inner1, gate1, up1, a2_1, gains, rope, bias, cot,
    )
    downs, gates = grads[:3], grads[3:]
    if not aligned:
        downs = order_blocks(back, downs[0], down_half, at.nz)
    sd = Scatter(at, order, *downs)
    sg = Scatter(at, order, *gates)
    sd.core(0)
    sg.core(0)
    sd.core(1)
    sg.core(1)
    sd.come_core(0)
    sd.first()
    sg.come_core(0)
    sg.first()
    sd.come_core(1)
    sg.come_core(1)
    own, *send = order.do(
        lambda *v: up_out_grad(sz, *v, half), back, (a2_1, a2_2), (gu1, gu2), (mixp1, mixp2), (gl1, gl2)
    )
    sd.come()
    su = Scatter(at, order, own, *send)
    su.core(0)
    su.core(1)
    sd.second()
    su.come_core(0)
    su.first()
    su.come_core(1)
    g_x, g_qkv1, gain_a1 = order.do(
        lambda *v: last_attention(sz, *v), gh1, gl1, x1, gains, wqkv, wo, rope, bias, heads1, lse1
    )
    sg.come()
    sd.come()
    sg.second()
    sd.along_z()
    own, *send = order.do(
        lambda *v: qkv_grad(sz, *v, half), back, (a1_1, a1_2), (g_qkv1, g_qkv2), gain2, gain_a1
    )
    sg.come()
    sd.come_z()
    sg.along_z()
    su.come()
    su.second()
    sa = Scatter(at, order, own, *send)
    sa.core(0)
    sa.core(1)
    sa.come_core(0)
    sa.first()
    sa.come_core(1)
    su.come()
    sg.come_z()
    su.along_z()
    sa.come()
    sa.second()
    sd.along_x()
    sg.along_x()
    second, g_x = order.do(settle, second, g_x)
    su.come_z()
    sa.come()
    sa.along_z()
    su.along_x()
    sd.come()
    sd.cores()
    sa.come_z()
    sa.along_x()
    sg.come()
    sg.cores()
    sd.come()
    r_down = sd.result()
    su.come()
    su.cores()
    sg.come()
    r_gate = sg.result()
    su.come()
    r_up = su.result()
    second, g_x = narrow(second, n, real, padded), narrow(g_x, n, real, padded)
    sa.come()
    sa.cores()
    sa.come()
    r_in = sa.result()
    kv = key_weight.shape[1]
    return (
        second,
        g_x,
        r_in[:real, :width],
        r_in[:real, width : width + kv],
        r_in[:real, width + kv :],
        narrow(r_up[:real, ff:], n, real, padded),
        r_gate[:real],
        r_up[:real, :ff],
        narrow(r_down, n, real, padded),
        r_in[real, :real],
        r_in[real + 1, :real],
    )


def solution(mesh):
    rows, split, gain = P(("dp", "fsdp"), None), P("fsdp", None), P("fsdp")
    return jax.shard_map(
        functools.partial(shards, mesh),
        mesh=mesh,
        in_specs=(rows, rows) + (split,) * 7 + (gain, gain, rows),
        out_specs=(rows, rows) + (split,) * 7 + (gain, gain),
        check_vma=False,
    )
```
